32 devices in a mesh: dom: 8 (over z, x), sub: 4 (over y, core).
Axes of the slice: x: 2, y: 2, z: 4, core: 2. Of those that a mesh axis runs over, the one named last changes fastest.
Arguments:
- segments: float32 [4096, 9, 128], P(('dom', 'sub')), may hold values from -6 to 6
- send_tiles: int32 [32, 32, 16], P(('dom', 'sub')), may hold values from 0 to 127
- pair_local: int32 [32, 512], P(('dom', 'sub')), may hold values from 0 to 127
- pair_remote: int32 [32, 512], P(('dom', 'sub')), may hold values from 0 to 511, each once within a row
- pair_count: int32 [32], P(('dom', 'sub')), may hold values from 64 to 512, as said below
- tile_cell: int32 [4096], P(('dom', 'sub')), may hold values from 0 to 63
Outputs:
- forces: float32 [4096, 3, 128], P(('dom', 'sub'))
The draws below stay inside these ranges and needn't reach their ends.
Inputs may be any that keep to these rules, and one draw needn't show every extreme that they name: `send_tiles`: every slot names a tile; each device sends exactly 16 tiles to every device. `pair_remote`: each device's row names every one of its 512 received slots once. `pair_count`: some device holds 512 live pairs.
All inputs are finite; a program needn't handle non-finite values.
Results may differ from the reference program's by a relative error of at most 0.00018.
Values sent between devices are 32-bit elements; how exact they have to be, the bound alone decides.
No kernel may reach another device: no remote copies, remote signals or barrier semaphores. Data moves between devices by JAX's collectives and lax.ppermute only.
A program may use at most 64 MiB of HBM per device.

```python
import jax
import jax.numpy as jnp
from jax import lax

TILE = 128
TILES_DEV = 128
PAIRS_DEV = 512
BLOCK = 64
NCELL = 64
CAP = 16
TILES = 4096
DEVICES = 32


def draw_pair_count(key, part):
    key = jax.random.fold_in(key, 7)
    first, second = jax.random.split(key)
    lighter = jax.random.randint(first, (DEVICES,), PAIRS_DEV // 8, PAIRS_DEV // 2 + 1)
    busiest = jax.random.randint(second, (), 0, DEVICES)
    return jnp.where(jnp.arange(DEVICES) == busiest, PAIRS_DEV, lighter).astype(jnp.int32)


def touch_ends(array, stream_key, low, high):
    shape = array.shape
    place = [jax.random.randint(jax.random.fold_in(stream_key, axis), (), 0, shape[axis]) for axis in range(len(shape))]
    array = array.at[tuple(place)].set(low)
    longest = shape.index(max(shape))
    place[longest] = (place[longest] + 1) % shape[longest]
    return array.at[tuple(place)].set(high)


def block_scale(stream_key, extent, cuts, low, largest):
    gain, own = 1.0, jax.random.fold_in(stream_key, 6)
    for axis_at, parts in cuts:
        draws = jnp.exp(jax.random.uniform(jax.random.fold_in(own, axis_at), (parts,), jnp.float32, low / len(cuts), largest / len(cuts)))
        gain = gain * jnp.repeat(draws, extent[axis_at] // parts).reshape([-1 if axis == axis_at else 1 for axis in range(len(extent))])
    return gain


def bell_draw(stream_key, extent, scale, reach, pieces=(), dtype=jnp.bfloat16):
    array = jax.random.normal(stream_key, extent, jnp.float32) * scale
    if len(pieces) > 0:
        array = block_scale(stream_key, extent, pieces, -0.22, 0.18) * array
    return jnp.clip(array, min=-reach, max=reach).astype(dtype)


def setup_inputs(seed: int = 0) -> dict:
    arg_keys = jax.random.split(jax.random.key(seed), 7)
    return {
        "segments": bell_draw(arg_keys[0], (TILES, 9, TILE), 1.0, 6.0, ((0, 32),), jnp.float32),
        "send_tiles": touch_ends(jax.random.randint(arg_keys[1], (DEVICES, DEVICES, CAP), 0, TILES_DEV), jax.random.fold_in(arg_keys[1], 1), 0, TILES_DEV - 1).astype(jnp.int32),
        "pair_local": touch_ends(jax.random.randint(arg_keys[2], (DEVICES, PAIRS_DEV), 0, TILES_DEV), jax.random.fold_in(arg_keys[2], 1), 0, TILES_DEV - 1).astype(jnp.int32),
        "pair_remote": jax.vmap(lambda own: jax.random.permutation(own, PAIRS_DEV))(jax.random.split(arg_keys[3], DEVICES)).reshape((DEVICES, PAIRS_DEV)).astype(jnp.int32),
        "pair_count": draw_pair_count(jax.random.fold_in(arg_keys[6], 71), 0),
        "tile_cell": touch_ends(jax.random.randint(arg_keys[5], (TILES,), 0, NCELL), jax.random.fold_in(arg_keys[5], 1), 0, NCELL - 1).astype(jnp.int32),
    }


core_square = 0.25

def interact(near_block, far_block, live_mask):
    apart = near_block[:, 0:3, :, None] - far_block[:, 0:3, None, :]
    spread = lax.optimization_barrier(jnp.sum(apart * apart, axis=1)) + core_square
    inverse = lax.rsqrt(spread)
    inverse = inverse * inverse * inverse
    burgers_dot = lax.optimization_barrier(jnp.sum(near_block[:, 3:6, :, None] * far_block[:, 3:6, None, :], axis=1))
    cross_first = lax.optimization_barrier(jnp.sum(near_block[:, 3:6, :, None] * far_block[:, 6:9, None, :], axis=1))
    cross_second = lax.optimization_barrier(jnp.sum(far_block[:, 3:6, None, :] * near_block[:, 6:9, :, None], axis=1))
    coupling = (burgers_dot + cross_first * cross_second) * inverse * live_mask[:, None, None]
    weighted = apart * coupling[:, None]
    return (lax.optimization_barrier(jnp.sum(weighted, axis=3)), -lax.optimization_barrier(jnp.sum(weighted, axis=2)))

def far_field(segments, tile_cell, moment_sums, total_segments):
    moments = moment_sums.reshape(NCELL, 3, 3) / jnp.sqrt(jnp.float32(total_segments))
    moments = 0.5 * (moments + jnp.transpose(moments, (0, 2, 1)))
    cells = jnp.arange(NCELL).astype(jnp.float32)
    weights = 8.0 / (8.0 + jnp.abs(cells[:, None] - cells[None, :]))
    stress = jnp.dot(weights, moments.reshape(NCELL, 9), precision=lax.Precision.HIGHEST)
    onehot = (tile_cell[:, None] == jnp.arange(NCELL)[None, :]).astype(jnp.float32)
    tile_stress = jnp.dot(onehot, stress, precision=lax.Precision.HIGHEST).reshape(-1, 3, 3)
    traction = lax.optimization_barrier(jnp.sum(tile_stress[:, :, :, None] * segments[:, None, 3:6, :], axis=2))
    lines = segments[:, 6:9, :]
    return jnp.stack([traction[:, 1] * lines[:, 2] - traction[:, 2] * lines[:, 1], traction[:, 2] * lines[:, 0] - traction[:, 0] * lines[:, 2], traction[:, 0] * lines[:, 1] - traction[:, 1] * lines[:, 0]], axis=1)

def local_moments(segments, tile_cell):
    outer = lax.optimization_barrier(jnp.sum(segments[:, 3:6, None, :] * segments[:, None, 6:9, :], axis=3)).reshape(-1, 9)
    onehot = (jnp.arange(NCELL)[:, None] == tile_cell[None, :]).astype(jnp.float32)
    return jnp.dot(onehot, outer, precision=lax.Precision.HIGHEST)

def reference(segments, send_tiles, pair_local, pair_remote, pair_count, tile_cell):
    devices = send_tiles.shape[0]
    slots = send_tiles.shape[2]
    tiles_dev = segments.shape[0] // devices
    owner = jnp.arange(devices).astype(jnp.int32)[:, None]
    source = pair_remote // slots
    column = pair_remote % slots
    far_tile = (source * tiles_dev + send_tiles[source, owner, column]).astype(jnp.int32)
    near_tile = (owner * tiles_dev + pair_local).astype(jnp.int32)
    live = (jnp.arange(PAIRS_DEV)[None, :] < pair_count[:, None]).astype(jnp.float32)
    near_blocks = near_tile.reshape(-1, BLOCK)
    far_blocks = far_tile.reshape(-1, BLOCK)
    live_blocks = live.reshape(-1, BLOCK)

    def advance(totals, inputs):
        near_ids, far_ids, live_mask = inputs
        near_part, far_part = interact(segments[near_ids], segments[far_ids], live_mask)
        totals = totals.at[near_ids].add(near_part)
        totals = totals.at[far_ids].add(far_part)
        return (totals, None)
    start = jnp.zeros((segments.shape[0], 3, segments.shape[2]), jnp.float32)
    pair_forces, unused = lax.scan(advance, start, (near_blocks, far_blocks, live_blocks))
    moment_sums = local_moments(segments, tile_cell)
    total_segments = segments.shape[0] * segments.shape[2]
    return pair_forces + far_field(segments, tile_cell, moment_sums, total_segments)
```

```python
import functools
import jax
import jax.numpy as jnp
from jax import lax
from jax.sharding import PartitionSpec as P
from jax.experimental import pallas as pl
from jax.experimental.pallas import tpu as pltpu

CORE = 0.25
UNROLL = 4


def head(value):
    return value.astype(jnp.bfloat16).astype(jnp.float32)


def pair_terms(near, near_row, far, far_row):
    sub = lax.broadcasted_iota(jnp.int32, (8, 128), 0)
    first = sub < 3
    second = jnp.logical_and(sub >= 3, sub < 6)
    third = sub == 5
    zero = jnp.zeros((8, 128), jnp.float32)

    def thirds(row):
        high = head(row)
        rest = row - high
        middle = head(rest)
        return high, middle, rest - middle

    near_high, near_mid, near_low = thirds(near)
    row_high, row_mid, row_low = thirds(jnp.broadcast_to(near_row, (8, 128)))
    row_part = jnp.where(sub == 0, row_high, jnp.where(sub == 1, row_mid, jnp.where(sub == 2, row_low, jnp.where(second, 1.0, 0.0))))
    left = jnp.concatenate([near_high, near_mid, near_low, near_high, row_part, zero], axis=0)

    far_high = head(far)
    far_mid = far - far_high

    def minus_part(row, others):
        high, middle, low = thirds(jnp.broadcast_to(row, (8, 128)))
        return jnp.where(sub == 3, -high, jnp.where(sub == 4, -middle, jnp.where(third, -low, others)))

    burgers = [jnp.where(first, part, 0.0) for part in (far_high, far_mid)]
    lines_up = [jnp.where(first, pltpu.roll(part, 5, 0), 0.0) for part in (far_high, far_mid)]
    burgers_down = [jnp.where(second, pltpu.roll(part, 3, 0), 0.0) for part in (far_high, far_mid)]
    ones_six = jnp.where(sub == 6, 1.0, 0.0)
    ones_seven = jnp.where(sub == 7, 1.0, 0.0)
    ones_first = jnp.where(first, 1.0, 0.0)
    columns = [
        [pair[0], pair[0], zero, pair[1], zero, zero] for pair in (burgers, lines_up, burgers_down)
    ]
    columns.append([ones_six, ones_six, ones_six, zero, minus_part(far[6:7], zero), zero])
    columns.append([ones_seven, ones_seven, ones_seven, zero, minus_part(far[7:8], zero), zero])
    columns.append([zero, zero, zero, zero, minus_part(far_row, ones_first), zero])
    right = jnp.concatenate([jnp.concatenate(column, axis=0).astype(jnp.bfloat16) for column in columns], axis=1)
    left = left.T.astype(jnp.bfloat16)
    return lax.dot_general(left, right, (((1,), (0,)), ((), ())), preferred_element_type=jnp.float32)


def pair_forces(terms):
    burgers_dot, first, second, x, y, z = [terms[:, 128 * k : 128 * (k + 1)] for k in range(6)]
    spread = x * x + y * y + z * z + CORE
    inverse = lax.rsqrt(spread)
    coupling = (burgers_dot + first * second) * (inverse * inverse * inverse)
    weighted = [coupling * part for part in (x, y, z)]
    far_rows = [-jnp.sum(part, axis=0, keepdims=True) for part in weighted]
    sums = [jnp.sum(part, axis=1, keepdims=True) for part in weighted]
    lane = lax.broadcasted_iota(jnp.int32, (128, 128), 1)
    packed = jnp.where(lane == 0, sums[0], jnp.where(lane == 1, sums[1], sums[2])).T
    return [packed[k : k + 1] for k in range(3)], far_rows


def pair_kernel(near_tiles, far_tiles, count_ref, near_ids, far_ids, near_ref, far_ref, near_out, far_out):
    near_out[...] = jnp.zeros_like(near_out)
    far_out[...] = jnp.zeros_like(far_out)
    count = count_ref[0]
    last = near_ids.shape[0] - 1

    def load(ref, tiles, index):
        group = index // tiles
        tile = index % tiles
        return ref[group, tile], ref[group, tiles + tile // 8, pl.ds(tile % 8, 1), :]

    def step(block, carry):
        picks = []
        for k in range(UNROLL):
            position = block * UNROLL + k
            place = jnp.minimum(position, last)
            live = jnp.where(position < count, 1.0, 0.0)
            near_id = near_ids[place]
            far_id = far_ids[place]
            near, near_row = load(near_ref, near_tiles, near_id)
            far, far_row = load(far_ref, far_tiles, far_id)
            picks.append((near_id, far_id, live, pair_forces(pair_terms(near, near_row, far, far_row))))
        for near_id, far_id, live, (near_rows, far_rows) in picks:
            for axis in range(3):
                near_out[axis, pl.ds(near_id, 1), :] += near_rows[axis] * live
                far_out[axis, pl.ds(far_id, 1), :] += far_rows[axis] * live
        return carry

    lax.fori_loop(0, (count + UNROLL - 1) // UNROLL, step, 0)


def run_pairs(count, near_ids, far_ids, near, far, near_tiles, far_tiles):
    near_total = near.shape[0] * near_tiles
    far_total = far.shape[0] * far_tiles
    smem = pl.BlockSpec(memory_space=pltpu.SMEM)
    vmem = pl.BlockSpec(memory_space=pltpu.VMEM)
    width = near.shape[-1]
    return pl.pallas_call(
        functools.partial(pair_kernel, near_tiles, far_tiles),
        out_shape=(
            jax.ShapeDtypeStruct((3, near_total, width), jnp.float32),
            jax.ShapeDtypeStruct((3, far_total, width), jnp.float32),
        ),
        in_specs=[smem, smem, smem, vmem, vmem],
        out_specs=(vmem, vmem),
        compiler_params=pltpu.CompilerParams(vmem_limit_bytes=48 * 1024 * 1024),
    )(count, near_ids, far_ids, near, far)


def tile_groups(tiles):
    main = jnp.concatenate([tiles[..., 3:9, :], tiles[..., 0:2, :]], axis=-2)
    rows = tiles[..., 2, :]
    short = -rows.shape[-2] % 8
    rows = jnp.pad(rows, [(0, 0)] * (rows.ndim - 2) + [(0, short), (0, 0)])
    rows = rows.reshape(rows.shape[:-2] + (rows.shape[-2] // 8, 8, rows.shape[-1]))
    return jnp.concatenate([main, rows], axis=-3)


NCELL = 64


def far_field(segments, tile_cell, moment_sums, total_segments):
    moments = moment_sums.reshape(NCELL, 3, 3) / jnp.sqrt(jnp.float32(total_segments))
    moments = 0.5 * (moments + jnp.transpose(moments, (0, 2, 1)))
    cells = jnp.arange(NCELL).astype(jnp.float32)
    weights = 8.0 / (8.0 + jnp.abs(cells[:, None] - cells[None, :]))
    stress = jnp.dot(weights, moments.reshape(NCELL, 9), precision=lax.Precision.HIGHEST)
    onehot = (tile_cell[:, None] == jnp.arange(NCELL)[None, :]).astype(jnp.float32)
    tile_stress = jnp.dot(onehot, stress, precision=lax.Precision.HIGHEST).reshape(-1, 3, 3)
    traction = jnp.sum(tile_stress[:, :, :, None] * segments[:, None, 3:6, :], axis=2)
    lines = segments[:, 6:9, :]
    return jnp.stack(
        [
            traction[:, 1] * lines[:, 2] - traction[:, 2] * lines[:, 1],
            traction[:, 2] * lines[:, 0] - traction[:, 0] * lines[:, 2],
            traction[:, 0] * lines[:, 1] - traction[:, 1] * lines[:, 0],
        ],
        axis=1,
    )


def local_moments(segments, tile_cell):
    outer = jnp.sum(segments[:, 3:6, None, :] * segments[:, None, 6:9, :], axis=3).reshape(-1, 9)
    onehot = (jnp.arange(NCELL)[:, None] == tile_cell[None, :]).astype(jnp.float32)
    return jnp.dot(onehot, outer, precision=lax.Precision.HIGHEST)


def on_device(segments, send_tiles, pair_local, pair_remote, pair_count, tile_cell):
    width = segments.shape[2]
    tiles = segments.shape[0]
    peers = send_tiles.shape[1]
    slots = send_tiles.shape[2]
    n_dom = lax.axis_size("dom")
    n_sub = lax.axis_size("sub")
    outgoing = tile_groups(segments[send_tiles[0]])
    arrived = lax.all_to_all(outgoing, ("dom", "sub"), split_axis=0, concat_axis=0, tiled=True)
    moment_sums = lax.psum(local_moments(segments, tile_cell), ("dom", "sub"))
    near_forces, far_forces = run_pairs(
        pair_count, pair_local[0], pair_remote[0], tile_groups(segments)[None], arrived, tiles, slots
    )
    returned = lax.all_to_all(
        far_forces.reshape(3, peers, slots, width),
        ("dom", "sub"),
        split_axis=1,
        concat_axis=1,
        tiled=True,
    )
    returned = returned.reshape(3, peers * slots, width)
    picks = (send_tiles[0].reshape(-1)[None, :] == jnp.arange(tiles)[:, None]).astype(jnp.float32)
    near_forces = near_forces + jnp.einsum("ts,ksw->ktw", picks, returned, precision=lax.Precision.HIGHEST)
    total_segments = tiles * width * n_dom * n_sub
    return near_forces.transpose(1, 0, 2) + far_field(segments, tile_cell, moment_sums, total_segments)


def solution(mesh):
    in_specs = (
        P(("dom", "sub"), None, None),
        P(("dom", "sub"), None, None),
        P(("dom", "sub"), None),
        P(("dom", "sub"), None),
        P(("dom", "sub")),
        P(("dom", "sub")),
    )
    out_specs = P(("dom", "sub"), None, None)
    return jax.shard_map(
        on_device, mesh=mesh, in_specs=in_specs, out_specs=out_specs, check_vma=False
    )
```

```python
import functools
import jax
import jax.numpy as jnp
from jax import lax
from jax.sharding import PartitionSpec as P
from jax.experimental import pallas as pl
from jax.experimental.pallas import tpu as pltpu

CORE = 0.25
GROUP = 4


def head(value):
    return value.astype(jnp.bfloat16).astype(jnp.float32)


def thirds(value):
    high = head(value)
    rest = value - high
    middle = head(rest)
    return high, middle, rest - middle


def halves(value):
    high = value.astype(jnp.bfloat16)
    return high, (value - high.astype(jnp.float32)).astype(jnp.bfloat16)


def tall(groups):
    return jnp.concatenate(groups, axis=0).astype(jnp.bfloat16)


def place(sub, rows, others=0.0):
    filled = others
    for at, row in rows.items():
        filled = jnp.where(sub == at, row, filled)
    return filled


def tile_parts(sub, tile, row):
    row = jnp.broadcast_to(row, tile.shape)
    square = row * row
    for at in (6, 7):
        other = jnp.broadcast_to(tile[at : at + 1], tile.shape)
        square = square + other * other
    main, last = thirds(tile), thirds(row)
    positions = [jnp.where(sub >= 6, m, jnp.where(sub == 5, r, 0.0)) for m, r in zip(main, last)]
    sums = tall([jnp.where(sub == 4, 1.0, positions[0]), positions[1], positions[2], jnp.zeros_like(tile)])
    spot = jnp.where(sub >= 6, tile, jnp.where(sub == 5, row, 0.0))
    return main, last, square, sums, spot


def operands(near, near_row, far, far_row):
    sub = lax.broadcasted_iota(jnp.int32, near.shape, 0)
    first = sub < 3
    second = jnp.logical_and(sub >= 3, sub < 6)
    zero = jnp.zeros_like(near)
    scale = 1.0 / near.shape[1]
    middle = jnp.where(sub >= 6, jnp.sum(near, axis=1, keepdims=True) * scale, 0.0)
    middle_row = jnp.sum(near_row, axis=1, keepdims=True) * scale
    near, far = near - middle, far - middle
    near_row, far_row = near_row - middle_row, far_row - middle_row
    (high, mid, low), (row_high, row_mid, row_low), square, near_sums, near_spot = tile_parts(sub, near, near_row)
    square_parts = thirds(square)
    left = tall(
        [
            high, mid, high, low, high, mid,
            place(sub, {0: row_high, 1: row_mid, 2: row_high, 3: row_low, 4: row_high, 5: row_mid}),
            place(sub, {0: square_parts[0], 1: square_parts[1], 2: square_parts[2]}, jnp.where(second, 1.0, 0.0)),
        ]
    )
    (high, mid, low), (row_high, row_mid, row_low), square, far_sums, far_spot = tile_parts(sub, far, far_row)
    square_parts = thirds(square + CORE)
    twice = [jnp.where(sub >= 6, -2.0 * part, 0.0) for part in (high, mid, low)]
    twice_row = [-2.0 * part for part in (row_high, row_mid, row_low)]
    spread = tall(
        [
            twice[0], twice[0], twice[1], twice[0], twice[2], twice[1],
            place(sub, {0: twice_row[0], 1: twice_row[0], 2: twice_row[1], 3: twice_row[0], 4: twice_row[2], 5: twice_row[1]}, zero),
            place(sub, {3: square_parts[0], 4: square_parts[1], 5: square_parts[2]}, jnp.where(first, 1.0, 0.0)),
        ]
    )
    dots = []
    for part in (
        [jnp.where(first, part, 0.0) for part in (high, mid)],
        [jnp.where(first, pltpu.roll(part, 5, 0), 0.0) for part in (high, mid)],
        [jnp.where(second, pltpu.roll(part, 3, 0), 0.0) for part in (high, mid)],
    ):
        dots.append(tall([part[0], part[0], part[1], zero]))
    return left.T, spread, dots, near_sums, near_spot, far_sums, far_spot


def matmul(left, right, contract=(1, 0)):
    dims = (((contract[0],), (contract[1],)), ((), ()))
    return lax.dot_general(left, right, dims, preferred_element_type=jnp.float32)


def live_list(near_rows, far_rows, ids_ref):
    slots = ids_ref.shape[1]

    def line(rows):
        return jnp.concatenate([rows[k : k + 1] for k in range(rows.shape[0])], axis=1)

    near, far = line(near_rows), line(far_rows)
    alive = near >= 0
    row = lax.broadcasted_iota(jnp.int32, (slots, slots), 0)
    lane = lax.broadcasted_iota(jnp.int32, (slots, slots), 1)
    before = jnp.where(row < lane, 1.0, 0.0).astype(jnp.bfloat16)
    flags = jnp.where(alive, 1.0, 0.0)
    rank = matmul(jnp.broadcast_to(flags, (8, slots)).astype(jnp.bfloat16), before)[0:1]
    rank = jnp.where(alive, rank, -1.0)
    chosen = jnp.where(jnp.broadcast_to(rank, (slots, slots)) == row.astype(jnp.float32), 1.0, 0.0).astype(jnp.bfloat16)
    sub = lax.broadcasted_iota(jnp.int32, (8, slots), 0)
    near, far = jnp.maximum(near, 0).astype(jnp.int32), far.astype(jnp.int32)
    values = [near >> 6, near & 63, far >> 6, far & 63]
    values = place(sub, {k: value.astype(jnp.float32) for k, value in enumerate(values)}, jnp.zeros((8, slots), jnp.float32))
    packed = matmul(values.astype(jnp.bfloat16), chosen, (1, 1)).astype(jnp.int32)
    number = jnp.sum(flags, axis=1, keepdims=True).astype(jnp.int32)
    ids_ref[0:1, :] = packed[0:1] * 64 + packed[1:2]
    ids_ref[1:2, :] = packed[2:3] * 64 + packed[3:4]
    ids_ref[2:3, :] = jnp.broadcast_to(number, (1, slots))


def pair_kernel(plan, refs_in, refs_out, scratch):
    tiles, slots, near_number, far_number, list_group = plan
    (blocks, lists, near_sum, far_sum, ids_vmem, ids, left_ref, wide_ref, cross_ref, part_ref, sums_ref, spots_ref,
     sems, list_sems, out_sems) = scratch
    list_copies = [
        pltpu.make_async_copy(source.at[list_group], lists.at[k], list_sems.at[k]) for k, source in enumerate(refs_in)
    ]
    copies = [pltpu.make_async_copy(source, blocks.at[k], sems.at[k]) for k, source in enumerate(refs_in)]
    for copy in list_copies + copies:
        copy.start()
    near_sum[...] = jnp.zeros_like(near_sum)
    far_sum[...] = jnp.zeros_like(far_sum)
    wide_ref[...] = jnp.zeros_like(wide_ref)
    for copy in list_copies:
        copy.wait()

    width = blocks.shape[-1]
    shape = (4, width)
    position = lax.broadcasted_iota(jnp.int32, shape, 0) * width + lax.broadcasted_iota(jnp.int32, shape, 1)
    near_ids = jnp.full(shape, -1.0)
    for k in range(near_number):
        given = lists[k, 0:4]
        given = jnp.where(given >= 0, given + k * tiles, given)
        near_ids = jnp.where(position // (far_number * slots) == k, given, near_ids)
    far_ids = jnp.zeros(shape)
    for k in range(far_number):
        given = lists[near_number - 1 + k if k else 0, 4:8] + k * tiles
        far_ids = jnp.where(position // slots % far_number == k, given, far_ids)
    live_list(near_ids, far_ids, ids_vmem)
    move = pltpu.make_async_copy(ids_vmem, ids, list_sems.at[0])
    move.start()
    move.wait()
    count = ids[2, 0]
    last = ids.shape[1] - 1
    for copy in copies:
        copy.wait()

    def tile_of(block, tile):
        return blocks[block, tile], blocks[block, tiles + tile // 8, pl.ds(tile % 8, 1), :]

    def pick(group, k):
        at = group * GROUP + k
        held = jnp.clip(at, 0, last)
        near, far = ids[0, held], ids[1, held]
        live = jnp.logical_and(at >= 0, at < count)
        return live, near // tiles, near % tiles, far // tiles, far % tiles

    def step(group, carry):
        for k in range(GROUP):
            live, near_block, near_tile, far_block, far_tile = pick(group - 2, k)
            stash = lax.rem(group + 1, 3)
            near_rows, far_rows = sums_ref[stash, k, 0], sums_ref[stash, k, 1]
            parts = part_ref[k]
            half = parts.shape[1] // 2
            for block, tile, spot, total, out in (
                (near_block, near_tile, 0, matmul(jnp.concatenate([far_rows, far_rows], axis=1), parts, (1, 1)), near_sum),
                (far_block, far_tile, 1, matmul(near_rows, parts), far_sum),
            ):
                total = total[0:8] + total[8:16] + total[16:24]
                if total.shape[1] > half:
                    total = total[:, :half] + total[:, half:]
                force = spots_ref[stash, k, spot] * jnp.broadcast_to(total[4:5], total.shape) - total
                out[block, tile] += jnp.where(live, force, 0.0)
        for k in range(GROUP):
            left = left_ref[k]
            terms = matmul(left, wide_ref[k])
            more = matmul(left[:, : cross_ref.shape[1]], cross_ref[k])
            spread, burgers_dot = terms[:, :width], terms[:, width:]
            inverse = lax.rsqrt(spread)
            coupling = (burgers_dot + more[:, :width] * more[:, width:]) * (inverse * inverse * inverse)
            high, low = halves(coupling)
            part_ref[k, :, :width] = high
            part_ref[k, :, width:] = low
        for k in range(GROUP):
            live, near_block, near_tile, far_block, far_tile = pick(group, k)
            far_place = jnp.where(far_block > 0, far_block + (near_number - 1), 0)
            left, spread, dots, near_rows, near_spot, far_rows, far_spot = operands(
                *tile_of(near_block, near_tile), *tile_of(far_place, far_tile)
            )
            stash = lax.rem(group, 3)
            left_ref[k] = left
            wide_ref[k, :, :width] = spread
            wide_ref[k, : dots[0].shape[0], width:] = dots[0]
            cross_ref[k, :, :width] = dots[1]
            cross_ref[k, :, width:] = dots[2]
            sums_ref[stash, k, 0] = near_rows
            sums_ref[stash, k, 1] = far_rows
            spots_ref[stash, k, 0] = near_spot
            spots_ref[stash, k, 1] = far_spot
        return carry

    lax.fori_loop(0, (count + GROUP - 1) // GROUP + 2, step, 0)

    for total, outs in ((near_sum, refs_out[:near_number]), (far_sum, refs_out[near_number:])):
        for k, out in enumerate(outs):
            for axis, row in enumerate((6, 7, 5)):
                out[axis] = total[k, :, row, :]


def run_pairs(blocks, tiles, slots, near_number, far_number, list_group):
    width = blocks[0].shape[-1]
    number = near_number + far_number
    slot_count = near_number * far_number * slots
    hbm = pl.BlockSpec(memory_space=pl.ANY)
    vmem = pl.BlockSpec(memory_space=pltpu.VMEM)
    forces = (3, tiles, width)
    plan = (tiles, slots, near_number, far_number, list_group)
    depth, dot_depth, sum_rows = 64, 32, 32

    def kernel(*refs):
        given = len(blocks)
        pair_kernel(plan, refs[:given], refs[given : given + number], refs[given + number :])

    return pl.pallas_call(
        kernel,
        out_shape=[jax.ShapeDtypeStruct(forces, jnp.float32)] * number,
        in_specs=[hbm] * len(blocks),
        out_specs=[vmem] * number,
        scratch_shapes=[
            pltpu.VMEM((len(blocks),) + blocks[0].shape, jnp.float32),
            pltpu.VMEM((len(blocks), 8, width), jnp.float32),
            pltpu.VMEM((near_number, tiles, 8, width), jnp.float32),
            pltpu.VMEM((far_number, tiles, 8, width), jnp.float32),
            pltpu.VMEM((8, slot_count), jnp.int32),
            pltpu.SMEM((8, slot_count), jnp.int32),
            pltpu.VMEM((GROUP, width, depth), jnp.bfloat16),
            pltpu.VMEM((GROUP, depth, 2 * width), jnp.bfloat16),
            pltpu.VMEM((GROUP, dot_depth, 2 * width), jnp.bfloat16),
            pltpu.VMEM((GROUP, width, 2 * width), jnp.bfloat16),
            pltpu.VMEM((3, GROUP, 2, sum_rows, width), jnp.bfloat16),
            pltpu.VMEM((3, GROUP, 2, 8, width), jnp.float32),
            pltpu.SemaphoreType.DMA((len(blocks),)),
            pltpu.SemaphoreType.DMA((len(blocks),)),
            pltpu.SemaphoreType.DMA((number,)),
        ],
        compiler_params=pltpu.CompilerParams(vmem_limit_bytes=60 * 1024 * 1024),
        name="pairs",
    )(*blocks)


def tile_groups(tiles):
    main = jnp.concatenate([tiles[..., 3:9, :], tiles[..., 0:2, :]], axis=-2)
    rows = tiles[..., 2, :]
    short = -rows.shape[-2] % 8
    rows = jnp.pad(rows, [(0, 0)] * (rows.ndim - 2) + [(0, short), (0, 0)])
    rows = rows.reshape(rows.shape[:-2] + (rows.shape[-2] // 8, 8, rows.shape[-1]))
    return jnp.concatenate([main, rows], axis=-3)


NCELL = 64


def far_field(segments, tile_cell, moment_sums, total_segments):
    moments = moment_sums.reshape(NCELL, 3, 3) / jnp.sqrt(jnp.float32(total_segments))
    moments = 0.5 * (moments + jnp.transpose(moments, (0, 2, 1)))
    cells = jnp.arange(NCELL).astype(jnp.float32)
    weights = 8.0 / (8.0 + jnp.abs(cells[:, None] - cells[None, :]))
    stress = jnp.dot(weights, moments.reshape(NCELL, 9), precision=lax.Precision.HIGHEST)
    onehot = (tile_cell[:, None] == jnp.arange(NCELL)[None, :]).astype(jnp.float32)
    tile_stress = jnp.dot(onehot, stress, precision=lax.Precision.HIGHEST).reshape(-1, 3, 3)
    traction = jnp.sum(tile_stress[:, :, :, None] * segments[:, None, 3:6, :], axis=2)
    lines = segments[:, 6:9, :]
    return jnp.stack(
        [
            traction[:, 1] * lines[:, 2] - traction[:, 2] * lines[:, 1],
            traction[:, 2] * lines[:, 0] - traction[:, 0] * lines[:, 2],
            traction[:, 0] * lines[:, 1] - traction[:, 1] * lines[:, 0],
        ],
        axis=1,
    )


def local_moments(segments, tile_cell):
    outer = jnp.sum(segments[:, 3:6, None, :] * segments[:, None, 6:9, :], axis=3).reshape(-1, 9)
    onehot = (jnp.arange(NCELL)[:, None] == tile_cell[None, :]).astype(jnp.float32)
    return jnp.dot(onehot, outer, precision=lax.Precision.HIGHEST)


AXES = ("dom", "sub")


def swap(value, mask):
    devices = lax.axis_size(AXES)
    return lax.ppermute(value, AXES, [(k, k ^ mask) for k in range(devices)])


def span(steps):
    masks = [0]
    for step in steps:
        masks += [mask ^ step for mask in masks]
    return masks


def mask_steps(devices):
    bits = devices.bit_length() - 1
    number = bits // 2
    far_steps = [devices >> (k + 2) for k in range(number)]
    near_steps = [devices >> 1] + [devices >> (k + 1) for k in range(number + 1, bits)]
    return near_steps, far_steps


def spread(block, near_steps, far_steps):
    steps = list(near_steps) + list(far_steps)
    allowed = set(span(near_steps)) | set(span(far_steps))
    held = {0: block}
    fresh = {0: -1}
    while fresh:
        arrived = {}
        for mask, last in fresh.items():
            for at in range(last + 1, len(steps)):
                if mask ^ steps[at] in allowed:
                    arrived[mask ^ steps[at]] = (swap(held[mask], steps[at]), at)
        if arrived:
            values = lax.optimization_barrier([value for value, at in arrived.values()])
            held.update(zip(arrived, values))
        fresh = {mask: at for mask, (value, at) in arrived.items()}
    return [held[mask] for mask in span(near_steps)], [held[mask] for mask in span(far_steps)]


def collect(near_parts, near_steps, far_parts, far_steps):
    totals = []
    for parts, steps in ((near_parts, near_steps), (far_parts, far_steps)):
        parts = list(parts)
        for step in reversed(steps):
            half = len(parts) // 2
            received = [swap(part, step) for part in reversed(parts[half:])]
            parts = [part + got for part, got in zip(parts[:half], reversed(received))]
        totals.append(parts[0])
    return totals[0] + totals[1]


def rows_of(values, width):
    flat = values.reshape(-1).astype(jnp.float32)
    groups = -(-flat.shape[0] // (8 * width))
    return jnp.pad(flat, (0, groups * 8 * width - flat.shape[0])).reshape(groups, 8, width)


def on_device(segments, send_tiles, pair_local, pair_remote, pair_count, tile_cell):
    width = segments.shape[2]
    tiles = segments.shape[0]
    devices = send_tiles.shape[1]
    slots = send_tiles.shape[2]
    pairs = pair_local.shape[1]
    near_steps, far_steps = mask_steps(devices)
    near_masks, far_masks = span(near_steps), span(far_steps)

    live = jnp.arange(pairs) < pair_count[0]
    me = lax.axis_index(AXES).astype(jnp.int32)
    peers = jnp.bitwise_xor(me, jnp.array([near ^ far for near in near_masks for far in far_masks], jnp.int32))
    order = (peers[:, None] * slots + jnp.arange(slots)[None, :]).reshape(-1)
    named = jnp.logical_and(pair_remote[0][:, None] == order[None, :], live[:, None])
    table = jnp.sum(jnp.where(named, pair_local[0][:, None] + 1, 0), axis=0) - 1
    chosen = peers[:, None] == jnp.arange(devices)[None, :]
    sent = jnp.sum(jnp.where(chosen[:, :, None], send_tiles[0][None], 0), axis=1)
    lists = jnp.concatenate([table, sent.reshape(-1)])
    moments = local_moments(segments, tile_cell)
    list_rows, moment_rows = rows_of(lists, width), rows_of(moments, width)
    main = tile_groups(segments)
    block = jnp.concatenate([main, list_rows, moment_rows], axis=0)

    near_blocks, far_blocks = spread(block, near_steps, far_steps)
    at_lists = main.shape[0]
    at_moments = at_lists + list_rows.shape[0]
    sums = functools.reduce(jnp.add, [given[at_moments:] for given in near_blocks])
    outs = run_pairs(near_blocks + far_blocks[1:], tiles, slots, len(near_masks), len(far_masks), at_lists)
    outs, sums = lax.optimization_barrier((outs, sums))
    for step in far_steps:
        sums = sums + swap(sums, step)
    moment_sums = sums.reshape(-1)[: NCELL * 9].reshape(NCELL, 9)
    forces = collect(outs[: len(near_masks)], near_steps, outs[len(near_masks) :], far_steps)
    total_segments = tiles * width * devices
    return forces.transpose(1, 0, 2) + far_field(segments, tile_cell, moment_sums, total_segments)


def solution(mesh):
    in_specs = (
        P(("dom", "sub"), None, None),
        P(("dom", "sub"), None, None),
        P(("dom", "sub"), None),
        P(("dom", "sub"), None),
        P(("dom", "sub")),
        P(("dom", "sub")),
    )
    out_specs = P(("dom", "sub"), None, None)
    return jax.shard_map(
        on_device, mesh=mesh, in_specs=in_specs, out_specs=out_specs, check_vma=False
    )
```

```python
import functools
import jax
import jax.numpy as jnp
from jax import lax
from jax.sharding import PartitionSpec as P
from jax.experimental import pallas as pl
from jax.experimental.pallas import tpu as pltpu

CORE = 0.25
GROUP = 8


def head(value):
    return value.astype(jnp.bfloat16).astype(jnp.float32)


def thirds(value):
    high = head(value)
    rest = value - high
    middle = head(rest)
    return high, middle, rest - middle


def halves(value):
    high = value.astype(jnp.bfloat16)
    return high, (value - high.astype(jnp.float32)).astype(jnp.bfloat16)


def tall(groups):
    return jnp.concatenate(groups, axis=0).astype(jnp.bfloat16)


def place(sub, rows, others=0.0):
    filled = others
    for at, row in rows.items():
        filled = jnp.where(sub == at, row, filled)
    return filled


def tile_parts(sub, tile, row):
    row = jnp.broadcast_to(row, tile.shape)
    square = row * row
    for at in (6, 7):
        other = jnp.broadcast_to(tile[at : at + 1], tile.shape)
        square = square + other * other
    main, last = thirds(tile), thirds(row)
    positions = [jnp.where(sub >= 6, m, jnp.where(sub == 5, r, 0.0)) for m, r in zip(main[:2], last[:2])]
    sums = tall([jnp.where(sub == 4, 1.0, positions[0]), positions[1]])
    spot = jnp.where(sub >= 6, tile, jnp.where(sub == 5, row, 0.0))
    return main, last, square, sums, spot


def operands(near, near_row, far, far_row):
    sub = lax.broadcasted_iota(jnp.int32, near.shape, 0)
    first = sub < 3
    second = jnp.logical_and(sub >= 3, sub < 6)
    zero = jnp.zeros_like(near)
    scale = 1.0 / near.shape[1]
    middle = jnp.where(sub >= 6, jnp.sum(near, axis=1, keepdims=True) * scale, 0.0)
    middle_row = jnp.sum(near_row, axis=1, keepdims=True) * scale
    near, far = near - middle, far - middle
    near_row, far_row = near_row - middle_row, far_row - middle_row
    (high, mid, low), (row_high, row_mid, row_low), square, near_sums, near_spot = tile_parts(sub, near, near_row)
    square_parts = thirds(square)
    left = tall(
        [
            high, mid, high, low, high, mid,
            place(sub, {0: row_high, 1: row_mid, 2: row_high, 3: row_low, 4: row_high, 5: row_mid}),
            place(sub, {0: square_parts[0], 1: square_parts[1], 2: square_parts[2]}, jnp.where(second, 1.0, 0.0)),
        ]
    )
    (high, mid, low), (row_high, row_mid, row_low), square, far_sums, far_spot = tile_parts(sub, far, far_row)
    square_parts = thirds(square + CORE)
    twice = [jnp.where(sub >= 6, -2.0 * part, 0.0) for part in (high, mid, low)]
    twice_row = [-2.0 * part for part in (row_high, row_mid, row_low)]
    spread = tall(
        [
            twice[0], twice[0], twice[1], twice[0], twice[2], twice[1],
            place(sub, {0: twice_row[0], 1: twice_row[0], 2: twice_row[1], 3: twice_row[0], 4: twice_row[2], 5: twice_row[1]}, zero),
            place(sub, {3: square_parts[0], 4: square_parts[1], 5: square_parts[2]}, jnp.where(first, 1.0, 0.0)),
        ]
    )
    dots = []
    for part in (
        [jnp.where(first, part, 0.0) for part in (high, mid)],
        [jnp.where(first, pltpu.roll(part, 5, 0), 0.0) for part in (high, mid)],
        [jnp.where(second, pltpu.roll(part, 3, 0), 0.0) for part in (high, mid)],
    ):
        dots.append(tall([part[0], part[0], part[1], zero]))
    return left.T, spread, dots, near_sums, near_spot, far_sums, far_spot


def matmul(left, right, contract=(1, 0)):
    dims = (((contract[0],), (contract[1],)), ((), ()))
    return lax.dot_general(left, right, dims, preferred_element_type=jnp.float32)


def live_list(near_rows, far_rows, ids_ref):
    slots = ids_ref.shape[1]

    def line(rows):
        return jnp.concatenate([rows[k : k + 1] for k in range(rows.shape[0])], axis=1)

    near, far = line(near_rows), line(far_rows)
    alive = near >= 0
    row = lax.broadcasted_iota(jnp.int32, (slots, slots), 0)
    lane = lax.broadcasted_iota(jnp.int32, (slots, slots), 1)
    before = jnp.where(row < lane, 1.0, 0.0).astype(jnp.bfloat16)
    flags = jnp.where(alive, 1.0, 0.0)
    rank = matmul(jnp.broadcast_to(flags, (8, slots)).astype(jnp.bfloat16), before)[0:1]
    rank = jnp.where(alive, rank, -1.0)
    chosen = jnp.where(jnp.broadcast_to(rank, (slots, slots)) == row.astype(jnp.float32), 1.0, 0.0).astype(jnp.bfloat16)
    sub = lax.broadcasted_iota(jnp.int32, (8, slots), 0)
    near, far = jnp.maximum(near, 0).astype(jnp.int32), far.astype(jnp.int32)
    values = [near >> 6, near & 63, far >> 6, far & 63]
    values = place(sub, {k: value.astype(jnp.float32) for k, value in enumerate(values)}, jnp.zeros((8, slots), jnp.float32))
    packed = matmul(values.astype(jnp.bfloat16), chosen, (1, 1)).astype(jnp.int32)
    number = jnp.sum(flags, axis=1, keepdims=True).astype(jnp.int32)
    ids_ref[0:1, :] = packed[0:1] * 64 + packed[1:2]
    ids_ref[1:2, :] = packed[2:3] * 64 + packed[3:4]
    ids_ref[2:3, :] = jnp.broadcast_to(number, (1, slots))


def pair_kernel(plan, refs_in, refs_out, scratch):
    tiles, slots, near_number, far_number, list_group = plan
    (blocks, lists, near_sum, far_sum, ids_vmem, ids, left_ref, wide_ref, cross_ref, part_ref, sums_ref, spots_ref,
     sems, list_sems) = scratch
    list_copies = [
        pltpu.make_async_copy(source.at[pl.ds(list_group, 2)], lists.at[k], list_sems.at[k]) for k, source in enumerate(refs_in)
    ]
    copies = [pltpu.make_async_copy(source, blocks.at[k], sems.at[k]) for k, source in enumerate(refs_in)]
    for copy in list_copies + copies:
        copy.start()
    near_sum[...] = jnp.zeros_like(near_sum)
    far_sum[...] = jnp.zeros_like(far_sum)
    wide_ref[...] = jnp.zeros_like(wide_ref)
    for copy in list_copies:
        copy.wait()

    width = blocks.shape[-1]
    shape = (4, width)
    position = lax.broadcasted_iota(jnp.int32, shape, 0) * width + lax.broadcasted_iota(jnp.int32, shape, 1)
    near_ids = jnp.full(shape, -1.0)
    for k in range(near_number):
        given = lists[k, 0, 0:4]
        given = jnp.where(given >= 0, given + k * tiles, given)
        near_ids = jnp.where(position // (far_number * slots) == k, given, near_ids)
    far_ids = jnp.zeros(shape)
    for k in range(far_number):
        given = lists[near_number - 1 + k if k else 0, 0, 4:8] + k * tiles
        far_ids = jnp.where(position // slots % far_number == k, given, far_ids)
    live_list(near_ids, far_ids, ids_vmem)
    move = pltpu.make_async_copy(ids_vmem, ids, list_sems.at[0])
    move.start()
    move.wait()
    count = ids[2, 0]
    last = ids.shape[1] - 1
    for copy in copies:
        copy.wait()

    def tile_of(block, tile):
        return blocks[block, tile], blocks[block, tiles + tile // 8, pl.ds(tile % 8, 1), :]

    def pick(group, k):
        at = group * GROUP + k
        held = jnp.clip(at, 0, last)
        near, far = ids[0, held], ids[1, held]
        live = jnp.logical_and(at >= 0, at < count)
        return live, near // tiles, near % tiles, far // tiles, far % tiles

    def step(group, carry):
        for k in range(GROUP):
            live, near_block, near_tile, far_block, far_tile = pick(group - 2, k)
            stash = lax.rem(group + 1, 3)
            near_rows, far_rows = sums_ref[stash, k, 0], sums_ref[stash, k, 1]
            parts = part_ref[k]
            half = parts.shape[1] // 2
            for block, tile, spot, total, out in (
                (near_block, near_tile, 0, matmul(jnp.concatenate([far_rows, far_rows], axis=1), parts, (1, 1)), near_sum),
                (far_block, far_tile, 1, matmul(near_rows, parts), far_sum),
            ):
                total = total[0:8] + total[8:16]
                if total.shape[1] > half:
                    total = total[:, :half] + total[:, half:]
                force = spots_ref[stash, k, spot] * jnp.broadcast_to(total[4:5], total.shape) - total
                out[block, tile] += jnp.where(live, force, 0.0)
        for k in range(GROUP):
            left = left_ref[k]
            terms = matmul(left, wide_ref[k])
            more = matmul(left[:, : cross_ref.shape[1]], cross_ref[k])
            spread, burgers_dot = terms[:, :width], terms[:, width:]
            inverse = lax.rsqrt(spread)
            coupling = (burgers_dot + more[:, :width] * more[:, width:]) * (inverse * inverse * inverse)
            high, low = halves(coupling)
            part_ref[k, :, :width] = high
            part_ref[k, :, width:] = low
        for k in range(GROUP):
            live, near_block, near_tile, far_block, far_tile = pick(group, k)
            far_place = jnp.where(far_block > 0, far_block + (near_number - 1), 0)
            left, spread, dots, near_rows, near_spot, far_rows, far_spot = operands(
                *tile_of(near_block, near_tile), *tile_of(far_place, far_tile)
            )
            stash = lax.rem(group, 3)
            left_ref[k] = left
            wide_ref[k, :, :width] = spread
            wide_ref[k, : dots[0].shape[0], width:] = dots[0]
            cross_ref[k, :, :width] = dots[1]
            cross_ref[k, :, width:] = dots[2]
            sums_ref[stash, k, 0] = near_rows
            sums_ref[stash, k, 1] = far_rows
            spots_ref[stash, k, 0] = near_spot
            spots_ref[stash, k, 1] = far_spot
        return carry

    lax.fori_loop(0, (count + GROUP - 1) // GROUP + 2, step, 0)

    moments = functools.reduce(jnp.add, [lists[k, 1] for k in range(near_number)])
    at = 0
    for out in refs_out:
        for k in range(out.shape[0]):
            total, block = (near_sum, at) if at < near_number else (far_sum, at - near_number)
            for axis, row in enumerate((6, 7, 5)):
                out[k, axis * tiles : (axis + 1) * tiles, :] = total[block, :, row, :]
            if at >= near_number:
                out[k, 3 * tiles :, :] = moments
            at += 1


def run_pairs(blocks, tiles, slots, near_counts, far_counts, list_group):
    width = blocks[0].shape[-1]
    near_number, far_number = sum(near_counts), sum(far_counts)
    slot_count = near_number * far_number * slots
    hbm = pl.BlockSpec(memory_space=pl.ANY)
    vmem = pl.BlockSpec(memory_space=pltpu.VMEM)
    plan = (tiles, slots, near_number, far_number, list_group)
    shapes = [(count, 3 * tiles, width) for count in near_counts]
    shapes += [(count, 3 * tiles + 8, width) for count in far_counts]
    depth, dot_depth, sum_rows = 64, 32, 16

    def kernel(*refs):
        given = len(blocks)
        pair_kernel(plan, refs[:given], refs[given : given + len(shapes)], refs[given + len(shapes) :])

    return pl.pallas_call(
        kernel,
        out_shape=[jax.ShapeDtypeStruct(shape, jnp.float32) for shape in shapes],
        in_specs=[hbm] * len(blocks),
        out_specs=[vmem] * len(shapes),
        scratch_shapes=[
            pltpu.VMEM((len(blocks),) + blocks[0].shape, jnp.float32),
            pltpu.VMEM((len(blocks), 2, 8, width), jnp.float32),
            pltpu.VMEM((near_number, tiles, 8, width), jnp.float32),
            pltpu.VMEM((far_number, tiles, 8, width), jnp.float32),
            pltpu.VMEM((8, slot_count), jnp.int32),
            pltpu.SMEM((8, slot_count), jnp.int32),
            pltpu.VMEM((GROUP, width, depth), jnp.bfloat16),
            pltpu.VMEM((GROUP, depth, 2 * width), jnp.bfloat16),
            pltpu.VMEM((GROUP, dot_depth, 2 * width), jnp.bfloat16),
            pltpu.VMEM((GROUP, width, 2 * width), jnp.bfloat16),
            pltpu.VMEM((3, GROUP, 2, sum_rows, width), jnp.bfloat16),
            pltpu.VMEM((3, GROUP, 2, 8, width), jnp.float32),
            pltpu.SemaphoreType.DMA((len(blocks),)),
            pltpu.SemaphoreType.DMA((len(blocks),)),
        ],
        compiler_params=pltpu.CompilerParams(vmem_limit_bytes=60 * 1024 * 1024),
        name="pairs",
    )(*blocks)


def tile_groups(tiles):
    main = jnp.concatenate([tiles[..., 3:9, :], tiles[..., 0:2, :]], axis=-2)
    rows = tiles[..., 2, :]
    short = -rows.shape[-2] % 8
    rows = jnp.pad(rows, [(0, 0)] * (rows.ndim - 2) + [(0, short), (0, 0)])
    rows = rows.reshape(rows.shape[:-2] + (rows.shape[-2] // 8, 8, rows.shape[-1]))
    return jnp.concatenate([main, rows], axis=-3)


NCELL = 64


def far_field(segments, tile_cell, moment_sums, total_segments):
    moments = moment_sums.reshape(NCELL, 3, 3) / jnp.sqrt(jnp.float32(total_segments))
    moments = 0.5 * (moments + jnp.transpose(moments, (0, 2, 1)))
    cells = jnp.arange(NCELL).astype(jnp.float32)
    weights = 8.0 / (8.0 + jnp.abs(cells[:, None] - cells[None, :]))
    stress = jnp.dot(weights, moments.reshape(NCELL, 9), precision=lax.Precision.HIGHEST)
    onehot = (tile_cell[:, None] == jnp.arange(NCELL)[None, :]).astype(jnp.float32)
    tile_stress = jnp.dot(onehot, stress, precision=lax.Precision.HIGHEST).reshape(-1, 3, 3)
    traction = jnp.sum(tile_stress[:, :, :, None] * segments[:, None, 3:6, :], axis=2)
    lines = segments[:, 6:9, :]
    return jnp.stack(
        [
            traction[:, 1] * lines[:, 2] - traction[:, 2] * lines[:, 1],
            traction[:, 2] * lines[:, 0] - traction[:, 0] * lines[:, 2],
            traction[:, 0] * lines[:, 1] - traction[:, 1] * lines[:, 0],
        ],
        axis=1,
    )


def local_moments(segments, tile_cell):
    outer = jnp.sum(segments[:, 3:6, None, :] * segments[:, None, 6:9, :], axis=3).reshape(-1, 9)
    onehot = (jnp.arange(NCELL)[:, None] == tile_cell[None, :]).astype(jnp.float32)
    return jnp.dot(onehot, outer, precision=lax.Precision.HIGHEST)


AXES = ("dom", "sub")


def swap(value, mask):
    devices = lax.axis_size(AXES)
    return lax.ppermute(value, AXES, [(k, k ^ mask) for k in range(devices)])


def span(steps):
    masks = [0]
    for step in steps:
        masks += [mask ^ step for mask in masks]
    return masks


def mask_steps(devices):
    bits = devices.bit_length() - 1
    number = bits // 2
    far_steps = [devices >> (k + 2) for k in range(number)]
    near_steps = [devices >> 1] + [devices >> (k + 1) for k in range(number + 1, bits)]
    return near_steps, far_steps


def spread(block, near_steps, far_steps):
    steps = list(near_steps) + list(far_steps)
    allowed = set(span(near_steps)) | set(span(far_steps))
    held = {0: block}
    fresh = {0: -1}
    while fresh:
        arrived = {}
        for mask, last in fresh.items():
            for at in range(last + 1, len(steps)):
                if mask ^ steps[at] in allowed:
                    arrived[mask ^ steps[at]] = (swap(held[mask], steps[at]), at)
        if arrived:
            values = lax.optimization_barrier([value for value, at in arrived.values()])
            held.update(zip(arrived, values))
        fresh = {mask: at for mask, (value, at) in arrived.items()}
    return [held[mask] for mask in span(near_steps)], [held[mask] for mask in span(far_steps)]


def message_counts(steps):
    counts = [1] * min(len(steps) and 2, 1 << len(steps))
    while sum(counts) < 1 << len(steps):
        counts.append(2 if sum(counts) >= 4 or len(steps) < 3 else 1)
    return counts


def collect(outs, counts, steps):
    groups = list(zip(outs, counts))
    for step in reversed(steps):
        half = sum(count for value, count in groups) // 2
        kept, sent, seen = [], [], 0
        for value, count in groups:
            (kept if seen < half else sent).append((value, count))
            seen += count
        arrived = []
        for value, count in reversed(sent):
            got = swap(value, step)
            arrived = [got[k : k + 1] for k in range(count)] + arrived
        merged, at = [], 0
        for value, count in kept:
            more = arrived[at : at + count]
            merged.append((value + (jnp.concatenate(more) if count > 1 else more[0]), count))
            at += count
        groups = merged
    return groups[0][0][0]


def rows_of(values, width):
    flat = values.reshape(-1).astype(jnp.float32)
    groups = -(-flat.shape[0] // (8 * width))
    return jnp.pad(flat, (0, groups * 8 * width - flat.shape[0])).reshape(groups, 8, width)


def on_device(segments, send_tiles, pair_local, pair_remote, pair_count, tile_cell):
    width = segments.shape[2]
    tiles = segments.shape[0]
    devices = send_tiles.shape[1]
    slots = send_tiles.shape[2]
    pairs = pair_local.shape[1]
    near_steps, far_steps = mask_steps(devices)
    near_masks, far_masks = span(near_steps), span(far_steps)

    live = jnp.arange(pairs) < pair_count[0]
    me = lax.axis_index(AXES).astype(jnp.int32)
    peers = jnp.bitwise_xor(me, jnp.array([near ^ far for near in near_masks for far in far_masks], jnp.int32))
    order = (peers[:, None] * slots + jnp.arange(slots)[None, :]).reshape(-1)
    named = jnp.logical_and(pair_remote[0][:, None] == order[None, :], live[:, None])
    table = jnp.sum(jnp.where(named, pair_local[0][:, None] + 1, 0), axis=0) - 1
    chosen = peers[:, None] == jnp.arange(devices)[None, :]
    sent = jnp.sum(jnp.where(chosen[:, :, None], send_tiles[0][None], 0), axis=1)
    lists = jnp.concatenate([table, sent.reshape(-1)])
    moments = local_moments(segments, tile_cell)
    list_rows, moment_rows = rows_of(lists, width), rows_of(moments, width)
    main = tile_groups(segments)
    block = jnp.concatenate([main, list_rows, moment_rows], axis=0)

    near_blocks, far_blocks = spread(block, near_steps, far_steps)
    at_lists = main.shape[0]
    near_counts, far_counts = message_counts(near_steps), message_counts(far_steps)
    outs = run_pairs(near_blocks + far_blocks[1:], tiles, slots, near_counts, far_counts, at_lists)
    near_total = collect(outs[: len(near_counts)], near_counts, near_steps)
    far_total = collect(outs[len(near_counts) :], far_counts, far_steps)
    forces = (near_total + far_total[: 3 * tiles]).reshape(3, tiles, width)
    moment_sums = far_total[3 * tiles :].reshape(-1)[: NCELL * 9].reshape(NCELL, 9)
    total_segments = tiles * width * devices
    return forces.transpose(1, 0, 2) + far_field(segments, tile_cell, moment_sums, total_segments)


def solution(mesh):
    in_specs = (
        P(("dom", "sub"), None, None),
        P(("dom", "sub"), None, None),
        P(("dom", "sub"), None),
        P(("dom", "sub"), None),
        P(("dom", "sub")),
        P(("dom", "sub")),
    )
    out_specs = P(("dom", "sub"), None, None)
    return jax.shard_map(
        on_device, mesh=mesh, in_specs=in_specs, out_specs=out_specs, check_vma=False
    )
```

```python
import functools
import jax
import jax.numpy as jnp
from jax import lax
from jax.sharding import PartitionSpec as P
from jax.experimental import pallas as pl
from jax.experimental.pallas import tpu as pltpu

CORE = 0.25
GROUP = 8


def head(value):
    return value.astype(jnp.bfloat16).astype(jnp.float32)


def thirds(value):
    high = head(value)
    rest = value - high
    middle = head(rest)
    return high, middle, rest - middle


def halves(value):
    high = value.astype(jnp.bfloat16)
    return high, (value - high.astype(jnp.float32)).astype(jnp.bfloat16)


def tall(groups):
    return jnp.concatenate(groups, axis=0).astype(jnp.bfloat16)


def place(sub, rows, others=0.0):
    filled = others
    for at, row in rows.items():
        filled = jnp.where(sub == at, row, filled)
    return filled


def tile_parts(sub, tile, row):
    row = jnp.broadcast_to(row, tile.shape)
    square = row * row
    for at in (6, 7):
        other = jnp.broadcast_to(tile[at : at + 1], tile.shape)
        square = square + other * other
    main, last = thirds(tile), thirds(row)
    positions = [jnp.where(sub >= 6, m, jnp.where(sub == 5, r, 0.0)) for m, r in zip(main[:2], last[:2])]
    sums = tall([jnp.where(sub == 4, 1.0, positions[0]), positions[1]])
    spot = jnp.where(sub >= 6, tile, jnp.where(sub == 5, row, 0.0))
    return main, last, square, sums, spot


def operands(near, near_row, far, far_row):
    sub = lax.broadcasted_iota(jnp.int32, near.shape, 0)
    first = sub < 3
    second = jnp.logical_and(sub >= 3, sub < 6)
    zero = jnp.zeros_like(near)
    scale = 1.0 / near.shape[1]
    middle = jnp.where(sub >= 6, jnp.sum(near, axis=1, keepdims=True) * scale, 0.0)
    middle_row = jnp.sum(near_row, axis=1, keepdims=True) * scale
    near, far = near - middle, far - middle
    near_row, far_row = near_row - middle_row, far_row - middle_row
    (high, mid, low), (row_high, row_mid, row_low), square, near_sums, near_spot = tile_parts(sub, near, near_row)
    square_parts = thirds(square)
    left = tall(
        [
            high, mid, high, low, high, mid,
            place(sub, {0: row_high, 1: row_mid, 2: row_high, 3: row_low, 4: row_high, 5: row_mid}),
            place(sub, {0: square_parts[0], 1: square_parts[1], 2: square_parts[2]}, jnp.where(second, 1.0, 0.0)),
        ]
    )
    (high, mid, low), (row_high, row_mid, row_low), square, far_sums, far_spot = tile_parts(sub, far, far_row)
    square_parts = thirds(square + CORE)
    twice = [jnp.where(sub >= 6, -2.0 * part, 0.0) for part in (high, mid, low)]
    twice_row = [-2.0 * part for part in (row_high, row_mid, row_low)]
    spread = tall(
        [
            twice[0], twice[0], twice[1], twice[0], twice[2], twice[1],
            place(sub, {0: twice_row[0], 1: twice_row[0], 2: twice_row[1], 3: twice_row[0], 4: twice_row[2], 5: twice_row[1]}, zero),
            place(sub, {3: square_parts[0], 4: square_parts[1], 5: square_parts[2]}, jnp.where(first, 1.0, 0.0)),
        ]
    )
    dots = []
    for part in (
        [jnp.where(first, part, 0.0) for part in (high, mid)],
        [jnp.where(first, pltpu.roll(part, 5, 0), 0.0) for part in (high, mid)],
        [jnp.where(second, pltpu.roll(part, 3, 0), 0.0) for part in (high, mid)],
    ):
        dots.append(tall([part[0], part[0], part[1], zero]))
    return left.T, spread, dots, near_sums, near_spot, far_sums, far_spot


def matmul(left, right, contract=(1, 0)):
    dims = (((contract[0],), (contract[1],)), ((), ()))
    return lax.dot_general(left, right, dims, preferred_element_type=jnp.float32)


def live_list(near_rows, far_rows, ids_ref):
    slots = ids_ref.shape[1]

    def line(rows):
        return jnp.concatenate([rows[k : k + 1] for k in range(rows.shape[0])], axis=1)

    near, far = line(near_rows), line(far_rows)
    alive = near >= 0
    row = lax.broadcasted_iota(jnp.int32, (slots, slots), 0)
    lane = lax.broadcasted_iota(jnp.int32, (slots, slots), 1)
    before = jnp.where(row < lane, 1.0, 0.0).astype(jnp.bfloat16)
    flags = jnp.where(alive, 1.0, 0.0)
    rank = matmul(jnp.broadcast_to(flags, (8, slots)).astype(jnp.bfloat16), before)[0:1]
    rank = jnp.where(alive, rank, -1.0)
    chosen = jnp.where(jnp.broadcast_to(rank, (slots, slots)) == row.astype(jnp.float32), 1.0, 0.0).astype(jnp.bfloat16)
    sub = lax.broadcasted_iota(jnp.int32, (8, slots), 0)
    near, far = jnp.maximum(near, 0).astype(jnp.int32), jnp.maximum(far, 0).astype(jnp.int32)
    values = [near >> 6, near & 63, far >> 6, far & 63]
    values = place(sub, {k: value.astype(jnp.float32) for k, value in enumerate(values)}, jnp.zeros((8, slots), jnp.float32))
    packed = matmul(values.astype(jnp.bfloat16), chosen, (1, 1)).astype(jnp.int32)
    number = jnp.sum(flags, axis=1, keepdims=True).astype(jnp.int32)
    ids_ref[0:1, :] = packed[0:1] * 64 + packed[1:2]
    ids_ref[1:2, :] = packed[2:3] * 64 + packed[3:4]
    ids_ref[2:3, :] = jnp.broadcast_to(number, (1, slots))


def pair_kernel(plan, sources, earlier, refs_out, scratch):
    tiles, slots, list_group, near_total, far_total, near, far, done, final = plan
    near_number, far_number = len(near), len(far)
    (blocks, lists, near_sum, far_sum, ids_vmem, ids, left_ref, wide_ref, cross_ref, part_ref, sums_ref, spots_ref,
     sems, list_sems) = scratch
    list_copies = [
        pltpu.make_async_copy(source.at[pl.ds(list_group, 2)], lists.at[k], list_sems.at[k])
        for k, source in enumerate(sources)
    ]
    copies = [pltpu.make_async_copy(source, blocks.at[k], sems.at[k]) for k, source in enumerate(sources)]
    for copy in list_copies + copies:
        copy.start()
    near_sum[...] = jnp.zeros_like(near_sum)
    far_sum[...] = jnp.zeros_like(far_sum)
    wide_ref[...] = jnp.zeros_like(wide_ref)
    for copy in list_copies:
        copy.wait()

    width = blocks.shape[-1]
    shape = (4, width)
    position = lax.broadcasted_iota(jnp.int32, shape, 0) * width + lax.broadcasted_iota(jnp.int32, shape, 1)
    near_ids = jnp.full(shape, -1.0)
    near_at = position // (far_total * slots)
    far_at = position // slots % far_total
    for k, block in enumerate(near):
        given = lists[k, 0, 0:4]
        given = jnp.where(given >= 0, given + k * tiles, given)
        near_ids = jnp.where(near_at == block, given, near_ids)
    far_ids = jnp.full(shape, -1.0)
    for k, block in enumerate(far):
        given = lists[near_number - 1 + k if k else 0, 0, 4:8] + k * tiles
        far_ids = jnp.where(far_at == block, given, far_ids)
    near_ids = jnp.where(far_ids >= 0, near_ids, -1.0)
    if done:
        old_near = functools.reduce(jnp.logical_or, [near_at == block for block in done[0]])
        old_far = functools.reduce(jnp.logical_or, [far_at == block for block in done[1]])
        near_ids = jnp.where(jnp.logical_and(old_near, old_far), -1.0, near_ids)
    live_list(near_ids, far_ids, ids_vmem)
    move = pltpu.make_async_copy(ids_vmem, ids, list_sems.at[0])
    move.start()
    move.wait()
    count = ids[2, 0]
    last = ids.shape[1] - 1
    for copy in copies:
        copy.wait()

    def tile_of(block, tile):
        return blocks[block, tile], blocks[block, tiles + tile // 8, pl.ds(tile % 8, 1), :]

    def pick(group, k):
        at = group * GROUP + k
        held = jnp.clip(at, 0, last)
        near, far = ids[0, held], ids[1, held]
        live = jnp.logical_and(at >= 0, at < count)
        return live, near // tiles, near % tiles, far // tiles, far % tiles

    def step(group, carry):
        for k in range(GROUP):
            live, near_block, near_tile, far_block, far_tile = pick(group - 2, k)
            stash = lax.rem(group + 1, 3)
            near_rows, far_rows = sums_ref[stash, k, 0], sums_ref[stash, k, 1]
            parts = part_ref[k]
            half = parts.shape[1] // 2
            for block, tile, spot, total, out in (
                (near_block, near_tile, 0, matmul(jnp.concatenate([far_rows, far_rows], axis=1), parts, (1, 1)), near_sum),
                (far_block, far_tile, 1, matmul(near_rows, parts), far_sum),
            ):
                total = total[0:8] + total[8:16]
                if total.shape[1] > half:
                    total = total[:, :half] + total[:, half:]
                force = spots_ref[stash, k, spot] * jnp.broadcast_to(total[4:5], total.shape) - total
                out[block, tile] += jnp.where(live, force, 0.0)
        for k in range(GROUP):
            left = left_ref[k]
            terms = matmul(left, wide_ref[k])
            more = matmul(left[:, : cross_ref.shape[1]], cross_ref[k])
            spread, burgers_dot = terms[:, :width], terms[:, width:]
            inverse = lax.rsqrt(spread)
            coupling = (burgers_dot + more[:, :width] * more[:, width:]) * (inverse * inverse * inverse)
            high, low = halves(coupling)
            part_ref[k, :, :width] = high
            part_ref[k, :, width:] = low
        for k in range(GROUP):
            live, near_block, near_tile, far_block, far_tile = pick(group, k)
            far_place = jnp.where(far_block > 0, far_block + (near_number - 1), 0)
            left, spread, dots, near_rows, near_spot, far_rows, far_spot = operands(
                *tile_of(near_block, near_tile), *tile_of(far_place, far_tile)
            )
            stash = lax.rem(group, 3)
            left_ref[k] = left
            wide_ref[k, :, :width] = spread
            wide_ref[k, : dots[0].shape[0], width:] = dots[0]
            cross_ref[k, :, :width] = dots[1]
            cross_ref[k, :, width:] = dots[2]
            sums_ref[stash, k, 0] = near_rows
            sums_ref[stash, k, 1] = far_rows
            spots_ref[stash, k, 0] = near_spot
            spots_ref[stash, k, 1] = far_spot
        return carry

    lax.fori_loop(0, (count + GROUP - 1) // GROUP + 2, step, 0)

    at = 0
    if final:
        moments = functools.reduce(jnp.add, [lists[k, 1] for k in range(near_number)])
        old = [list(blocks) for blocks in done]
    for out in refs_out:
        for k in range(out.shape[0]):
            is_near = at < near_number
            total, block = (near_sum, at) if is_near else (far_sum, at - near_number)
            known = None
            if final:
                row = old[0 if is_near else 1]
                if block in row:
                    known = earlier[row.index(block) + (0 if is_near else len(old[0]))]
            for axis, row in enumerate((6, 7, 5)):
                rows = slice(axis * tiles, (axis + 1) * tiles)
                value = total[block, :, row, :]
                out[k, rows, :] = value if known is None else value + known[0, rows, :]
            if final and not is_near:
                out[k, 3 * tiles :, :] = moments
            at += 1


def run_pairs(blocks, tiles, slots, list_group, totals, near, far, counts=None, done=None, earlier=()):
    width = blocks[0].shape[-1]
    final = counts is not None
    near_number, far_number = len(near), len(far)
    slot_count = totals[0] * totals[1] * slots
    hbm = pl.BlockSpec(memory_space=pl.ANY)
    vmem = pl.BlockSpec(memory_space=pltpu.VMEM)
    plan = (tiles, slots, list_group) + tuple(totals) + (near, far, done, final)
    if final:
        shapes = [(count, 3 * tiles, width) for count in counts[0]]
        shapes += [(count, 3 * tiles + 8, width) for count in counts[1]]
    else:
        shapes = [(1, 3 * tiles, width)] * (near_number + far_number)
    depth, dot_depth, sum_rows = 64, 32, 16
    share = len(near) * len(far) / (totals[0] * totals[1])
    elements = int(share * slot_count / 3) * width * width

    def kernel(*refs):
        given = len(blocks)
        known = given + len(earlier)
        made = known + len(shapes)
        pair_kernel(plan, refs[:given], refs[given:known], refs[known:made], refs[made:])

    return pl.pallas_call(
        kernel,
        out_shape=[jax.ShapeDtypeStruct(shape, jnp.float32) for shape in shapes],
        in_specs=[hbm] * len(blocks) + [vmem] * len(earlier),
        out_specs=[vmem] * len(shapes),
        scratch_shapes=[
            pltpu.VMEM((len(blocks),) + blocks[0].shape, jnp.float32),
            pltpu.VMEM((len(blocks), 2, 8, width), jnp.float32),
            pltpu.VMEM((near_number, tiles, 8, width), jnp.float32),
            pltpu.VMEM((far_number, tiles, 8, width), jnp.float32),
            pltpu.VMEM((8, slot_count), jnp.int32),
            pltpu.SMEM((8, slot_count), jnp.int32),
            pltpu.VMEM((GROUP, width, depth), jnp.bfloat16),
            pltpu.VMEM((GROUP, depth, 2 * width), jnp.bfloat16),
            pltpu.VMEM((GROUP, dot_depth, 2 * width), jnp.bfloat16),
            pltpu.VMEM((GROUP, width, 2 * width), jnp.bfloat16),
            pltpu.VMEM((3, GROUP, 2, sum_rows, width), jnp.bfloat16),
            pltpu.VMEM((3, GROUP, 2, 8, width), jnp.float32),
            pltpu.SemaphoreType.DMA((len(blocks),)),
            pltpu.SemaphoreType.DMA((len(blocks),)),
        ],
        compiler_params=pltpu.CompilerParams(vmem_limit_bytes=60 * 1024 * 1024),
        cost_estimate=pl.CostEstimate(flops=1000 * elements, bytes_accessed=1 << 22, transcendentals=elements),
        name="pairs" if final else "early_pairs",
    )(*blocks, *earlier)


def tile_groups(tiles):
    main = jnp.concatenate([tiles[..., 3:9, :], tiles[..., 0:2, :]], axis=-2)
    rows = tiles[..., 2, :]
    short = -rows.shape[-2] % 8
    rows = jnp.pad(rows, [(0, 0)] * (rows.ndim - 2) + [(0, short), (0, 0)])
    rows = rows.reshape(rows.shape[:-2] + (rows.shape[-2] // 8, 8, rows.shape[-1]))
    return jnp.concatenate([main, rows], axis=-3)


NCELL = 64


def far_field(segments, tile_cell, moment_sums, total_segments):
    moments = moment_sums.reshape(NCELL, 3, 3) / jnp.sqrt(jnp.float32(total_segments))
    moments = 0.5 * (moments + jnp.transpose(moments, (0, 2, 1)))
    cells = jnp.arange(NCELL).astype(jnp.float32)
    weights = 8.0 / (8.0 + jnp.abs(cells[:, None] - cells[None, :]))
    stress = jnp.dot(weights, moments.reshape(NCELL, 9), precision=lax.Precision.HIGHEST)
    onehot = (tile_cell[:, None] == jnp.arange(NCELL)[None, :]).astype(jnp.float32)
    tile_stress = jnp.dot(onehot, stress, precision=lax.Precision.HIGHEST).reshape(-1, 3, 3)
    traction = jnp.sum(tile_stress[:, :, :, None] * segments[:, None, 3:6, :], axis=2)
    lines = segments[:, 6:9, :]
    return jnp.stack(
        [
            traction[:, 1] * lines[:, 2] - traction[:, 2] * lines[:, 1],
            traction[:, 2] * lines[:, 0] - traction[:, 0] * lines[:, 2],
            traction[:, 0] * lines[:, 1] - traction[:, 1] * lines[:, 0],
        ],
        axis=1,
    )


def local_moments(segments, tile_cell):
    outer = jnp.sum(segments[:, 3:6, None, :] * segments[:, None, 6:9, :], axis=3).reshape(-1, 9)
    onehot = (jnp.arange(NCELL)[:, None] == tile_cell[None, :]).astype(jnp.float32)
    return jnp.dot(onehot, outer, precision=lax.Precision.HIGHEST)


AXES = ("dom", "sub")


def swap(value, mask):
    devices = lax.axis_size(AXES)
    return lax.ppermute(value, AXES, [(k, k ^ mask) for k in range(devices)])


def span(steps):
    masks = [0]
    for step in steps:
        masks += [mask ^ step for mask in masks]
    return masks


def mask_steps(devices):
    bits = devices.bit_length() - 1
    number = bits // 2
    far_steps = [devices >> (k + 2) for k in range(number)]
    near_steps = [devices >> 1] + [devices >> (k + 1) for k in range(number + 1, bits)]
    return near_steps, far_steps


def spread(block, near_steps, far_steps, work):
    steps = list(near_steps) + list(far_steps)
    allowed = set(span(near_steps)) | set(span(far_steps))
    held = {0: block}
    fresh = {0: -1}
    sums = None
    while fresh:
        arrived = {}
        for mask, last in fresh.items():
            for at in range(last + 1, len(steps)):
                if mask ^ steps[at] in allowed:
                    arrived[mask ^ steps[at]] = (swap(held[mask], steps[at]), at)
        if arrived:
            values = [value for value, at in arrived.values()]
            if len(held) > 1 and sums is None:
                sums = work([held[step] for step in near_steps], [held[step] for step in far_steps])
                values, sums = lax.optimization_barrier((values, sums))
            else:
                values = lax.optimization_barrier(values)
            held.update(zip(arrived, values))
        fresh = {mask: at for mask, (value, at) in arrived.items()}
    return [held[mask] for mask in span(near_steps)], [held[mask] for mask in span(far_steps)], sums


def message_counts(steps):
    counts = [1] * min(len(steps) and 2, 1 << len(steps))
    while sum(counts) < 1 << len(steps):
        counts.append(2 if sum(counts) >= 4 or len(steps) < 3 else 1)
    return counts


def collect(outs, counts, steps):
    groups = list(zip(outs, counts))
    for step in reversed(steps):
        half = sum(count for value, count in groups) // 2
        kept, sent, seen = [], [], 0
        for value, count in groups:
            (kept if seen < half else sent).append((value, count))
            seen += count
        arrived = []
        for value, count in reversed(sent):
            got = swap(value, step)
            arrived = [got[k : k + 1] for k in range(count)] + arrived
        merged, at = [], 0
        for value, count in kept:
            more = arrived[at : at + count]
            merged.append((value + (jnp.concatenate(more) if count > 1 else more[0]), count))
            at += count
        groups = merged
    return groups[0][0][0]


def rows_of(values, width):
    flat = values.reshape(-1).astype(jnp.float32)
    groups = -(-flat.shape[0] // (8 * width))
    return jnp.pad(flat, (0, groups * 8 * width - flat.shape[0])).reshape(groups, 8, width)


def on_device(segments, send_tiles, pair_local, pair_remote, pair_count, tile_cell):
    width = segments.shape[2]
    tiles = segments.shape[0]
    devices = send_tiles.shape[1]
    slots = send_tiles.shape[2]
    pairs = pair_local.shape[1]
    near_steps, far_steps = mask_steps(devices)
    near_masks, far_masks = span(near_steps), span(far_steps)

    live = jnp.arange(pairs) < pair_count[0]
    me = lax.axis_index(AXES).astype(jnp.int32)
    peers = jnp.bitwise_xor(me, jnp.array([near ^ far for near in near_masks for far in far_masks], jnp.int32))
    order = (peers[:, None] * slots + jnp.arange(slots)[None, :]).reshape(-1)
    named = jnp.logical_and(pair_remote[0][:, None] == order[None, :], live[:, None])
    table = jnp.sum(jnp.where(named, pair_local[0][:, None] + 1, 0), axis=0) - 1
    chosen = peers[:, None] == jnp.arange(devices)[None, :]
    sent = jnp.sum(jnp.where(chosen[:, :, None], send_tiles[0][None], 0), axis=1)
    lists = jnp.concatenate([table, sent.reshape(-1)])
    moments = local_moments(segments, tile_cell)
    list_rows, moment_rows = rows_of(lists, width), rows_of(moments, width)
    main = tile_groups(segments)
    block = jnp.concatenate([main, list_rows, moment_rows], axis=0)

    totals = (len(near_masks), len(far_masks))
    early = [[0] + [masks.index(step) for step in steps] for masks, steps in ((near_masks, near_steps), (far_masks, far_steps))]

    def early_pairs(near, far):
        return run_pairs([block] + near + far, tiles, slots, main.shape[0], totals, early[0], early[1])

    near_blocks, far_blocks, sums = spread(block, near_steps, far_steps, early_pairs)
    near_counts, far_counts = message_counts(near_steps), message_counts(far_steps)
    outs = run_pairs(
        near_blocks + far_blocks[1:], tiles, slots, main.shape[0], totals, list(range(totals[0])), list(range(totals[1])),
        (near_counts, far_counts), early, sums,
    )
    near_total = collect(outs[: len(near_counts)], near_counts, near_steps)
    far_total = collect(outs[len(near_counts) :], far_counts, far_steps)
    forces = (near_total + far_total[: 3 * tiles]).reshape(3, tiles, width)
    moment_sums = far_total[3 * tiles :].reshape(-1)[: NCELL * 9].reshape(NCELL, 9)
    total_segments = tiles * width * devices
    return forces.transpose(1, 0, 2) + far_field(segments, tile_cell, moment_sums, total_segments)


def solution(mesh):
    in_specs = (
        P(("dom", "sub"), None, None),
        P(("dom", "sub"), None, None),
        P(("dom", "sub"), None),
        P(("dom", "sub"), None),
        P(("dom", "sub")),
        P(("dom", "sub")),
    )
    out_specs = P(("dom", "sub"), None, None)
    return jax.shard_map(
        on_device, mesh=mesh, in_specs=in_specs, out_specs=out_specs, check_vma=False
    )
```

```python
import functools
import jax
import jax.numpy as jnp
from jax import lax
from jax.sharding import PartitionSpec as P
from jax.experimental import pallas as pl
from jax.experimental.pallas import tpu as pltpu

CORE = 0.25
GROUP = 8


def head(value):
    return value.astype(jnp.bfloat16).astype(jnp.float32)


def thirds(value):
    high = head(value)
    rest = value - high
    middle = head(rest)
    return high, middle, rest - middle


def halves(value):
    high = value.astype(jnp.bfloat16)
    return high, (value - high.astype(jnp.float32)).astype(jnp.bfloat16)


def tall(groups):
    return jnp.concatenate(groups, axis=0).astype(jnp.bfloat16)


def place(sub, rows, others=0.0):
    filled = others
    for at, row in rows.items():
        filled = jnp.where(sub == at, row, filled)
    return filled


def tile_parts(sub, rows):
    parts = [thirds(rows[k]) for k in range(3)]
    square = rows[0] * rows[0] + rows[1] * rows[1] + rows[2] * rows[2]
    ones = jnp.where(sub == 3, 1.0, 0.0)
    high, middle = [place(sub, {k: parts[k][at] for k in range(3)}, 0.0) for at in range(2)]
    sums = tall([high + ones, middle])
    return parts, square, sums, place(sub, {k: rows[k] for k in range(3)}, 0.0)


def products(sub, first, second, burgers):
    major = jnp.where(sub < 3, first[0], jnp.where(sub < 6, first[1], first[2]))
    minor = jnp.where(sub % 3 == 0, second[0], jnp.where(sub % 3 == 1, second[1], second[2]))
    rest = place(sub, {0: first[2] * second[2], 1: burgers[0], 2: burgers[1], 3: burgers[2]}, 0.0)
    return [head(major * minor), head(rest)], [major * minor - head(major * minor), rest - head(rest)]


def operands(near, far):
    sub = lax.broadcasted_iota(jnp.int32, (8, near[0].shape[1]), 0)
    near = [jnp.broadcast_to(row, sub.shape) for row in near]
    far = [jnp.broadcast_to(row, sub.shape) for row in far]
    scale = 1.0 / near[0].shape[1]
    for k in range(3):
        middle = jnp.sum(near[k], axis=1, keepdims=True) * scale
        near[k], far[k] = near[k] - middle, far[k] - middle
    zero = jnp.zeros(sub.shape, jnp.float32)
    parts, square, near_sums, near_spot = tile_parts(sub, near)
    square = thirds(square)
    ends = [{6: square[0], 7: square[1]}, {6: square[2], 7: 1.0}, {6: 1.0, 7: 1.0}]
    left = [
        place(sub, {1: middle, 5: middle, 3: low, **end}, high) for (high, middle, low), end in zip(parts, ends)
    ]
    high, low = products(sub, near[3:6], near[6:9], near[3:6])
    left = tall(left + [zero] + high + low + high)

    parts, square, far_sums, far_spot = tile_parts(sub, far)
    square = thirds(square + CORE)
    ends = [{6: 1.0, 7: 1.0}, {6: 1.0, 7: square[0]}, {6: square[1], 7: square[2]}]
    spread = [
        place(sub, {2: -2.0 * middle, 5: -2.0 * middle, 4: -2.0 * low, **end}, -2.0 * high)
        for (high, middle, low), end in zip(parts, ends)
    ]
    high, low = products(sub, far[6:9], far[3:6], far[3:6])
    return left.T, tall(spread + [zero]), tall(high + high + low), near_sums, near_spot, far_sums, far_spot


def matmul(left, right, contract=(1, 0)):
    dims = (((contract[0],), (contract[1],)), ((), ()))
    return lax.dot_general(left, right, dims, preferred_element_type=jnp.float32)


def live_list(near_rows, far_rows, ids_ref):
    slots = ids_ref.shape[1]

    def line(rows):
        return jnp.concatenate([rows[k : k + 1] for k in range(rows.shape[0])], axis=1)

    near, far = line(near_rows), line(far_rows)
    alive = near >= 0
    row = lax.broadcasted_iota(jnp.int32, (slots, slots), 0)
    lane = lax.broadcasted_iota(jnp.int32, (slots, slots), 1)
    before = jnp.where(row < lane, 1.0, 0.0).astype(jnp.bfloat16)
    flags = jnp.where(alive, 1.0, 0.0)
    rank = matmul(jnp.broadcast_to(flags, (8, slots)).astype(jnp.bfloat16), before)[0:1]
    rank = jnp.where(alive, rank, -1.0)
    chosen = jnp.where(jnp.broadcast_to(rank, (slots, slots)) == row.astype(jnp.float32), 1.0, 0.0).astype(jnp.bfloat16)
    sub = lax.broadcasted_iota(jnp.int32, (8, slots), 0)
    near, far = jnp.maximum(near, 0).astype(jnp.int32), jnp.maximum(far, 0).astype(jnp.int32)
    values = [near >> 6, near & 63, far >> 6, far & 63]
    values = place(sub, {k: value.astype(jnp.float32) for k, value in enumerate(values)}, jnp.zeros((8, slots), jnp.float32))
    packed = matmul(values.astype(jnp.bfloat16), chosen, (1, 1)).astype(jnp.int32)
    number = jnp.sum(flags, axis=1, keepdims=True).astype(jnp.int32)
    ids_ref[0:1, :] = packed[0:1] * 64 + packed[1:2]
    ids_ref[1:2, :] = packed[2:3] * 64 + packed[3:4]
    ids_ref[2:3, :] = jnp.broadcast_to(number, (1, slots))


def pair_kernel(plan, sources, earlier, refs_out, scratch):
    tiles, slots, list_group, near_total, far_total, near, far, done, final = plan
    near_number, far_number = len(near), len(far)
    (blocks, lists, near_sum, far_sum, ids_vmem, ids, left_ref, right_ref, part_ref, sums_ref, spots_ref,
     sems, list_sems) = scratch
    list_copies = [
        pltpu.make_async_copy(source.at[pl.ds(list_group, 2)], lists.at[k], list_sems.at[k])
        for k, source in enumerate(sources)
    ]
    copies = [pltpu.make_async_copy(source, blocks.at[k], sems.at[k]) for k, source in enumerate(sources)]
    for copy in list_copies + copies:
        copy.start()
    near_sum[...] = jnp.zeros_like(near_sum)
    far_sum[...] = jnp.zeros_like(far_sum)
    right_ref[...] = jnp.zeros_like(right_ref)
    for copy in list_copies:
        copy.wait()

    width = blocks.shape[-1]
    shape = (4, width)
    position = lax.broadcasted_iota(jnp.int32, shape, 0) * width + lax.broadcasted_iota(jnp.int32, shape, 1)
    near_ids = jnp.full(shape, -1.0)
    near_at = position // (far_total * slots)
    far_at = position // slots % far_total
    for k, block in enumerate(near):
        given = lists[k, 0, 0:4]
        given = jnp.where(given >= 0, given + k * tiles, given)
        near_ids = jnp.where(near_at == block, given, near_ids)
    far_ids = jnp.full(shape, -1.0)
    for k, block in enumerate(far):
        given = lists[near_number - 1 + k if k else 0, 0, 4:8] + k * tiles
        far_ids = jnp.where(far_at == block, given, far_ids)
    near_ids = jnp.where(far_ids >= 0, near_ids, -1.0)
    if done:
        old_near = functools.reduce(jnp.logical_or, [near_at == block for block in done[0]])
        old_far = functools.reduce(jnp.logical_or, [far_at == block for block in done[1]])
        near_ids = jnp.where(jnp.logical_and(old_near, old_far), -1.0, near_ids)
    live_list(near_ids, far_ids, ids_vmem)
    move = pltpu.make_async_copy(ids_vmem, ids, list_sems.at[0])
    move.start()
    move.wait()
    count = ids[2, 0]
    last = ids.shape[1] - 1
    for copy in copies:
        copy.wait()

    def tile_of(block, tile):
        rows = [blocks[block, tile, pl.ds(k, 1), :] for k in range(8)]
        return rows[6:8] + [blocks[block, tiles + tile // 8, pl.ds(tile % 8, 1), :]] + rows[0:6]

    def pick(group, k):
        at = group * GROUP + k
        held = jnp.clip(at, 0, last)
        near, far = ids[0, held], ids[1, held]
        live = jnp.logical_and(at >= 0, at < count)
        return live, near // tiles, near % tiles, far // tiles, far % tiles

    def step(group, carry):
        for k in range(GROUP):
            live, near_block, near_tile, far_block, far_tile = pick(group - 2, k)
            stash = lax.rem(group + 1, 3)
            near_rows, far_rows = sums_ref[stash, k, 0], sums_ref[stash, k, 1]
            parts = part_ref[k]
            half = parts.shape[1] // 2
            for block, tile, spot, total, out in (
                (near_block, near_tile, 0, matmul(jnp.concatenate([far_rows, far_rows], axis=1), parts, (1, 1)), near_sum),
                (far_block, far_tile, 1, matmul(near_rows, parts), far_sum),
            ):
                total = total[0:8] + total[8:16]
                if total.shape[1] > half:
                    total = total[:, :half] + total[:, half:]
                force = spots_ref[stash, k, spot] * jnp.broadcast_to(total[3:4], total.shape) - total
                out[block, pl.ds(pl.multiple_of(tile * 8, 8), 8), :] += jnp.where(live, force, 0.0)
        for k in range(GROUP):
            terms = matmul(left_ref[k], right_ref[k])
            inverse = lax.rsqrt(terms[:, :width])
            coupling = terms[:, width:] * (inverse * inverse * inverse)
            high, low = halves(coupling)
            part_ref[k, :, :width] = high
            part_ref[k, :, width:] = low
        for k in range(GROUP):
            live, near_block, near_tile, far_block, far_tile = pick(group, k)
            far_place = jnp.where(far_block > 0, far_block + (near_number - 1), 0)
            left, spread, numerator, near_rows, near_spot, far_rows, far_spot = operands(
                tile_of(near_block, near_tile), tile_of(far_place, far_tile)
            )
            stash = lax.rem(group, 3)
            left_ref[k] = left
            right_ref[k, : spread.shape[0], :width] = spread
            right_ref[k, spread.shape[0] :, width:] = numerator
            sums_ref[stash, k, 0] = near_rows
            sums_ref[stash, k, 1] = far_rows
            spots_ref[stash, k, 0] = near_spot
            spots_ref[stash, k, 1] = far_spot
        return carry

    lax.fori_loop(0, (count + GROUP - 1) // GROUP + 2, step, 0)

    at = 0
    if final:
        moments = functools.reduce(jnp.add, [lists[k, 1] for k in range(near_number)])
        old = [list(blocks) for blocks in done]
    for out in refs_out:
        for k in range(out.shape[0]):
            is_near = at < near_number
            total, block = (near_sum, at) if is_near else (far_sum, at - near_number)
            known = None
            if final:
                row = old[0 if is_near else 1]
                if block in row:
                    known = earlier[row.index(block) + (0 if is_near else len(old[0]))]
            for axis in range(3):
                rows = slice(axis * tiles, (axis + 1) * tiles)
                value = total[block, pl.ds(axis, tiles, stride=8), :]
                out[k, rows, :] = value if known is None else value + known[0, rows, :]
            if final and not is_near:
                out[k, 3 * tiles :, :] = moments
            at += 1


def run_pairs(blocks, tiles, slots, list_group, totals, near, far, counts=None, done=None, earlier=()):
    width = blocks[0].shape[-1]
    final = counts is not None
    near_number, far_number = len(near), len(far)
    slot_count = totals[0] * totals[1] * slots
    hbm = pl.BlockSpec(memory_space=pl.ANY)
    vmem = pl.BlockSpec(memory_space=pltpu.VMEM)
    plan = (tiles, slots, list_group) + tuple(totals) + (near, far, done, final)
    if final:
        shapes = [(count, 3 * tiles, width) for count in counts[0]]
        shapes += [(count, 3 * tiles + 8, width) for count in counts[1]]
    else:
        shapes = [(1, 3 * tiles, width)] * (near_number + far_number)
    depth, sum_rows = 80, 16
    share = len(near) * len(far) / (totals[0] * totals[1])
    elements = int(share * slot_count / 3) * width * width

    def kernel(*refs):
        given = len(blocks)
        known = given + len(earlier)
        made = known + len(shapes)
        pair_kernel(plan, refs[:given], refs[given:known], refs[known:made], refs[made:])

    return pl.pallas_call(
        kernel,
        out_shape=[jax.ShapeDtypeStruct(shape, jnp.float32) for shape in shapes],
        in_specs=[hbm] * len(blocks) + [vmem] * len(earlier),
        out_specs=[vmem] * len(shapes),
        scratch_shapes=[
            pltpu.VMEM((len(blocks),) + blocks[0].shape, jnp.float32),
            pltpu.VMEM((len(blocks), 2, 8, width), jnp.float32),
            pltpu.VMEM((near_number, 8 * tiles, width), jnp.float32),
            pltpu.VMEM((far_number, 8 * tiles, width), jnp.float32),
            pltpu.VMEM((8, slot_count), jnp.int32),
            pltpu.SMEM((8, slot_count), jnp.int32),
            pltpu.VMEM((GROUP, width, depth), jnp.bfloat16),
            pltpu.VMEM((GROUP, depth, 2 * width), jnp.bfloat16),
            pltpu.VMEM((GROUP, width, 2 * width), jnp.bfloat16),
            pltpu.VMEM((3, GROUP, 2, sum_rows, width), jnp.bfloat16),
            pltpu.VMEM((3, GROUP, 2, 8, width), jnp.float32),
            pltpu.SemaphoreType.DMA((len(blocks),)),
            pltpu.SemaphoreType.DMA((len(blocks),)),
        ],
        compiler_params=pltpu.CompilerParams(vmem_limit_bytes=60 * 1024 * 1024),
        cost_estimate=pl.CostEstimate(flops=1000 * elements, bytes_accessed=1 << 22, transcendentals=elements),
        name="pairs" if final else "early_pairs",
    )(*blocks, *earlier)


def tile_groups(tiles):
    main = jnp.concatenate([tiles[..., 3:9, :], tiles[..., 0:2, :]], axis=-2)
    rows = tiles[..., 2, :]
    short = -rows.shape[-2] % 8
    rows = jnp.pad(rows, [(0, 0)] * (rows.ndim - 2) + [(0, short), (0, 0)])
    rows = rows.reshape(rows.shape[:-2] + (rows.shape[-2] // 8, 8, rows.shape[-1]))
    return jnp.concatenate([main, rows], axis=-3)


NCELL = 64


def far_field(segments, tile_cell, moment_sums, total_segments):
    moments = moment_sums.reshape(NCELL, 3, 3) / jnp.sqrt(jnp.float32(total_segments))
    moments = 0.5 * (moments + jnp.transpose(moments, (0, 2, 1)))
    cells = jnp.arange(NCELL).astype(jnp.float32)
    weights = 8.0 / (8.0 + jnp.abs(cells[:, None] - cells[None, :]))
    stress = jnp.dot(weights, moments.reshape(NCELL, 9), precision=lax.Precision.HIGHEST)
    onehot = (tile_cell[:, None] == jnp.arange(NCELL)[None, :]).astype(jnp.float32)
    tile_stress = jnp.dot(onehot, stress, precision=lax.Precision.HIGHEST).reshape(-1, 3, 3)
    traction = jnp.sum(tile_stress[:, :, :, None] * segments[:, None, 3:6, :], axis=2)
    lines = segments[:, 6:9, :]
    return jnp.stack(
        [
            traction[:, 1] * lines[:, 2] - traction[:, 2] * lines[:, 1],
            traction[:, 2] * lines[:, 0] - traction[:, 0] * lines[:, 2],
            traction[:, 0] * lines[:, 1] - traction[:, 1] * lines[:, 0],
        ],
        axis=1,
    )


def local_moments(segments, tile_cell):
    outer = jnp.sum(segments[:, 3:6, None, :] * segments[:, None, 6:9, :], axis=3).reshape(-1, 9)
    onehot = (jnp.arange(NCELL)[:, None] == tile_cell[None, :]).astype(jnp.float32)
    return jnp.dot(onehot, outer, precision=lax.Precision.HIGHEST)


AXES = ("dom", "sub")


def swap(value, mask):
    devices = lax.axis_size(AXES)
    return lax.ppermute(value, AXES, [(k, k ^ mask) for k in range(devices)])


def span(steps):
    masks = [0]
    for step in steps:
        masks += [mask ^ step for mask in masks]
    return masks


def mask_steps(devices):
    bits = devices.bit_length() - 1
    number = bits // 2
    far_steps = [devices >> (k + 2) for k in range(number)]
    near_steps = [devices >> 1] + [devices >> (k + 1) for k in range(number + 1, bits)]
    return near_steps, far_steps


def spread(block, near_steps, far_steps, work):
    steps = list(near_steps) + list(far_steps)
    allowed = set(span(near_steps)) | set(span(far_steps))
    held = {0: block}
    fresh = {0: -1}
    sums = None
    while fresh:
        arrived = {}
        for mask, last in fresh.items():
            for at in range(last + 1, len(steps)):
                if mask ^ steps[at] in allowed:
                    arrived[mask ^ steps[at]] = (swap(held[mask], steps[at]), at)
        if arrived:
            values = [value for value, at in arrived.values()]
            if len(held) > 1 and sums is None:
                sums = work([held[step] for step in near_steps], [held[step] for step in far_steps])
                values, sums = lax.optimization_barrier((values, sums))
            else:
                values = lax.optimization_barrier(values)
            held.update(zip(arrived, values))
        fresh = {mask: at for mask, (value, at) in arrived.items()}
    return [held[mask] for mask in span(near_steps)], [held[mask] for mask in span(far_steps)], sums


def message_counts(steps):
    counts = [1] * min(len(steps) and 2, 1 << len(steps))
    while sum(counts) < 1 << len(steps):
        counts.append(2 if sum(counts) >= 4 or len(steps) < 3 else 1)
    return counts


def collect(outs, counts, steps):
    groups = list(zip(outs, counts))
    for step in reversed(steps):
        half = sum(count for value, count in groups) // 2
        kept, sent, seen = [], [], 0
        for value, count in groups:
            (kept if seen < half else sent).append((value, count))
            seen += count
        arrived = []
        for value, count in reversed(sent):
            got = swap(value, step)
            arrived = [got[k : k + 1] for k in range(count)] + arrived
        merged, at = [], 0
        for value, count in kept:
            more = arrived[at : at + count]
            merged.append((value + (jnp.concatenate(more) if count > 1 else more[0]), count))
            at += count
        groups = merged
    return groups[0][0][0]


def rows_of(values, width):
    flat = values.reshape(-1).astype(jnp.float32)
    groups = -(-flat.shape[0] // (8 * width))
    return jnp.pad(flat, (0, groups * 8 * width - flat.shape[0])).reshape(groups, 8, width)


def on_device(segments, send_tiles, pair_local, pair_remote, pair_count, tile_cell):
    width = segments.shape[2]
    tiles = segments.shape[0]
    devices = send_tiles.shape[1]
    slots = send_tiles.shape[2]
    pairs = pair_local.shape[1]
    near_steps, far_steps = mask_steps(devices)
    near_masks, far_masks = span(near_steps), span(far_steps)

    live = jnp.arange(pairs) < pair_count[0]
    me = lax.axis_index(AXES).astype(jnp.int32)
    peers = jnp.bitwise_xor(me, jnp.array([near ^ far for near in near_masks for far in far_masks], jnp.int32))
    order = (peers[:, None] * slots + jnp.arange(slots)[None, :]).reshape(-1)
    named = jnp.logical_and(pair_remote[0][:, None] == order[None, :], live[:, None])
    table = jnp.sum(jnp.where(named, pair_local[0][:, None] + 1, 0), axis=0) - 1
    chosen = peers[:, None] == jnp.arange(devices)[None, :]
    sent = jnp.sum(jnp.where(chosen[:, :, None], send_tiles[0][None], 0), axis=1)
    lists = jnp.concatenate([table, sent.reshape(-1)])
    moments = local_moments(segments, tile_cell)
    list_rows, moment_rows = rows_of(lists, width), rows_of(moments, width)
    main = tile_groups(segments)
    block = jnp.concatenate([main, list_rows, moment_rows], axis=0)

    totals = (len(near_masks), len(far_masks))
    early = [[0] + [masks.index(step) for step in steps] for masks, steps in ((near_masks, near_steps), (far_masks, far_steps))]

    def early_pairs(near, far):
        return run_pairs([block] + near + far, tiles, slots, main.shape[0], totals, early[0], early[1])

    near_blocks, far_blocks, sums = spread(block, near_steps, far_steps, early_pairs)
    near_counts, far_counts = message_counts(near_steps), message_counts(far_steps)
    outs = run_pairs(
        near_blocks + far_blocks[1:], tiles, slots, main.shape[0], totals, list(range(totals[0])), list(range(totals[1])),
        (near_counts, far_counts), early, sums,
    )
    near_total = collect(outs[: len(near_counts)], near_counts, near_steps)
    far_total = collect(outs[len(near_counts) :], far_counts, far_steps)
    forces = (near_total + far_total[: 3 * tiles]).reshape(3, tiles, width)
    moment_sums = far_total[3 * tiles :].reshape(-1)[: NCELL * 9].reshape(NCELL, 9)
    total_segments = tiles * width * devices
    return forces.transpose(1, 0, 2) + far_field(segments, tile_cell, moment_sums, total_segments)


def solution(mesh):
    in_specs = (
        P(("dom", "sub"), None, None),
        P(("dom", "sub"), None, None),
        P(("dom", "sub"), None),
        P(("dom", "sub"), None),
        P(("dom", "sub")),
        P(("dom", "sub")),
    )
    out_specs = P(("dom", "sub"), None, None)
    return jax.shard_map(
        on_device, mesh=mesh, in_specs=in_specs, out_specs=out_specs, check_vma=False
    )
```

```python
import functools
import jax
import jax.numpy as jnp
from jax import lax
from jax.sharding import PartitionSpec as P
from jax.experimental import pallas as pl
from jax.experimental.pallas import tpu as pltpu

CORE = 0.25
GROUP = 8


def head(value):
    return value.astype(jnp.bfloat16).astype(jnp.float32)


def thirds(value):
    high = head(value)
    rest = value - high
    middle = head(rest)
    return high, middle, rest - middle


def halves(value):
    high = value.astype(jnp.bfloat16)
    return high, (value - high.astype(jnp.float32)).astype(jnp.bfloat16)


def tall(groups):
    return jnp.concatenate(groups, axis=0).astype(jnp.bfloat16)


def place(sub, rows, others=0.0):
    filled = others
    for at, row in rows.items():
        filled = jnp.where(sub == at, row, filled)
    return filled


def tile_parts(sub, rows):
    parts = [thirds(rows[k]) for k in range(3)]
    square = rows[0] * rows[0] + rows[1] * rows[1] + rows[2] * rows[2]
    ones = jnp.where(sub == 3, 1.0, 0.0)
    high, middle = [place(sub, {k: parts[k][at] for k in range(3)}, 0.0) for at in range(2)]
    sums = tall([high + ones, middle])
    return parts, square, sums, place(sub, {k: rows[k] for k in range(3)}, 0.0)


def products(sub, first, second, burgers):
    major = jnp.where(sub < 3, first[0], jnp.where(sub < 6, first[1], first[2]))
    minor = jnp.where(sub % 3 == 0, second[0], jnp.where(sub % 3 == 1, second[1], second[2]))
    rest = place(sub, {0: first[2] * second[2], 1: burgers[0], 2: burgers[1], 3: burgers[2]}, 0.0)
    return [head(major * minor), head(rest)], [major * minor - head(major * minor), rest - head(rest)]


def operands(near, far):
    sub = lax.broadcasted_iota(jnp.int32, (8, near[0].shape[1]), 0)
    near = [jnp.broadcast_to(row, sub.shape) for row in near]
    far = [jnp.broadcast_to(row, sub.shape) for row in far]
    scale = 1.0 / near[0].shape[1]
    for k in range(3):
        middle = jnp.sum(near[k], axis=1, keepdims=True) * scale
        near[k], far[k] = near[k] - middle, far[k] - middle
    zero = jnp.zeros(sub.shape, jnp.float32)
    parts, square, near_sums, near_spot = tile_parts(sub, near)
    square = thirds(square)
    ends = [{6: square[0], 7: square[1]}, {6: square[2], 7: 1.0}, {6: 1.0, 7: 1.0}]
    left = [
        place(sub, {1: middle, 5: middle, 3: low, **end}, high) for (high, middle, low), end in zip(parts, ends)
    ]
    high, low = products(sub, near[3:6], near[6:9], near[3:6])
    left = tall(left + [zero] + high + low + high)

    parts, square, far_sums, far_spot = tile_parts(sub, far)
    square = thirds(square + CORE)
    ends = [{6: 1.0, 7: 1.0}, {6: 1.0, 7: square[0]}, {6: square[1], 7: square[2]}]
    spread = [
        place(sub, {2: -2.0 * middle, 5: -2.0 * middle, 4: -2.0 * low, **end}, -2.0 * high)
        for (high, middle, low), end in zip(parts, ends)
    ]
    high, low = products(sub, far[6:9], far[3:6], far[3:6])
    return left.T, tall(spread + [zero]), tall(high + high + low), near_sums, near_spot, far_sums, far_spot


def matmul(left, right, contract=(1, 0)):
    dims = (((contract[0],), (contract[1],)), ((), ()))
    return lax.dot_general(left, right, dims, preferred_element_type=jnp.float32)


def live_list(near_rows, far_rows, ids_ref):
    slots = ids_ref.shape[1]

    def line(rows):
        return jnp.concatenate([rows[k : k + 1] for k in range(rows.shape[0])], axis=1)

    near, far = line(near_rows), line(far_rows)
    alive = near >= 0
    row = lax.broadcasted_iota(jnp.int32, (slots, slots), 0)
    lane = lax.broadcasted_iota(jnp.int32, (slots, slots), 1)
    before = jnp.where(row < lane, 1.0, 0.0).astype(jnp.bfloat16)
    flags = jnp.where(alive, 1.0, 0.0)
    rank = matmul(jnp.broadcast_to(flags, (8, slots)).astype(jnp.bfloat16), before)[0:1]
    rank = jnp.where(alive, rank, -1.0)
    chosen = jnp.where(jnp.broadcast_to(rank, (slots, slots)) == row.astype(jnp.float32), 1.0, 0.0).astype(jnp.bfloat16)
    sub = lax.broadcasted_iota(jnp.int32, (8, slots), 0)
    near, far = jnp.maximum(near, 0).astype(jnp.int32), jnp.maximum(far, 0).astype(jnp.int32)
    values = [near >> 6, near & 63, far >> 6, far & 63]
    values = place(sub, {k: value.astype(jnp.float32) for k, value in enumerate(values)}, jnp.zeros((8, slots), jnp.float32))
    packed = matmul(values.astype(jnp.bfloat16), chosen, (1, 1)).astype(jnp.int32)
    number = jnp.sum(flags, axis=1, keepdims=True).astype(jnp.int32)
    ids_ref[0:1, :] = packed[0:1] * 64 + packed[1:2]
    ids_ref[1:2, :] = packed[2:3] * 64 + packed[3:4]
    ids_ref[2:3, :] = jnp.broadcast_to(number, (1, slots))


def pair_kernel(plan, sources, earlier, refs_out, scratch):
    tiles, slots, list_group, near_total, far_total, near, far, combos, done, final, layout = plan
    near_number, far_number = len(near), len(far)
    (blocks, lists, near_sum, far_sum, ids_vmem, ids, left_ref, right_ref, part_ref, sums_ref, spots_ref,
     sems, list_sems) = scratch
    list_copies, copies = [], []
    for at, (k, offset, size) in enumerate(layout):
        copies.append(pltpu.make_async_copy(sources[at], blocks.at[k, pl.ds(offset, size)], sems.at[at]))
        if offset <= list_group < offset + size:
            rows = sources[at].at[pl.ds(list_group - offset, 2)]
            list_copies.append(pltpu.make_async_copy(rows, lists.at[k], list_sems.at[k]))
    for copy in list_copies + copies:
        copy.start()
    near_sum[...] = jnp.zeros_like(near_sum)
    far_sum[...] = jnp.zeros_like(far_sum)
    right_ref[...] = jnp.zeros_like(right_ref)
    for copy in list_copies:
        copy.wait()

    width = blocks.shape[-1]
    shape = (4, width)
    position = lax.broadcasted_iota(jnp.int32, shape, 0) * width + lax.broadcasted_iota(jnp.int32, shape, 1)
    near_ids = jnp.full(shape, -1.0)
    near_at = position // (far_total * slots)
    far_at = position // slots % far_total
    for k, block in enumerate(near):
        given = lists[k, 0, 0:4]
        given = jnp.where(given >= 0, given + k * tiles, given)
        wanted = [far_at == other for first, other in combos if first == block]
        if wanted:
            wanted = functools.reduce(jnp.logical_or, wanted)
            near_ids = jnp.where(jnp.logical_and(near_at == block, wanted), given, near_ids)
    far_ids = jnp.full(shape, -1.0)
    for k, block in enumerate(far):
        given = lists[near_number - 1 + k if k else 0, 0, 4:8] + k * tiles
        far_ids = jnp.where(far_at == block, given, far_ids)
    live_list(near_ids, far_ids, ids_vmem)
    move = pltpu.make_async_copy(ids_vmem, ids, list_sems.at[0])
    move.start()
    move.wait()
    count = ids[2, 0]
    last = ids.shape[1] - 1
    for copy in copies:
        copy.wait()

    def tile_of(block, tile):
        rows = [blocks[block, tile, pl.ds(k, 1), :] for k in range(8)]
        return rows[6:8] + [blocks[block, tiles + tile // 8, pl.ds(tile % 8, 1), :]] + rows[0:6]

    def pick(group, k):
        at = group * GROUP + k
        held = jnp.clip(at, 0, last)
        near, far = ids[0, held], ids[1, held]
        live = jnp.logical_and(at >= 0, at < count)
        return live, near // tiles, near % tiles, far // tiles, far % tiles

    def step(group, carry):
        for k in range(GROUP):
            live, near_block, near_tile, far_block, far_tile = pick(group - 2, k)
            stash = lax.rem(group + 1, 3)
            near_rows, far_rows = sums_ref[stash, k, 0], sums_ref[stash, k, 1]
            parts = part_ref[k]
            half = parts.shape[1] // 2
            for block, tile, spot, total, out in (
                (near_block, near_tile, 0, matmul(jnp.concatenate([far_rows, far_rows], axis=1), parts, (1, 1)), near_sum),
                (far_block, far_tile, 1, matmul(near_rows, parts), far_sum),
            ):
                total = total[0:8] + total[8:16]
                if total.shape[1] > half:
                    total = total[:, :half] + total[:, half:]
                force = spots_ref[stash, k, spot] * jnp.broadcast_to(total[3:4], total.shape) - total
                out[block, pl.ds(pl.multiple_of(tile * 8, 8), 8), :] += jnp.where(live, force, 0.0)
        for k in range(GROUP):
            terms = matmul(left_ref[k], right_ref[k])
            inverse = lax.rsqrt(terms[:, :width])
            coupling = terms[:, width:] * (inverse * inverse * inverse)
            high, low = halves(coupling)
            part_ref[k, :, :width] = high
            part_ref[k, :, width:] = low
        for k in range(GROUP):
            live, near_block, near_tile, far_block, far_tile = pick(group, k)
            far_place = jnp.where(far_block > 0, far_block + (near_number - 1), 0)
            left, spread, numerator, near_rows, near_spot, far_rows, far_spot = operands(
                tile_of(near_block, near_tile), tile_of(far_place, far_tile)
            )
            stash = lax.rem(group, 3)
            left_ref[k] = left
            right_ref[k, : spread.shape[0], :width] = spread
            right_ref[k, spread.shape[0] :, width:] = numerator
            sums_ref[stash, k, 0] = near_rows
            sums_ref[stash, k, 1] = far_rows
            spots_ref[stash, k, 0] = near_spot
            spots_ref[stash, k, 1] = far_spot
        return carry

    lax.fori_loop(0, (count + GROUP - 1) // GROUP + 2, step, 0)

    at = 0
    if final:
        moments = functools.reduce(jnp.add, [lists[k, 1] for k in range(near_number)])
    for out in refs_out:
        for k in range(out.shape[0]):
            is_near = at < near_number
            total, block = (near_sum, at) if is_near else (far_sum, at - near_number)
            old, name = (done[0], near[block]) if is_near else (done[1], far[block])
            known = earlier[old.index(name) + (0 if is_near else len(done[0]))] if name in old else None
            for axis in range(3):
                rows = slice(axis * tiles, (axis + 1) * tiles)
                value = total[block, pl.ds(axis, tiles, stride=8), :]
                out[k, rows, :] = value if known is None else value + known[0, rows, :]
            if final and not is_near:
                out[k, 3 * tiles :, :] = moments
            at += 1


def run_pairs(held, sizes, near, far, combos, done=((), ()), earlier=(), counts=None):
    tiles, slots, list_group, near_total, far_total = sizes
    given_blocks = [held[0][k] for k in near] + [held[1][k] for k in far if k]
    layout, blocks = [], []
    for k, pieces in enumerate(given_blocks):
        offset = 0
        for piece in pieces:
            layout.append((k, offset, piece.shape[0]))
            blocks.append(piece)
            offset += piece.shape[0]
    groups, width = offset, blocks[0].shape[-1]
    final = counts is not None
    near_number, far_number = len(near), len(far)
    slot_count = near_total * far_total * slots
    hbm = pl.BlockSpec(memory_space=pl.ANY)
    vmem = pl.BlockSpec(memory_space=pltpu.VMEM)
    plan = tuple(sizes) + (near, far, combos, done, final, layout)
    if final:
        shapes = [(count, 3 * tiles, width) for count in counts[0]]
        shapes += [(count, 3 * tiles + 8, width) for count in counts[1]]
    else:
        shapes = [(1, 3 * tiles, width)] * (near_number + far_number)
    depth, sum_rows = 80, 16
    elements = len(combos) * slots // 3 * width * width

    def kernel(*refs):
        given = len(blocks)
        known = given + len(earlier)
        made = known + len(shapes)
        pair_kernel(plan, refs[:given], refs[given:known], refs[known:made], refs[made:])

    return pl.pallas_call(
        kernel,
        out_shape=[jax.ShapeDtypeStruct(shape, jnp.float32) for shape in shapes],
        in_specs=[hbm] * len(blocks) + [vmem] * len(earlier),
        out_specs=[vmem] * len(shapes),
        scratch_shapes=[
            pltpu.VMEM((len(given_blocks), groups, 8, width), jnp.float32),
            pltpu.VMEM((len(given_blocks), 2, 8, width), jnp.float32),
            pltpu.VMEM((near_number, 8 * tiles, width), jnp.float32),
            pltpu.VMEM((far_number, 8 * tiles, width), jnp.float32),
            pltpu.VMEM((8, slot_count), jnp.int32),
            pltpu.SMEM((8, slot_count), jnp.int32),
            pltpu.VMEM((GROUP, width, depth), jnp.bfloat16),
            pltpu.VMEM((GROUP, depth, 2 * width), jnp.bfloat16),
            pltpu.VMEM((GROUP, width, 2 * width), jnp.bfloat16),
            pltpu.VMEM((3, GROUP, 2, sum_rows, width), jnp.bfloat16),
            pltpu.VMEM((3, GROUP, 2, 8, width), jnp.float32),
            pltpu.SemaphoreType.DMA((len(blocks),)),
            pltpu.SemaphoreType.DMA((len(blocks),)),
        ],
        compiler_params=pltpu.CompilerParams(vmem_limit_bytes=60 * 1024 * 1024),
        cost_estimate=pl.CostEstimate(flops=1000 * elements, bytes_accessed=1 << 22, transcendentals=elements),
        name="pairs" if final else "early_pairs",
    )(*blocks, *earlier)


def tile_groups(tiles):
    main = jnp.concatenate([tiles[..., 3:9, :], tiles[..., 0:2, :]], axis=-2)
    rows = tiles[..., 2, :]
    short = -rows.shape[-2] % 8
    rows = jnp.pad(rows, [(0, 0)] * (rows.ndim - 2) + [(0, short), (0, 0)])
    rows = rows.reshape(rows.shape[:-2] + (rows.shape[-2] // 8, 8, rows.shape[-1]))
    return jnp.concatenate([main, rows], axis=-3)


NCELL = 64


def far_field(segments, tile_cell, moment_sums, total_segments):
    moments = moment_sums.reshape(NCELL, 3, 3) / jnp.sqrt(jnp.float32(total_segments))
    moments = 0.5 * (moments + jnp.transpose(moments, (0, 2, 1)))
    cells = jnp.arange(NCELL).astype(jnp.float32)
    weights = 8.0 / (8.0 + jnp.abs(cells[:, None] - cells[None, :]))
    stress = jnp.dot(weights, moments.reshape(NCELL, 9), precision=lax.Precision.HIGHEST)
    onehot = (tile_cell[:, None] == jnp.arange(NCELL)[None, :]).astype(jnp.float32)
    tile_stress = jnp.dot(onehot, stress, precision=lax.Precision.HIGHEST).reshape(-1, 3, 3)
    traction = jnp.sum(tile_stress[:, :, :, None] * segments[:, None, 3:6, :], axis=2)
    lines = segments[:, 6:9, :]
    return jnp.stack(
        [
            traction[:, 1] * lines[:, 2] - traction[:, 2] * lines[:, 1],
            traction[:, 2] * lines[:, 0] - traction[:, 0] * lines[:, 2],
            traction[:, 0] * lines[:, 1] - traction[:, 1] * lines[:, 0],
        ],
        axis=1,
    )


def local_moments(segments, tile_cell):
    outer = jnp.sum(segments[:, 3:6, None, :] * segments[:, None, 6:9, :], axis=3).reshape(-1, 9)
    onehot = (jnp.arange(NCELL)[:, None] == tile_cell[None, :]).astype(jnp.float32)
    return jnp.dot(onehot, outer, precision=lax.Precision.HIGHEST)


AXES = ("dom", "sub")


def swap(value, mask):
    devices = lax.axis_size(AXES)
    return lax.ppermute(value, AXES, [(k, k ^ mask) for k in range(devices)])


def span(steps):
    masks = [0]
    for step in steps:
        masks += [mask ^ step for mask in masks]
    return masks


def mask_steps(devices):
    bits = devices.bit_length() - 1
    number = bits // 2
    far_steps = [devices >> (k + 2) for k in range(number)]
    near_steps = [devices >> 1] + [devices >> (k + 1) for k in range(number + 1, bits)]
    return near_steps, far_steps


def spread(block, pieces, steps, allowed, work):
    held = {0: [block]}

    def onward(items):
        made = []
        for mask, at, last, value in items:
            for step in range(last + 1, len(steps)):
                if mask ^ steps[step] in allowed:
                    made.append((mask ^ steps[step], at, step, swap(value, steps[step])))
        return made

    def settle(items, sums):
        values, sums = lax.optimization_barrier(([item[3] for item in items], sums))
        fresh = [item[:3] + (value,) for item, value in zip(items, values)]
        for mask, at, last, value in fresh:
            held.setdefault(mask, []).insert(at, value)
        return fresh, sums

    first = [(steps[0], at, 0, swap(piece, steps[0])) for at, piece in enumerate(pieces)]
    fresh, sums = settle(first[:1] + onward([(0, 0, 0, block)]), ())
    late = first[1:]
    stage = 0
    while fresh:
        made = onward(fresh) + late
        late = []
        if not made:
            break
        if stage < 2:
            sums = work(stage, held, sums)
        fresh, sums = settle(made, sums)
        stage += 1
    return held, sums


def message_counts(steps):
    counts = [1] * min(len(steps) and 2, 1 << len(steps))
    while sum(counts) < 1 << len(steps):
        counts.append(2 if sum(counts) >= 4 or len(steps) < 3 else 1)
    return counts


def collect(outs, counts, steps):
    groups = list(zip(outs, counts))
    for step in reversed(steps):
        half = sum(count for value, count in groups) // 2
        kept, sent, seen = [], [], 0
        for value, count in groups:
            (kept if seen < half else sent).append((value, count))
            seen += count
        arrived = []
        for value, count in reversed(sent):
            got = swap(value, step)
            arrived = [got[k : k + 1] for k in range(count)] + arrived
        merged, at = [], 0
        for value, count in kept:
            more = arrived[at : at + count]
            merged.append((value + (jnp.concatenate(more) if count > 1 else more[0]), count))
            at += count
        groups = merged
    return groups[0][0][0]


def rows_of(values, width):
    flat = values.reshape(-1).astype(jnp.float32)
    groups = -(-flat.shape[0] // (8 * width))
    return jnp.pad(flat, (0, groups * 8 * width - flat.shape[0])).reshape(groups, 8, width)


def on_device(segments, send_tiles, pair_local, pair_remote, pair_count, tile_cell):
    width = segments.shape[2]
    tiles = segments.shape[0]
    devices = send_tiles.shape[1]
    slots = send_tiles.shape[2]
    pairs = pair_local.shape[1]
    near_steps, far_steps = mask_steps(devices)
    near_masks, far_masks = span(near_steps), span(far_steps[::-1])

    live = jnp.arange(pairs) < pair_count[0]
    me = lax.axis_index(AXES).astype(jnp.int32)
    peers = jnp.bitwise_xor(me, jnp.array([near ^ far for near in near_masks for far in far_masks], jnp.int32))
    order = (peers[:, None] * slots + jnp.arange(slots)[None, :]).reshape(-1)
    named = jnp.logical_and(pair_remote[0][:, None] == order[None, :], live[:, None])
    table = jnp.sum(jnp.where(named, pair_local[0][:, None] + 1, 0), axis=0) - 1
    chosen = peers[:, None] == jnp.arange(devices)[None, :]
    sent = jnp.sum(jnp.where(chosen[:, :, None], send_tiles[0][None], 0), axis=1)
    lists = jnp.concatenate([table, sent.reshape(-1)])
    moments = local_moments(segments, tile_cell)
    list_rows, moment_rows = rows_of(lists, width), rows_of(moments, width)
    main = tile_groups(segments)
    cut = main.shape[0] // 2
    pieces = [main[:cut], jnp.concatenate([main[cut:], list_rows, moment_rows], axis=0)]
    block = jnp.concatenate(pieces, axis=0)

    sizes = (tiles, slots, main.shape[0], len(near_masks), len(far_masks))
    near_all, far_all = list(range(len(near_masks))), list(range(len(far_masks)))
    state = {"near": (), "far": (), "combos": []}

    def chosen_blocks(held):
        return {k: held[mask] for k, mask in enumerate(near_masks) if mask in held}, {
            k: held[mask] for k, mask in enumerate(far_masks) if mask in held
        }

    def work(stage, held, sums):
        split = near_steps[0]
        ready = [
            [k for k in every if masks[k] in held and len(held[masks[k]]) == (2 if masks[k] & split else 1)]
            for every, masks in ((near_all, near_masks), (far_all, far_masks))
        ]
        combos = [(i, j) for i in ready[0] for j in ready[1] if (i, j) not in state["combos"]]
        done = (state["near"], state["far"])
        state.update(near=ready[0], far=ready[1], combos=state["combos"] + combos)
        return run_pairs(chosen_blocks(held), sizes, ready[0], ready[1], combos, done, sums)

    held, sums = spread(block, pieces, near_steps + far_steps, set(near_masks) | set(far_masks), work)
    near_counts, far_counts = message_counts(near_steps), message_counts(far_steps)
    combos = [(i, j) for i in near_all for j in far_all if (i, j) not in state["combos"]]
    outs = run_pairs(
        chosen_blocks(held), sizes, near_all, far_all, combos, (state["near"], state["far"]), sums,
        (near_counts, far_counts),
    )
    near_total = collect(outs[: len(near_counts)], near_counts, near_steps)
    far_total = collect(outs[len(near_counts) :], far_counts, far_steps[::-1])
    forces = (near_total + far_total[: 3 * tiles]).reshape(3, tiles, width)
    moment_sums = far_total[3 * tiles :].reshape(-1)[: NCELL * 9].reshape(NCELL, 9)
    total_segments = tiles * width * devices
    return forces.transpose(1, 0, 2) + far_field(segments, tile_cell, moment_sums, total_segments)


def solution(mesh):
    in_specs = (
        P(("dom", "sub"), None, None),
        P(("dom", "sub"), None, None),
        P(("dom", "sub"), None),
        P(("dom", "sub"), None),
        P(("dom", "sub")),
        P(("dom", "sub")),
    )
    out_specs = P(("dom", "sub"), None, None)
    return jax.shard_map(
        on_device, mesh=mesh, in_specs=in_specs, out_specs=out_specs, check_vma=False
    )
```

```python
import functools
import jax
import jax.numpy as jnp
from jax import lax
from jax.sharding import PartitionSpec as P
from jax.experimental import pallas as pl
from jax.experimental.pallas import tpu as pltpu

CORE = 0.25
GROUP = 8


def head(value):
    return value.astype(jnp.bfloat16).astype(jnp.float32)


def thirds(value):
    high = head(value)
    rest = value - high
    middle = head(rest)
    return high, middle, rest - middle


def halves(value):
    high = value.astype(jnp.bfloat16)
    return high, (value - high.astype(jnp.float32)).astype(jnp.bfloat16)


def tall(groups):
    return jnp.concatenate(groups, axis=0).astype(jnp.bfloat16)


def place(sub, rows, others=0.0):
    filled = others
    for at, row in rows.items():
        filled = jnp.where(sub == at, row, filled)
    return filled


def tile_parts(sub, rows):
    parts = [thirds(rows[k]) for k in range(3)]
    square = rows[0] * rows[0] + rows[1] * rows[1] + rows[2] * rows[2]
    ones = jnp.where(sub == 3, 1.0, 0.0)
    high, middle = [place(sub, {k: parts[k][at] for k in range(3)}, 0.0) for at in range(2)]
    sums = tall([high + ones, middle])
    return parts, square, sums, place(sub, {k: rows[k] for k in range(3)}, 0.0)


def products(sub, first, second, burgers):
    major = jnp.where(sub < 3, first[0], jnp.where(sub < 6, first[1], first[2]))
    minor = jnp.where(sub % 3 == 0, second[0], jnp.where(sub % 3 == 1, second[1], second[2]))
    rest = place(sub, {0: first[2] * second[2], 1: burgers[0], 2: burgers[1], 3: burgers[2]}, 0.0)
    return [head(major * minor), head(rest)], [major * minor - head(major * minor), rest - head(rest)]


def operands(near, far):
    sub = lax.broadcasted_iota(jnp.int32, (8, near[0].shape[1]), 0)
    near = [jnp.broadcast_to(row, sub.shape) for row in near]
    far = [jnp.broadcast_to(row, sub.shape) for row in far]
    scale = 1.0 / near[0].shape[1]
    for k in range(3):
        middle = jnp.sum(near[k], axis=1, keepdims=True) * scale
        near[k], far[k] = near[k] - middle, far[k] - middle
    zero = jnp.zeros(sub.shape, jnp.float32)
    parts, square, near_sums, near_spot = tile_parts(sub, near)
    square = thirds(square)
    ends = [{6: square[0], 7: square[1]}, {6: square[2], 7: 1.0}, {6: 1.0, 7: 1.0}]
    left = [
        place(sub, {1: middle, 5: middle, 3: low, **end}, high) for (high, middle, low), end in zip(parts, ends)
    ]
    high, low = products(sub, near[3:6], near[6:9], near[3:6])
    left = tall(left + [zero] + high + low + high)

    parts, square, far_sums, far_spot = tile_parts(sub, far)
    square = thirds(square + CORE)
    ends = [{6: 1.0, 7: 1.0}, {6: 1.0, 7: square[0]}, {6: square[1], 7: square[2]}]
    spread = [
        place(sub, {2: -2.0 * middle, 5: -2.0 * middle, 4: -2.0 * low, **end}, -2.0 * high)
        for (high, middle, low), end in zip(parts, ends)
    ]
    high, low = products(sub, far[6:9], far[3:6], far[3:6])
    return left.T, tall(spread + [zero]), tall(high + high + low), near_sums, near_spot, far_sums, far_spot


def matmul(left, right, contract=(1, 0)):
    dims = (((contract[0],), (contract[1],)), ((), ()))
    return lax.dot_general(left, right, dims, preferred_element_type=jnp.float32)


def live_list(near_rows, far_rows, ids_ref):
    slots = ids_ref.shape[1]

    def line(rows):
        return jnp.concatenate([rows[k : k + 1] for k in range(rows.shape[0])], axis=1)

    near, far = line(near_rows), line(far_rows)
    alive = near >= 0
    row = lax.broadcasted_iota(jnp.int32, (slots, slots), 0)
    lane = lax.broadcasted_iota(jnp.int32, (slots, slots), 1)
    before = jnp.where(row < lane, 1.0, 0.0).astype(jnp.bfloat16)
    flags = jnp.where(alive, 1.0, 0.0)
    rank = matmul(jnp.broadcast_to(flags, (8, slots)).astype(jnp.bfloat16), before)[0:1]
    rank = jnp.where(alive, rank, -1.0)
    chosen = jnp.where(jnp.broadcast_to(rank, (slots, slots)) == row.astype(jnp.float32), 1.0, 0.0).astype(jnp.bfloat16)
    sub = lax.broadcasted_iota(jnp.int32, (8, slots), 0)
    near, far = jnp.maximum(near, 0).astype(jnp.int32), jnp.maximum(far, 0).astype(jnp.int32)
    values = [near >> 6, near & 63, far >> 6, far & 63]
    values = place(sub, {k: value.astype(jnp.float32) for k, value in enumerate(values)}, jnp.zeros((8, slots), jnp.float32))
    packed = matmul(values.astype(jnp.bfloat16), chosen, (1, 1)).astype(jnp.int32)
    number = jnp.sum(flags, axis=1, keepdims=True).astype(jnp.int32)
    ids_ref[0:1, :] = packed[0:1] * 64 + packed[1:2]
    ids_ref[1:2, :] = packed[2:3] * 64 + packed[3:4]
    ids_ref[2:3, :] = jnp.broadcast_to(number, (1, slots))


def pair_kernel(plan, sources, earlier, refs_out, scratch):
    tiles, slots, list_group, near_total, far_total, near, far, done, final = plan
    near_number, far_number = len(near), len(far)
    (blocks, lists, near_sum, far_sum, ids_vmem, ids, left_ref, right_ref, part_ref, sums_ref, spots_ref, earlier_sums,
     sems, list_sems, sum_sems) = scratch
    list_copies = [
        pltpu.make_async_copy(source.at[pl.ds(list_group, 2)], lists.at[k], list_sems.at[k])
        for k, source in enumerate(sources)
    ]
    copies = [pltpu.make_async_copy(source, blocks.at[k], sems.at[k]) for k, source in enumerate(sources)]
    sum_copies = [pltpu.make_async_copy(given.at[0], earlier_sums.at[k], sum_sems.at[k]) for k, given in enumerate(earlier)]
    for copy in list_copies + copies + sum_copies:
        copy.start()
    near_sum[...] = jnp.zeros_like(near_sum)
    far_sum[...] = jnp.zeros_like(far_sum)
    right_ref[...] = jnp.zeros_like(right_ref)
    for copy in list_copies:
        copy.wait()

    width = blocks.shape[-1]
    shape = (4, width)
    position = lax.broadcasted_iota(jnp.int32, shape, 0) * width + lax.broadcasted_iota(jnp.int32, shape, 1)
    near_ids = jnp.full(shape, -1.0)
    near_at = position // (far_total * slots)
    far_at = position // slots % far_total
    for k, block in enumerate(near):
        given = lists[k, 0, 0:4]
        given = jnp.where(given >= 0, given + k * tiles, given)
        near_ids = jnp.where(near_at == block, given, near_ids)
    far_ids = jnp.full(shape, -1.0)
    for k, block in enumerate(far):
        given = lists[near_number - 1 + k if k else 0, 0, 4:8] + k * tiles
        far_ids = jnp.where(far_at == block, given, far_ids)
    near_ids = jnp.where(far_ids >= 0, near_ids, -1.0)
    if done:
        old_near = functools.reduce(jnp.logical_or, [near_at == block for block in done[0]])
        old_far = functools.reduce(jnp.logical_or, [far_at == block for block in done[1]])
        near_ids = jnp.where(jnp.logical_and(old_near, old_far), -1.0, near_ids)
    live_list(near_ids, far_ids, ids_vmem)
    move = pltpu.make_async_copy(ids_vmem, ids, list_sems.at[0])
    move.start()
    move.wait()
    count = ids[2, 0]
    last = ids.shape[1] - 1
    for copy in copies:
        copy.wait()

    def tile_of(block, tile):
        rows = [blocks[block, tile, pl.ds(k, 1), :] for k in range(8)]
        return rows[6:8] + [blocks[block, tiles + tile // 8, pl.ds(tile % 8, 1), :]] + rows[0:6]

    def pick(group, k):
        at = group * GROUP + k
        held = jnp.clip(at, 0, last)
        near, far = ids[0, held], ids[1, held]
        live = jnp.logical_and(at >= 0, at < count)
        return live, near // tiles, near % tiles, far // tiles, far % tiles

    def add_sums(group):
        for k in range(GROUP):
            live, near_block, near_tile, far_block, far_tile = pick(group, k)
            stash = lax.rem(group, 3)
            near_rows, far_rows = sums_ref[stash, k, 0], sums_ref[stash, k, 1]
            parts = part_ref[k]
            half = parts.shape[1] // 2
            for block, tile, spot, total, out in (
                (near_block, near_tile, 0, matmul(jnp.concatenate([far_rows, far_rows], axis=1), parts, (1, 1)), near_sum),
                (far_block, far_tile, 1, matmul(near_rows, parts), far_sum),
            ):
                total = total[0:8] + total[8:16]
                if total.shape[1] > half:
                    total = total[:, :half] + total[:, half:]
                force = spots_ref[stash, k, spot] * jnp.broadcast_to(total[3:4], total.shape) - total
                out[block, pl.ds(pl.multiple_of(tile * 8, 8), 8), :] += jnp.where(live, force, 0.0)

    def couple():
        for k in range(GROUP):
            terms = matmul(left_ref[k], right_ref[k])
            inverse = lax.rsqrt(terms[:, :width])
            coupling = terms[:, width:] * (inverse * inverse * inverse)
            high, low = halves(coupling)
            part_ref[k, :, :width] = high
            part_ref[k, :, width:] = low

    def build(group):
        for k in range(GROUP):
            live, near_block, near_tile, far_block, far_tile = pick(group, k)
            far_place = jnp.where(far_block > 0, far_block + (near_number - 1), 0)
            left, spread, numerator, near_rows, near_spot, far_rows, far_spot = operands(
                tile_of(near_block, near_tile), tile_of(far_place, far_tile)
            )
            stash = lax.rem(group, 3)
            left_ref[k] = left
            right_ref[k, : spread.shape[0], :width] = spread
            right_ref[k, spread.shape[0] :, width:] = numerator
            sums_ref[stash, k, 0] = near_rows
            sums_ref[stash, k, 1] = far_rows
            spots_ref[stash, k, 0] = near_spot
            spots_ref[stash, k, 1] = far_spot

    def step(group, carry):
        add_sums(group - 2)
        couple()
        build(group)
        return carry

    groups = jnp.maximum((count + GROUP - 1) // GROUP, 2)
    build(jnp.int32(0))
    couple()
    build(jnp.int32(1))
    lax.fori_loop(2, groups, step, 0)
    add_sums(groups - 2)
    couple()
    add_sums(groups - 1)

    for copy in sum_copies:
        copy.wait()
    at = 0
    if final:
        moments = functools.reduce(jnp.add, [lists[k, 1] for k in range(near_number)])
        old = [list(blocks) for blocks in done]
    for out in refs_out:
        for k in range(out.shape[0]):
            is_near = at < near_number
            total, block = (near_sum, at) if is_near else (far_sum, at - near_number)
            known = None
            if final:
                row = old[0 if is_near else 1]
                if block in row:
                    known = earlier_sums.at[row.index(block) + (0 if is_near else len(old[0]))]
            for axis in range(3):
                rows = slice(axis * tiles, (axis + 1) * tiles)
                value = total[block, pl.ds(axis, tiles, stride=8), :]
                out[k, rows, :] = value if known is None else value + known[rows, :]
            if final and not is_near:
                out[k, 3 * tiles :, :] = moments
            at += 1


def run_pairs(blocks, tiles, slots, list_group, totals, near, far, counts=None, done=None, earlier=()):
    width = blocks[0].shape[-1]
    final = counts is not None
    near_number, far_number = len(near), len(far)
    slot_count = totals[0] * totals[1] * slots
    hbm = pl.BlockSpec(memory_space=pl.ANY)
    vmem = pl.BlockSpec(memory_space=pltpu.VMEM)
    plan = (tiles, slots, list_group) + tuple(totals) + (near, far, done, final)
    if final:
        shapes = [(count, 3 * tiles, width) for count in counts[0]]
        shapes += [(count, 3 * tiles + 8, width) for count in counts[1]]
    else:
        shapes = [(1, 3 * tiles, width)] * (near_number + far_number)
    depth, sum_rows = 80, 16
    share = len(near) * len(far) / (totals[0] * totals[1])
    elements = int(share * slot_count / 3) * width * width

    scratch = [
        pltpu.VMEM((len(blocks),) + blocks[0].shape, jnp.float32),
        pltpu.VMEM((len(blocks), 2, 8, width), jnp.float32),
        pltpu.VMEM((near_number, 8 * tiles, width), jnp.float32),
        pltpu.VMEM((far_number, 8 * tiles, width), jnp.float32),
        pltpu.VMEM((8, slot_count), jnp.int32),
        pltpu.SMEM((8, slot_count), jnp.int32),
        pltpu.VMEM((GROUP, width, depth), jnp.bfloat16),
        pltpu.VMEM((GROUP, depth, 2 * width), jnp.bfloat16),
        pltpu.VMEM((GROUP, width, 2 * width), jnp.bfloat16),
        pltpu.VMEM((3, GROUP, 2, sum_rows, width), jnp.bfloat16),
        pltpu.VMEM((3, GROUP, 2, 8, width), jnp.float32),
        pltpu.VMEM((max(len(earlier), 1), 3 * tiles, width), jnp.float32),
        pltpu.SemaphoreType.DMA((len(blocks),)),
        pltpu.SemaphoreType.DMA((len(blocks),)),
        pltpu.SemaphoreType.DMA((max(len(earlier), 1),)),
    ]
    rows = 8 * blocks[0].shape[0] * len(blocks) + (11 * (near_number + far_number) + 3 * len(earlier)) * tiles
    limit = 4 * width * rows + 8 * 1024 * 1024

    def kernel(*refs):
        given = len(blocks)
        known = given + len(earlier)
        made = known + len(shapes)
        pair_kernel(plan, refs[:given], refs[given:known], refs[known:made], refs[made:])

    return pl.pallas_call(
        kernel,
        out_shape=[jax.ShapeDtypeStruct(shape, jnp.float32) for shape in shapes],
        in_specs=[hbm] * (len(blocks) + len(earlier)),
        out_specs=[vmem] * len(shapes),
        scratch_shapes=scratch,
        compiler_params=pltpu.CompilerParams(vmem_limit_bytes=limit),
        cost_estimate=pl.CostEstimate(flops=1000 * elements, bytes_accessed=1 << 22, transcendentals=elements),
        name="pairs" if final else "early_pairs",
    )(*blocks, *earlier)


def tile_groups(tiles):
    main = jnp.concatenate([tiles[..., 3:9, :], tiles[..., 0:2, :]], axis=-2)
    rows = tiles[..., 2, :]
    short = -rows.shape[-2] % 8
    rows = jnp.pad(rows, [(0, 0)] * (rows.ndim - 2) + [(0, short), (0, 0)])
    rows = rows.reshape(rows.shape[:-2] + (rows.shape[-2] // 8, 8, rows.shape[-1]))
    return jnp.concatenate([main, rows], axis=-3)


NCELL = 64


def far_field(segments, tile_cell, moment_sums, total_segments):
    moments = moment_sums.reshape(NCELL, 3, 3) / jnp.sqrt(jnp.float32(total_segments))
    moments = 0.5 * (moments + jnp.transpose(moments, (0, 2, 1)))
    cells = jnp.arange(NCELL).astype(jnp.float32)
    weights = 8.0 / (8.0 + jnp.abs(cells[:, None] - cells[None, :]))
    stress = jnp.dot(weights, moments.reshape(NCELL, 9), precision=lax.Precision.HIGHEST)
    onehot = (tile_cell[:, None] == jnp.arange(NCELL)[None, :]).astype(jnp.float32)
    tile_stress = jnp.dot(onehot, stress, precision=lax.Precision.HIGHEST).reshape(-1, 3, 3)
    traction = jnp.sum(tile_stress[:, :, :, None] * segments[:, None, 3:6, :], axis=2)
    lines = segments[:, 6:9, :]
    return jnp.stack(
        [
            traction[:, 1] * lines[:, 2] - traction[:, 2] * lines[:, 1],
            traction[:, 2] * lines[:, 0] - traction[:, 0] * lines[:, 2],
            traction[:, 0] * lines[:, 1] - traction[:, 1] * lines[:, 0],
        ],
        axis=1,
    )


def local_moments(segments, tile_cell):
    outer = jnp.sum(segments[:, 3:6, None, :] * segments[:, None, 6:9, :], axis=3).reshape(-1, 9)
    onehot = (jnp.arange(NCELL)[:, None] == tile_cell[None, :]).astype(jnp.float32)
    return jnp.dot(onehot, outer, precision=lax.Precision.HIGHEST)


AXES = ("dom", "sub")


def swap(value, mask):
    devices = lax.axis_size(AXES)
    return lax.ppermute(value, AXES, [(k, k ^ mask) for k in range(devices)])


def span(steps):
    masks = [0]
    for step in steps:
        masks += [mask ^ step for mask in masks]
    return masks


def mask_steps(devices):
    bits = devices.bit_length() - 1
    number = bits // 2
    far_steps = [devices >> (k + 2) for k in range(number)]
    near_steps = [devices >> 1] + [devices >> (k + 1) for k in range(number + 1, bits)]
    return near_steps, far_steps


def spread(block, near_steps, far_steps, work):
    steps = list(near_steps) + list(far_steps)
    allowed = set(span(near_steps)) | set(span(far_steps))
    held = {0: block}
    fresh = {0: -1}
    sums = None
    while fresh:
        arrived = {}
        for mask, last in fresh.items():
            for at in range(last + 1, len(steps)):
                if mask ^ steps[at] in allowed:
                    arrived[mask ^ steps[at]] = (swap(held[mask], steps[at]), at)
        if arrived:
            values = [value for value, at in arrived.values()]
            if len(held) > 1 and sums is None:
                sums = work([held[step] for step in near_steps], [held[step] for step in far_steps])
                values, sums = lax.optimization_barrier((values, sums))
            else:
                values = lax.optimization_barrier(values)
            held.update(zip(arrived, values))
        fresh = {mask: at for mask, (value, at) in arrived.items()}
    return [held[mask] for mask in span(near_steps)], [held[mask] for mask in span(far_steps)], sums


def message_counts(steps):
    counts = [1] * min(len(steps) and 2, 1 << len(steps))
    while sum(counts) < 1 << len(steps):
        counts.append(2 if sum(counts) >= 4 or len(steps) < 3 else 1)
    return counts


def collect(outs, counts, steps):
    groups = list(zip(outs, counts))
    for step in reversed(steps):
        half = sum(count for value, count in groups) // 2
        kept, sent, seen = [], [], 0
        for value, count in groups:
            (kept if seen < half else sent).append((value, count))
            seen += count
        arrived = []
        for value, count in reversed(sent):
            got = swap(value, step)
            arrived = [got[k : k + 1] for k in range(count)] + arrived
        merged, at = [], 0
        for value, count in kept:
            more = arrived[at : at + count]
            merged.append((value + (jnp.concatenate(more) if count > 1 else more[0]), count))
            at += count
        groups = merged
    return groups[0][0][0]


def rows_of(values, width):
    flat = values.reshape(-1).astype(jnp.float32)
    groups = -(-flat.shape[0] // (8 * width))
    return jnp.pad(flat, (0, groups * 8 * width - flat.shape[0])).reshape(groups, 8, width)


def on_device(segments, send_tiles, pair_local, pair_remote, pair_count, tile_cell):
    width = segments.shape[2]
    tiles = segments.shape[0]
    devices = send_tiles.shape[1]
    slots = send_tiles.shape[2]
    pairs = pair_local.shape[1]
    near_steps, far_steps = mask_steps(devices)
    near_masks, far_masks = span(near_steps), span(far_steps)

    live = jnp.arange(pairs) < pair_count[0]
    me = lax.axis_index(AXES).astype(jnp.int32)
    peers = jnp.bitwise_xor(me, jnp.array([near ^ far for near in near_masks for far in far_masks], jnp.int32))
    order = (peers[:, None] * slots + jnp.arange(slots)[None, :]).reshape(-1)
    named = jnp.logical_and(pair_remote[0][:, None] == order[None, :], live[:, None])
    table = jnp.sum(jnp.where(named, pair_local[0][:, None] + 1, 0), axis=0) - 1
    chosen = peers[:, None] == jnp.arange(devices)[None, :]
    sent = jnp.sum(jnp.where(chosen[:, :, None], send_tiles[0][None], 0), axis=1)
    lists = jnp.concatenate([table, sent.reshape(-1)])
    moments = local_moments(segments, tile_cell)
    list_rows, moment_rows = rows_of(lists, width), rows_of(moments, width)
    main = tile_groups(segments)
    block = jnp.concatenate([main, list_rows, moment_rows], axis=0)

    totals = (len(near_masks), len(far_masks))
    early = [[0] + [masks.index(step) for step in steps] for masks, steps in ((near_masks, near_steps), (far_masks, far_steps))]

    def early_pairs(near, far):
        return run_pairs([block] + near + far, tiles, slots, main.shape[0], totals, early[0], early[1])

    near_blocks, far_blocks, sums = spread(block, near_steps, far_steps, early_pairs)
    near_counts, far_counts = message_counts(near_steps), message_counts(far_steps)
    outs = run_pairs(
        near_blocks + far_blocks[1:], tiles, slots, main.shape[0], totals, list(range(totals[0])), list(range(totals[1])),
        (near_counts, far_counts), early, sums,
    )
    near_total = collect(outs[: len(near_counts)], near_counts, near_steps)
    far_total = collect(outs[len(near_counts) :], far_counts, far_steps)
    forces = (near_total + far_total[: 3 * tiles]).reshape(3, tiles, width)
    moment_sums = far_total[3 * tiles :].reshape(-1)[: NCELL * 9].reshape(NCELL, 9)
    total_segments = tiles * width * devices
    return forces.transpose(1, 0, 2) + far_field(segments, tile_cell, moment_sums, total_segments)


def solution(mesh):
    in_specs = (
        P(("dom", "sub"), None, None),
        P(("dom", "sub"), None, None),
        P(("dom", "sub"), None),
        P(("dom", "sub"), None),
        P(("dom", "sub")),
        P(("dom", "sub")),
    )
    out_specs = P(("dom", "sub"), None, None)
    return jax.shard_map(
        on_device, mesh=mesh, in_specs=in_specs, out_specs=out_specs, check_vma=False
    )
```

```python
import functools
import jax
import jax.numpy as jnp
from jax import lax
from jax.sharding import PartitionSpec as P
from jax.experimental import pallas as pl
from jax.experimental.pallas import tpu as pltpu

CORE = 0.25
GROUP = 8


def head(value):
    return value.astype(jnp.bfloat16).astype(jnp.float32)


def thirds(value):
    high = head(value)
    rest = value - high
    middle = head(rest)
    return high, middle, rest - middle


def halves(value):
    high = value.astype(jnp.bfloat16)
    return high, (value - high.astype(jnp.float32)).astype(jnp.bfloat16)


def tall(groups):
    return jnp.concatenate(groups, axis=0).astype(jnp.bfloat16)


def place(sub, rows, others=0.0):
    filled = others
    for at, row in rows.items():
        filled = jnp.where(sub == at, row, filled)
    return filled


def tile_parts(sub, rows):
    parts = [thirds(rows[k]) for k in range(3)]
    square = rows[0] * rows[0] + rows[1] * rows[1] + rows[2] * rows[2]
    ones = jnp.where(sub == 3, 1.0, 0.0)
    high, middle = [place(sub, {k: parts[k][at] for k in range(3)}, 0.0) for at in range(2)]
    sums = tall([high + ones, middle])
    return parts, square, sums, place(sub, {k: rows[k] for k in range(3)}, 0.0)


def products(sub, first, second, burgers):
    major = jnp.where(sub < 3, first[0], jnp.where(sub < 6, first[1], first[2]))
    minor = jnp.where(sub % 3 == 0, second[0], jnp.where(sub % 3 == 1, second[1], second[2]))
    rest = place(sub, {0: first[2] * second[2], 1: burgers[0], 2: burgers[1], 3: burgers[2]}, 0.0)
    return [head(major * minor), head(rest)], [major * minor - head(major * minor), rest - head(rest)]


def operands(near, far):
    sub = lax.broadcasted_iota(jnp.int32, (8, near[0].shape[1]), 0)
    near = [jnp.broadcast_to(row, sub.shape) for row in near]
    far = [jnp.broadcast_to(row, sub.shape) for row in far]
    scale = 1.0 / near[0].shape[1]
    for k in range(3):
        middle = jnp.sum(near[k], axis=1, keepdims=True) * scale
        near[k], far[k] = near[k] - middle, far[k] - middle
    zero = jnp.zeros(sub.shape, jnp.float32)
    parts, square, near_sums, near_spot = tile_parts(sub, near)
    square = thirds(square)
    ends = [{6: square[0], 7: square[1]}, {6: square[2], 7: 1.0}, {6: 1.0, 7: 1.0}]
    left = [
        place(sub, {1: middle, 5: middle, 3: low, **end}, high) for (high, middle, low), end in zip(parts, ends)
    ]
    high, low = products(sub, near[3:6], near[6:9], near[3:6])
    left = tall(left + [zero] + high + low + high)

    parts, square, far_sums, far_spot = tile_parts(sub, far)
    square = thirds(square + CORE)
    ends = [{6: 1.0, 7: 1.0}, {6: 1.0, 7: square[0]}, {6: square[1], 7: square[2]}]
    spread = [
        place(sub, {2: -2.0 * middle, 5: -2.0 * middle, 4: -2.0 * low, **end}, -2.0 * high)
        for (high, middle, low), end in zip(parts, ends)
    ]
    high, low = products(sub, far[6:9], far[3:6], far[3:6])
    return left.T, tall(spread + [zero]), tall(high + high + low), near_sums, near_spot, far_sums, far_spot


def matmul(left, right, contract=(1, 0)):
    dims = (((contract[0],), (contract[1],)), ((), ()))
    return lax.dot_general(left, right, dims, preferred_element_type=jnp.float32)


def live_list(near_rows, far_rows, ids_ref):
    slots = ids_ref.shape[1]

    def line(rows):
        return jnp.concatenate([rows[k : k + 1] for k in range(rows.shape[0])], axis=1)

    near, far = line(near_rows), line(far_rows)
    alive = near >= 0
    row = lax.broadcasted_iota(jnp.int32, (slots, slots), 0)
    lane = lax.broadcasted_iota(jnp.int32, (slots, slots), 1)
    before = jnp.where(row < lane, 1.0, 0.0).astype(jnp.bfloat16)
    flags = jnp.where(alive, 1.0, 0.0)
    rank = matmul(jnp.broadcast_to(flags, (8, slots)).astype(jnp.bfloat16), before)[0:1]
    rank = jnp.where(alive, rank, -1.0)
    chosen = jnp.where(jnp.broadcast_to(rank, (slots, slots)) == row.astype(jnp.float32), 1.0, 0.0).astype(jnp.bfloat16)
    sub = lax.broadcasted_iota(jnp.int32, (8, slots), 0)
    near, far = jnp.maximum(near, 0).astype(jnp.int32), jnp.maximum(far, 0).astype(jnp.int32)
    values = [near >> 6, near & 63, far >> 6, far & 63]
    values = place(sub, {k: value.astype(jnp.float32) for k, value in enumerate(values)}, jnp.zeros((8, slots), jnp.float32))
    packed = matmul(values.astype(jnp.bfloat16), chosen, (1, 1)).astype(jnp.int32)
    number = jnp.sum(flags, axis=1, keepdims=True).astype(jnp.int32)
    ids_ref[0:1, :] = packed[0:1] * 64 + packed[1:2]
    ids_ref[1:2, :] = packed[2:3] * 64 + packed[3:4]
    ids_ref[2:3, :] = jnp.broadcast_to(number, (1, slots))


def pair_kernel(plan, sources, earlier, refs_out, scratch):
    tiles, slots, list_group, near_total, far_total, near, far, done, final = plan
    near_number, far_number = len(near), len(far)
    (blocks, lists, near_sum, far_sum, ids_vmem, ids, left_ref, right_ref, part_ref, sums_ref, spots_ref, earlier_sums,
     sems, list_sems, sum_sems) = scratch
    list_copies = [
        pltpu.make_async_copy(source.at[pl.ds(list_group, 2)], lists.at[k], list_sems.at[k])
        for k, source in enumerate(sources)
    ]
    copies = [pltpu.make_async_copy(source, blocks.at[k], sems.at[k]) for k, source in enumerate(sources)]
    sum_copies = [pltpu.make_async_copy(given.at[0], earlier_sums.at[k], sum_sems.at[k]) for k, given in enumerate(earlier)]
    for copy in list_copies + copies + sum_copies:
        copy.start()
    near_sum[...] = jnp.zeros_like(near_sum)
    far_sum[...] = jnp.zeros_like(far_sum)
    right_ref[...] = jnp.zeros_like(right_ref)
    for copy in list_copies:
        copy.wait()

    width = blocks.shape[-1]
    shape = (4, width)
    position = lax.broadcasted_iota(jnp.int32, shape, 0) * width + lax.broadcasted_iota(jnp.int32, shape, 1)
    near_ids = jnp.full(shape, -1.0)
    near_at = position // (far_total * slots)
    far_at = position // slots % far_total
    for k, block in enumerate(near):
        given = lists[k, 0, 0:4]
        given = jnp.where(given >= 0, given + k * tiles, given)
        near_ids = jnp.where(near_at == block, given, near_ids)
    far_ids = jnp.full(shape, -1.0)
    for k, block in enumerate(far):
        given = lists[near_number - 1 + k if k else 0, 0, 4:8] + k * tiles
        far_ids = jnp.where(far_at == block, given, far_ids)
    near_ids = jnp.where(far_ids >= 0, near_ids, -1.0)
    if done:
        old_near = functools.reduce(jnp.logical_or, [near_at == block for block in done[0]])
        old_far = functools.reduce(jnp.logical_or, [far_at == block for block in done[1]])
        near_ids = jnp.where(jnp.logical_and(old_near, old_far), -1.0, near_ids)
    live_list(near_ids, far_ids, ids_vmem)
    move = pltpu.make_async_copy(ids_vmem, ids, list_sems.at[0])
    move.start()
    move.wait()
    count = ids[2, 0]
    last = ids.shape[1] - 1
    for copy in copies:
        copy.wait()

    def tile_of(block, tile):
        rows = [blocks[block, tile, pl.ds(k, 1), :] for k in range(8)]
        return rows[6:8] + [blocks[block, tiles + tile // 8, pl.ds(tile % 8, 1), :]] + rows[0:6]

    def pick(group, k):
        at = group * GROUP + k
        held = jnp.clip(at, 0, last)
        near, far = ids[0, held], ids[1, held]
        live = jnp.logical_and(at >= 0, at < count)
        return live, near // tiles, near % tiles, far // tiles, far % tiles

    def add_sums(group):
        for k in range(GROUP):
            live, near_block, near_tile, far_block, far_tile = pick(group, k)
            stash = lax.rem(group, 3)
            near_rows, far_rows = sums_ref[stash, k, 0], sums_ref[stash, k, 1]
            parts = part_ref[k]
            half = parts.shape[1] // 2
            for block, tile, spot, total, out in (
                (near_block, near_tile, 0, matmul(jnp.concatenate([far_rows, far_rows], axis=1), parts, (1, 1)), near_sum),
                (far_block, far_tile, 1, matmul(near_rows, parts), far_sum),
            ):
                total = total[0:8] + total[8:16]
                if total.shape[1] > half:
                    total = total[:, :half] + total[:, half:]
                force = spots_ref[stash, k, spot] * jnp.broadcast_to(total[3:4], total.shape) - total
                out[block, pl.ds(pl.multiple_of(tile * 8, 8), 8), :] += jnp.where(live, force, 0.0)

    def couple():
        for k in range(GROUP):
            terms = matmul(left_ref[k], right_ref[k])
            inverse = lax.rsqrt(terms[:, :width])
            coupling = terms[:, width:] * (inverse * inverse * inverse)
            high, low = halves(coupling)
            part_ref[k, :, :width] = high
            part_ref[k, :, width:] = low

    def build(group):
        for k in range(GROUP):
            live, near_block, near_tile, far_block, far_tile = pick(group, k)
            far_place = jnp.where(far_block > 0, far_block + (near_number - 1), 0)
            left, spread, numerator, near_rows, near_spot, far_rows, far_spot = operands(
                tile_of(near_block, near_tile), tile_of(far_place, far_tile)
            )
            stash = lax.rem(group, 3)
            left_ref[k] = left
            right_ref[k, : spread.shape[0], :width] = spread
            right_ref[k, spread.shape[0] :, width:] = numerator
            sums_ref[stash, k, 0] = near_rows
            sums_ref[stash, k, 1] = far_rows
            spots_ref[stash, k, 0] = near_spot
            spots_ref[stash, k, 1] = far_spot

    def step(group, carry):
        add_sums(group - 2)
        couple()
        build(group)
        return carry

    groups = jnp.maximum((count + GROUP - 1) // GROUP, 2)
    build(jnp.int32(0))
    couple()
    build(jnp.int32(1))
    lax.fori_loop(2, groups, step, 0)
    add_sums(groups - 2)
    couple()
    add_sums(groups - 1)

    for copy in sum_copies:
        copy.wait()
    at = 0
    if final:
        moments = functools.reduce(jnp.add, [lists[k, 1] for k in range(near_number)])
        old = [list(blocks) for blocks in done]
    for out in refs_out:
        for k in range(out.shape[0]):
            is_near = at < near_number
            total, block = (near_sum, at) if is_near else (far_sum, at - near_number)
            known = None
            if final:
                row = old[0 if is_near else 1]
                if block in row:
                    known = earlier_sums.at[row.index(block) + (0 if is_near else len(old[0]))]
            for axis in range(3):
                rows = slice(axis * tiles, (axis + 1) * tiles)
                value = total[block, pl.ds(axis, tiles, stride=8), :]
                out[k, rows, :] = value if known is None else value + known[rows, :]
            if final and not is_near:
                out[k, 3 * tiles :, :] = moments
            at += 1


def run_pairs(blocks, tiles, slots, list_group, totals, near, far, counts=None, done=None, earlier=()):
    width = blocks[0].shape[-1]
    final = counts is not None
    near_number, far_number = len(near), len(far)
    slot_count = totals[0] * totals[1] * slots
    hbm = pl.BlockSpec(memory_space=pl.ANY)
    vmem = pl.BlockSpec(memory_space=pltpu.VMEM)
    plan = (tiles, slots, list_group) + tuple(totals) + (near, far, done, final)
    if final:
        shapes = [(count, 3 * tiles, width) for count in counts[0]]
        shapes += [(count, 3 * tiles + 8, width) for count in counts[1]]
    else:
        shapes = [(1, 3 * tiles, width)] * (near_number + far_number)
    depth, sum_rows = 80, 16
    share = len(near) * len(far) / (totals[0] * totals[1])
    elements = int(share * slot_count / 3) * width * width

    scratch = [
        pltpu.VMEM((len(blocks),) + blocks[0].shape, jnp.float32),
        pltpu.VMEM((len(blocks), 2, 8, width), jnp.float32),
        pltpu.VMEM((near_number, 8 * tiles, width), jnp.float32),
        pltpu.VMEM((far_number, 8 * tiles, width), jnp.float32),
        pltpu.VMEM((8, slot_count), jnp.int32),
        pltpu.SMEM((8, slot_count), jnp.int32),
        pltpu.VMEM((GROUP, width, depth), jnp.bfloat16),
        pltpu.VMEM((GROUP, depth, 2 * width), jnp.bfloat16),
        pltpu.VMEM((GROUP, width, 2 * width), jnp.bfloat16),
        pltpu.VMEM((3, GROUP, 2, sum_rows, width), jnp.bfloat16),
        pltpu.VMEM((3, GROUP, 2, 8, width), jnp.float32),
        pltpu.VMEM((max(len(earlier), 1), 3 * tiles, width), jnp.float32),
        pltpu.SemaphoreType.DMA((len(blocks),)),
        pltpu.SemaphoreType.DMA((len(blocks),)),
        pltpu.SemaphoreType.DMA((max(len(earlier), 1),)),
    ]
    rows = 8 * blocks[0].shape[0] * len(blocks) + (11 * (near_number + far_number) + 3 * len(earlier)) * tiles
    limit = 4 * width * rows + 8 * 1024 * 1024

    def kernel(*refs):
        given = len(blocks)
        known = given + len(earlier)
        made = known + len(shapes)
        pair_kernel(plan, refs[:given], refs[given:known], refs[known:made], refs[made:])

    return pl.pallas_call(
        kernel,
        out_shape=[jax.ShapeDtypeStruct(shape, jnp.float32) for shape in shapes],
        in_specs=[hbm] * (len(blocks) + len(earlier)),
        out_specs=[vmem] * len(shapes),
        scratch_shapes=scratch,
        compiler_params=pltpu.CompilerParams(vmem_limit_bytes=limit),
        cost_estimate=pl.CostEstimate(flops=(1000 if final else 1) * elements, bytes_accessed=1 << 16, transcendentals=0),
        name="pairs" if final else "early_pairs",
    )(*blocks, *earlier)


def tile_groups(tiles):
    main = jnp.concatenate([tiles[..., 3:9, :], tiles[..., 0:2, :]], axis=-2)
    rows = tiles[..., 2, :]
    short = -rows.shape[-2] % 8
    rows = jnp.pad(rows, [(0, 0)] * (rows.ndim - 2) + [(0, short), (0, 0)])
    rows = rows.reshape(rows.shape[:-2] + (rows.shape[-2] // 8, 8, rows.shape[-1]))
    return jnp.concatenate([main, rows], axis=-3)


NCELL = 64


def far_field(segments, tile_cell, moment_sums, total_segments):
    moments = moment_sums.reshape(NCELL, 3, 3) / jnp.sqrt(jnp.float32(total_segments))
    moments = 0.5 * (moments + jnp.transpose(moments, (0, 2, 1)))
    cells = jnp.arange(NCELL).astype(jnp.float32)
    weights = 8.0 / (8.0 + jnp.abs(cells[:, None] - cells[None, :]))
    stress = jnp.dot(weights, moments.reshape(NCELL, 9), precision=lax.Precision.HIGHEST)
    onehot = (tile_cell[:, None] == jnp.arange(NCELL)[None, :]).astype(jnp.float32)
    tile_stress = jnp.dot(onehot, stress, precision=lax.Precision.HIGHEST).reshape(-1, 3, 3)
    traction = jnp.sum(tile_stress[:, :, :, None] * segments[:, None, 3:6, :], axis=2)
    lines = segments[:, 6:9, :]
    return jnp.stack(
        [
            traction[:, 1] * lines[:, 2] - traction[:, 2] * lines[:, 1],
            traction[:, 2] * lines[:, 0] - traction[:, 0] * lines[:, 2],
            traction[:, 0] * lines[:, 1] - traction[:, 1] * lines[:, 0],
        ],
        axis=1,
    )


def local_moments(segments, tile_cell):
    outer = jnp.sum(segments[:, 3:6, None, :] * segments[:, None, 6:9, :], axis=3).reshape(-1, 9)
    onehot = (jnp.arange(NCELL)[:, None] == tile_cell[None, :]).astype(jnp.float32)
    return jnp.dot(onehot, outer, precision=lax.Precision.HIGHEST)


AXES = ("dom", "sub")


def swap(value, mask):
    devices = lax.axis_size(AXES)
    return lax.ppermute(value, AXES, [(k, k ^ mask) for k in range(devices)])


def span(steps):
    masks = [0]
    for step in steps:
        masks += [mask ^ step for mask in masks]
    return masks


def mask_steps(devices):
    bits = devices.bit_length() - 1
    number = bits // 2
    far_steps = [devices >> (k + 2) for k in range(number)]
    near_steps = [devices >> 1] + [devices >> (k + 1) for k in range(number + 1, bits)]
    return near_steps, far_steps


def spread(block, near_steps, far_steps, work):
    steps = list(near_steps) + list(far_steps)
    allowed = set(span(near_steps)) | set(span(far_steps))
    held = {0: block}
    fresh = {0: -1}
    sums = None
    while fresh:
        arrived = {}
        for mask, last in fresh.items():
            for at in range(last + 1, len(steps)):
                if mask ^ steps[at] in allowed:
                    arrived[mask ^ steps[at]] = (swap(held[mask], steps[at]), at)
        if arrived:
            quick, slow = [], list(arrived)
            if len(held) > 1 and sums is None:
                quick = [mask for mask in arrived if arrived[mask][1] == len(near_steps) - 1]
                slow = [mask for mask in arrived if mask not in quick]
                held.update(zip(quick, lax.optimization_barrier([arrived[mask][0] for mask in quick])))
                sums = work(held)
            values, sums = lax.optimization_barrier(([arrived[mask][0] for mask in slow], sums))
            held.update(zip(slow, values))
        fresh = {mask: at for mask, (value, at) in arrived.items()}
    return [held[mask] for mask in span(near_steps)], [held[mask] for mask in span(far_steps)], sums


def message_counts(steps):
    counts = [1] * min(len(steps) and 2, 1 << len(steps))
    while sum(counts) < 1 << len(steps):
        counts.append(2 if sum(counts) >= 4 or len(steps) < 3 else 1)
    return counts


def collect(outs, counts, steps):
    groups = list(zip(outs, counts))
    for step in reversed(steps):
        half = sum(count for value, count in groups) // 2
        kept, sent, seen = [], [], 0
        for value, count in groups:
            (kept if seen < half else sent).append((value, count))
            seen += count
        arrived = []
        for value, count in reversed(sent):
            got = swap(value, step)
            arrived = [got[k : k + 1] for k in range(count)] + arrived
        merged, at = [], 0
        for value, count in kept:
            more = arrived[at : at + count]
            merged.append((value + (jnp.concatenate(more) if count > 1 else more[0]), count))
            at += count
        groups = merged
    return groups[0][0][0]


def rows_of(values, width):
    flat = values.reshape(-1).astype(jnp.float32)
    groups = -(-flat.shape[0] // (8 * width))
    return jnp.pad(flat, (0, groups * 8 * width - flat.shape[0])).reshape(groups, 8, width)


def on_device(segments, send_tiles, pair_local, pair_remote, pair_count, tile_cell):
    width = segments.shape[2]
    tiles = segments.shape[0]
    devices = send_tiles.shape[1]
    slots = send_tiles.shape[2]
    pairs = pair_local.shape[1]
    near_steps, far_steps = mask_steps(devices)
    near_masks, far_masks = span(near_steps), span(far_steps)

    live = jnp.arange(pairs) < pair_count[0]
    me = lax.axis_index(AXES).astype(jnp.int32)
    peers = jnp.bitwise_xor(me, jnp.array([near ^ far for near in near_masks for far in far_masks], jnp.int32))
    order = (peers[:, None] * slots + jnp.arange(slots)[None, :]).reshape(-1)
    named = jnp.logical_and(pair_remote[0][:, None] == order[None, :], live[:, None])
    table = jnp.sum(jnp.where(named, pair_local[0][:, None] + 1, 0), axis=0) - 1
    chosen = peers[:, None] == jnp.arange(devices)[None, :]
    sent = jnp.sum(jnp.where(chosen[:, :, None], send_tiles[0][None], 0), axis=1)
    lists = jnp.concatenate([table, sent.reshape(-1)])
    moments = local_moments(segments, tile_cell)
    list_rows, moment_rows = rows_of(lists, width), rows_of(moments, width)
    main = tile_groups(segments)
    block = jnp.concatenate([main, list_rows, moment_rows], axis=0)

    totals = (len(near_masks), len(far_masks))
    early = []

    def early_pairs(held):
        early.extend([k for k, mask in enumerate(masks) if mask in held] for masks in (near_masks, far_masks))
        blocks = [held[near_masks[k]] for k in early[0]] + [held[far_masks[k]] for k in early[1][1:]]
        return run_pairs(blocks, tiles, slots, main.shape[0], totals, early[0], early[1])

    near_blocks, far_blocks, sums = spread(block, near_steps, far_steps, early_pairs)
    near_counts, far_counts = message_counts(near_steps), message_counts(far_steps)
    outs = run_pairs(
        near_blocks + far_blocks[1:], tiles, slots, main.shape[0], totals, list(range(totals[0])), list(range(totals[1])),
        (near_counts, far_counts), early, sums,
    )
    near_total = collect(outs[: len(near_counts)], near_counts, near_steps)
    far_total = collect(outs[len(near_counts) :], far_counts, far_steps)
    forces = (near_total + far_total[: 3 * tiles]).reshape(3, tiles, width)
    moment_sums = far_total[3 * tiles :].reshape(-1)[: NCELL * 9].reshape(NCELL, 9)
    total_segments = tiles * width * devices
    return forces.transpose(1, 0, 2) + far_field(segments, tile_cell, moment_sums, total_segments)


def solution(mesh):
    in_specs = (
        P(("dom", "sub"), None, None),
        P(("dom", "sub"), None, None),
        P(("dom", "sub"), None),
        P(("dom", "sub"), None),
        P(("dom", "sub")),
        P(("dom", "sub")),
    )
    out_specs = P(("dom", "sub"), None, None)
    return jax.shard_map(
        on_device, mesh=mesh, in_specs=in_specs, out_specs=out_specs, check_vma=False
    )
```

```python
import functools
import jax
import jax.numpy as jnp
from jax import lax
from jax.sharding import PartitionSpec as P
from jax.experimental import pallas as pl
from jax.experimental.pallas import tpu as pltpu

CORE = 0.25
GROUP = 8


def head(value):
    return value.astype(jnp.bfloat16).astype(jnp.float32)


def thirds(value):
    high = head(value)
    rest = value - high
    middle = head(rest)
    return high, middle, rest - middle


def halves(value):
    high = value.astype(jnp.bfloat16)
    return high, (value - high.astype(jnp.float32)).astype(jnp.bfloat16)


def tall(groups):
    return jnp.concatenate(groups, axis=0).astype(jnp.bfloat16)


def place(sub, rows, others=0.0):
    filled = others
    for at, row in rows.items():
        filled = jnp.where(sub == at, row, filled)
    return filled


def tile_parts(sub, rows):
    parts = [thirds(rows[k]) for k in range(3)]
    square = rows[0] * rows[0] + rows[1] * rows[1] + rows[2] * rows[2]
    ones = jnp.where(sub == 3, 1.0, 0.0)
    high, middle = [place(sub, {k: parts[k][at] for k in range(3)}, 0.0) for at in range(2)]
    sums = tall([high + ones, middle])
    return parts, square, sums, place(sub, {k: rows[k] for k in range(3)}, 0.0)


def products(sub, first, second, burgers):
    major = jnp.where(sub < 3, first[0], jnp.where(sub < 6, first[1], first[2]))
    minor = jnp.where(sub % 3 == 0, second[0], jnp.where(sub % 3 == 1, second[1], second[2]))
    rest = place(sub, {0: first[2] * second[2], 1: burgers[0], 2: burgers[1], 3: burgers[2]}, 0.0)
    return [head(major * minor), head(rest)], [major * minor - head(major * minor), rest - head(rest)]


def operands(near, far):
    sub = lax.broadcasted_iota(jnp.int32, (8, near[0].shape[1]), 0)
    near = [jnp.broadcast_to(row, sub.shape) for row in near]
    far = [jnp.broadcast_to(row, sub.shape) for row in far]
    scale = 1.0 / near[0].shape[1]
    for k in range(3):
        middle = jnp.sum(near[k], axis=1, keepdims=True) * scale
        near[k], far[k] = near[k] - middle, far[k] - middle
    zero = jnp.zeros(sub.shape, jnp.float32)
    parts, square, near_sums, near_spot = tile_parts(sub, near)
    square = thirds(square)
    ends = [{6: square[0], 7: square[1]}, {6: square[2], 7: 1.0}, {6: 1.0, 7: 1.0}]
    left = [
        place(sub, {1: middle, 5: middle, 3: low, **end}, high) for (high, middle, low), end in zip(parts, ends)
    ]
    high, low = products(sub, near[3:6], near[6:9], near[3:6])
    left = tall(left + [zero] + high + low + high)

    parts, square, far_sums, far_spot = tile_parts(sub, far)
    square = thirds(square + CORE)
    ends = [{6: 1.0, 7: 1.0}, {6: 1.0, 7: square[0]}, {6: square[1], 7: square[2]}]
    spread = [
        place(sub, {2: -2.0 * middle, 5: -2.0 * middle, 4: -2.0 * low, **end}, -2.0 * high)
        for (high, middle, low), end in zip(parts, ends)
    ]
    high, low = products(sub, far[6:9], far[3:6], far[3:6])
    return left.T, tall(spread + [zero]), tall(high + high + low), near_sums, near_spot, far_sums, far_spot


def matmul(left, right, contract=(1, 0)):
    dims = (((contract[0],), (contract[1],)), ((), ()))
    return lax.dot_general(left, right, dims, preferred_element_type=jnp.float32)


def live_list(near_rows, far_rows, ids_ref):
    slots = ids_ref.shape[1]

    def line(rows):
        return jnp.concatenate([rows[k : k + 1] for k in range(rows.shape[0])], axis=1)

    near, far = line(near_rows), line(far_rows)
    alive = near >= 0
    row = lax.broadcasted_iota(jnp.int32, (slots, slots), 0)
    lane = lax.broadcasted_iota(jnp.int32, (slots, slots), 1)
    before = jnp.where(row < lane, 1.0, 0.0).astype(jnp.bfloat16)
    flags = jnp.where(alive, 1.0, 0.0)
    rank = matmul(jnp.broadcast_to(flags, (8, slots)).astype(jnp.bfloat16), before)[0:1]
    rank = jnp.where(alive, rank, -1.0)
    chosen = jnp.where(jnp.broadcast_to(rank, (slots, slots)) == row.astype(jnp.float32), 1.0, 0.0).astype(jnp.bfloat16)
    sub = lax.broadcasted_iota(jnp.int32, (8, slots), 0)
    near, far = jnp.maximum(near, 0).astype(jnp.int32), jnp.maximum(far, 0).astype(jnp.int32)
    values = [near >> 6, near & 63, far >> 6, far & 63]
    values = place(sub, {k: value.astype(jnp.float32) for k, value in enumerate(values)}, jnp.zeros((8, slots), jnp.float32))
    packed = matmul(values.astype(jnp.bfloat16), chosen, (1, 1)).astype(jnp.int32)
    number = jnp.sum(flags, axis=1, keepdims=True).astype(jnp.int32)
    ids_ref[0:1, :] = packed[0:1] * 64 + packed[1:2]
    ids_ref[1:2, :] = packed[2:3] * 64 + packed[3:4]
    ids_ref[2:3, :] = jnp.broadcast_to(number, (1, slots))


def pair_kernel(plan, sources, earlier, refs_out, scratch):
    tiles, slots, list_group, near_total, far_total, near, far, done, final = plan
    near_number, far_number = len(near), len(far)
    (blocks, lists, near_sum, far_sum, ids_vmem, ids, left_ref, right_ref, part_ref, sums_ref, spots_ref, earlier_sums,
     sems, list_sems, sum_sems) = scratch
    list_copies = [
        pltpu.make_async_copy(source.at[pl.ds(list_group, 2)], lists.at[k], list_sems.at[k])
        for k, source in enumerate(sources)
    ]
    copies = [pltpu.make_async_copy(source, blocks.at[k], sems.at[k]) for k, source in enumerate(sources)]
    sum_copies = [pltpu.make_async_copy(given.at[0], earlier_sums.at[k], sum_sems.at[k]) for k, given in enumerate(earlier)]
    for copy in list_copies + copies + sum_copies:
        copy.start()
    near_sum[...] = jnp.zeros_like(near_sum)
    far_sum[...] = jnp.zeros_like(far_sum)
    right_ref[...] = jnp.zeros_like(right_ref)
    for copy in list_copies:
        copy.wait()

    width = blocks.shape[-1]
    shape = (4, width)
    position = lax.broadcasted_iota(jnp.int32, shape, 0) * width + lax.broadcasted_iota(jnp.int32, shape, 1)
    near_ids = jnp.full(shape, -1.0)
    near_at = position // (far_total * slots)
    far_at = position // slots % far_total
    for k, block in enumerate(near):
        given = lists[k, 0, 0:4]
        given = jnp.where(given >= 0, given + k * tiles, given)
        near_ids = jnp.where(near_at == block, given, near_ids)
    far_ids = jnp.full(shape, -1.0)
    for k, block in enumerate(far):
        given = lists[near_number - 1 + k if k else 0, 0, 4:8] + k * tiles
        far_ids = jnp.where(far_at == block, given, far_ids)
    near_ids = jnp.where(far_ids >= 0, near_ids, -1.0)
    if done:
        old_near = functools.reduce(jnp.logical_or, [near_at == block for block in done[0]])
        old_far = functools.reduce(jnp.logical_or, [far_at == block for block in done[1]])
        near_ids = jnp.where(jnp.logical_and(old_near, old_far), -1.0, near_ids)
    live_list(near_ids, far_ids, ids_vmem)
    move = pltpu.make_async_copy(ids_vmem, ids, list_sems.at[0])
    move.start()
    move.wait()
    count = ids[2, 0]
    last = ids.shape[1] - 1
    for copy in copies:
        copy.wait()

    def tile_of(block, tile):
        rows = [blocks[block, tile, pl.ds(k, 1), :] for k in range(8)]
        return rows[6:8] + [blocks[block, tiles + tile // 8, pl.ds(tile % 8, 1), :]] + rows[0:6]

    def pick(group, k):
        at = group * GROUP + k
        held = jnp.clip(at, 0, last)
        near, far = ids[0, held], ids[1, held]
        live = jnp.logical_and(at >= 0, at < count)
        return live, near // tiles, near % tiles, far // tiles, far % tiles

    def add_sums(group):
        for k in range(GROUP):
            live, near_block, near_tile, far_block, far_tile = pick(group, k)
            stash = lax.rem(group, 3)
            near_rows, far_rows = sums_ref[stash, k, 0], sums_ref[stash, k, 1]
            parts = part_ref[k]
            half = parts.shape[1] // 2
            for block, tile, spot, total, out in (
                (near_block, near_tile, 0, matmul(jnp.concatenate([far_rows, far_rows], axis=1), parts, (1, 1)), near_sum),
                (far_block, far_tile, 1, matmul(near_rows, parts), far_sum),
            ):
                total = total[0:8] + total[8:16]
                if total.shape[1] > half:
                    total = total[:, :half] + total[:, half:]
                force = spots_ref[stash, k, spot] * jnp.broadcast_to(total[3:4], total.shape) - total
                out[block, pl.ds(pl.multiple_of(tile * 8, 8), 8), :] += jnp.where(live, force, 0.0)

    def couple():
        for k in range(GROUP):
            terms = matmul(left_ref[k], right_ref[k])
            inverse = lax.rsqrt(terms[:, :width])
            coupling = terms[:, width:] * (inverse * inverse * inverse)
            high, low = halves(coupling)
            part_ref[k, :, :width] = high
            part_ref[k, :, width:] = low

    def build(group):
        for k in range(GROUP):
            live, near_block, near_tile, far_block, far_tile = pick(group, k)
            far_place = jnp.where(far_block > 0, far_block + (near_number - 1), 0)
            left, spread, numerator, near_rows, near_spot, far_rows, far_spot = operands(
                tile_of(near_block, near_tile), tile_of(far_place, far_tile)
            )
            stash = lax.rem(group, 3)
            left_ref[k] = left
            right_ref[k, : spread.shape[0], :width] = spread
            right_ref[k, spread.shape[0] :, width:] = numerator
            sums_ref[stash, k, 0] = near_rows
            sums_ref[stash, k, 1] = far_rows
            spots_ref[stash, k, 0] = near_spot
            spots_ref[stash, k, 1] = far_spot

    def step(group, carry):
        add_sums(group - 2)
        couple()
        build(group)
        return carry

    groups = jnp.maximum((count + GROUP - 1) // GROUP, 2)
    build(jnp.int32(0))
    couple()
    build(jnp.int32(1))
    lax.fori_loop(2, groups, step, 0)
    add_sums(groups - 2)
    couple()
    add_sums(groups - 1)

    for copy in sum_copies:
        copy.wait()
    at = 0
    if final:
        moments = functools.reduce(jnp.add, [lists[k, 1] for k in range(near_number)])
        old = [list(blocks) for blocks in done]
    for out in refs_out:
        for k in range(out.shape[0]):
            is_near = at < near_number
            total, block = (near_sum, at) if is_near else (far_sum, at - near_number)
            known = None
            if final:
                row = old[0 if is_near else 1]
                if block in row:
                    known = earlier_sums.at[row.index(block) + (0 if is_near else len(old[0]))]
            for axis in range(3):
                rows = slice(axis * tiles, (axis + 1) * tiles)
                value = total[block, pl.ds(axis, tiles, stride=8), :]
                out[k, rows, :] = value if known is None else value + known[rows, :]
            if final and not is_near:
                out[k, 3 * tiles :, :] = moments
            at += 1


def run_pairs(blocks, tiles, slots, list_group, totals, near, far, counts=None, done=None, earlier=()):
    width = blocks[0].shape[-1]
    final = counts is not None
    near_number, far_number = len(near), len(far)
    slot_count = totals[0] * totals[1] * slots
    hbm = pl.BlockSpec(memory_space=pl.ANY)
    vmem = pl.BlockSpec(memory_space=pltpu.VMEM)
    plan = (tiles, slots, list_group) + tuple(totals) + (near, far, done, final)
    if final:
        shapes = [(count, 3 * tiles, width) for count in counts[0]]
        shapes += [(count, 3 * tiles + 8, width) for count in counts[1]]
    else:
        shapes = [(1, 3 * tiles, width)] * (near_number + far_number)
    depth, sum_rows = 80, 16
    share = len(near) * len(far) / (totals[0] * totals[1])
    elements = int(share * slot_count / 3) * width * width

    scratch = [
        pltpu.VMEM((len(blocks),) + blocks[0].shape, jnp.float32),
        pltpu.VMEM((len(blocks), 2, 8, width), jnp.float32),
        pltpu.VMEM((near_number, 8 * tiles, width), jnp.float32),
        pltpu.VMEM((far_number, 8 * tiles, width), jnp.float32),
        pltpu.VMEM((8, slot_count), jnp.int32),
        pltpu.SMEM((8, slot_count), jnp.int32),
        pltpu.VMEM((GROUP, width, depth), jnp.bfloat16),
        pltpu.VMEM((GROUP, depth, 2 * width), jnp.bfloat16),
        pltpu.VMEM((GROUP, width, 2 * width), jnp.bfloat16),
        pltpu.VMEM((3, GROUP, 2, sum_rows, width), jnp.bfloat16),
        pltpu.VMEM((3, GROUP, 2, 8, width), jnp.float32),
        pltpu.VMEM((max(len(earlier), 1), 3 * tiles, width), jnp.float32),
        pltpu.SemaphoreType.DMA((len(blocks),)),
        pltpu.SemaphoreType.DMA((len(blocks),)),
        pltpu.SemaphoreType.DMA((max(len(earlier), 1),)),
    ]
    rows = 8 * blocks[0].shape[0] * len(blocks) + (11 * (near_number + far_number) + 3 * len(earlier)) * tiles
    limit = 4 * width * rows + 8 * 1024 * 1024

    def kernel(*refs):
        given = len(blocks)
        known = given + len(earlier)
        made = known + len(shapes)
        pair_kernel(plan, refs[:given], refs[given:known], refs[known:made], refs[made:])

    return pl.pallas_call(
        kernel,
        out_shape=[jax.ShapeDtypeStruct(shape, jnp.float32) for shape in shapes],
        in_specs=[hbm] * (len(blocks) + len(earlier)),
        out_specs=[vmem] * len(shapes),
        scratch_shapes=scratch,
        compiler_params=pltpu.CompilerParams(vmem_limit_bytes=limit),
        cost_estimate=pl.CostEstimate(flops=(1000 if final else 1) * elements, bytes_accessed=1 << 16, transcendentals=0),
        name="pairs" if final else "early_pairs",
    )(*blocks, *earlier)


NCELL = 64


def pack_kernel(steps, me_ref, count_ref, segment_ref, local_ref, remote_ref, sent_ref, cell_ref, out_ref):
    tiles, width = segment_ref.shape[1:]
    slots, devices = sent_ref.shape
    pairs = local_ref.shape[1]
    for row, axis in enumerate((3, 4, 5, 6, 7, 8, 0, 1)):
        out_ref[pl.ds(row, tiles, stride=8), :] = segment_ref[axis]
    out_ref[8 * tiles : 9 * tiles, :] = segment_ref[2]

    def order(shape, dim):
        slot = lax.broadcasted_iota(jnp.int32, shape, dim)
        part = slot // slots
        peer = jnp.full(shape, me_ref[0])
        for k, step in enumerate(steps):
            peer = jnp.bitwise_xor(peer, step * jnp.bitwise_and(part >> k, 1))
        return peer, slot % slots

    peer, column = order((pairs, width), 0)
    wanted = peer * slots + column
    table = jnp.zeros((8, pairs), jnp.float32)
    for k in range(pairs // width):
        lanes = slice(k * width, (k + 1) * width)
        position = lax.broadcasted_iota(jnp.int32, (8, width), 1) + k * width
        near = jnp.where(position < count_ref[0], local_ref[:, lanes] + 1, 0).astype(jnp.float32)
        named = jnp.where(wanted == remote_ref[:, lanes], 1.0, 0.0)
        table += matmul(near.astype(jnp.bfloat16), named.astype(jnp.bfloat16), (1, 1))
    peer = order((pairs, devices), 0)[0]
    named = jnp.where(peer == lax.broadcasted_iota(jnp.int32, (pairs, devices), 1), 1.0, 0.0)
    sent = matmul(sent_ref[...].astype(jnp.float32).astype(jnp.bfloat16), named.astype(jnp.bfloat16), (1, 1))
    column = lax.broadcasted_iota(jnp.int32, (slots, pairs), 1) % slots
    sent = jnp.where(lax.broadcasted_iota(jnp.int32, (slots, pairs), 0) == column, sent, 0.0)
    sent = jnp.sum(sent, axis=0, keepdims=True)
    for k in range(pairs // width):
        lanes = slice(k * width, (k + 1) * width)
        out_ref[9 * tiles + k : 9 * tiles + k + 1, :] = table[0:1, lanes] - 1.0
        out_ref[9 * tiles + 4 + k : 9 * tiles + 5 + k, :] = sent[:, lanes]

    lane = lax.broadcasted_iota(jnp.int32, (tiles, width), 1)
    outer = jnp.zeros((tiles, width), jnp.float32)
    for k in range(9):
        product = segment_ref[3 + k // 3] * segment_ref[6 + k % 3]
        outer = jnp.where(lane == k, jnp.sum(product, axis=1, keepdims=True), outer)
    cells = lax.broadcasted_iota(jnp.int32, (NCELL, tiles), 0)
    held = jnp.where(cells == cell_ref[...], 1.0, 0.0).astype(jnp.bfloat16)
    moments = sum(matmul(part.astype(jnp.bfloat16), held, (1, 1)) for part in thirds(outer.T[0:16]))
    last = jnp.where(lax.broadcasted_iota(jnp.int32, (8, NCELL), 0) == 0, moments[8:16], 0.0)
    out_ref[9 * tiles + 8 : 9 * tiles + 16, :] = jnp.concatenate([moments[0:8], last], axis=1)


def pack(me, segments, send_tiles, pair_local, pair_remote, pair_count, tile_cell, steps):
    tiles, rows, width = segments.shape
    smem = pl.BlockSpec(memory_space=pltpu.SMEM)
    vmem = pl.BlockSpec(memory_space=pltpu.VMEM)
    block = pl.pallas_call(
        functools.partial(pack_kernel, steps),
        out_shape=jax.ShapeDtypeStruct((rows * tiles + 16, width), jnp.float32),
        in_specs=[smem, smem] + [vmem] * 5,
        out_specs=vmem,
        compiler_params=pltpu.CompilerParams(vmem_limit_bytes=16 * 1024 * 1024),
        name="pack",
    )(
        me, pair_count, segments.transpose(1, 0, 2), pair_local, pair_remote, send_tiles[0].T, tile_cell.reshape(1, -1)
    )
    return block.reshape(-1, 8, width)


def far_field(segments, tile_cell, moment_sums, total_segments):
    moments = moment_sums.reshape(NCELL, 3, 3) / jnp.sqrt(jnp.float32(total_segments))
    moments = 0.5 * (moments + jnp.transpose(moments, (0, 2, 1)))
    cells = jnp.arange(NCELL).astype(jnp.float32)
    weights = 8.0 / (8.0 + jnp.abs(cells[:, None] - cells[None, :]))
    stress = jnp.dot(weights, moments.reshape(NCELL, 9), precision=lax.Precision.HIGHEST)
    onehot = (tile_cell[:, None] == jnp.arange(NCELL)[None, :]).astype(jnp.float32)
    tile_stress = jnp.dot(onehot, stress, precision=lax.Precision.HIGHEST).reshape(-1, 3, 3)
    traction = jnp.sum(tile_stress[:, :, :, None] * segments[:, None, 3:6, :], axis=2)
    lines = segments[:, 6:9, :]
    return jnp.stack(
        [
            traction[:, 1] * lines[:, 2] - traction[:, 2] * lines[:, 1],
            traction[:, 2] * lines[:, 0] - traction[:, 0] * lines[:, 2],
            traction[:, 0] * lines[:, 1] - traction[:, 1] * lines[:, 0],
        ],
        axis=1,
    )


AXES = ("dom", "sub")


def swap(value, mask):
    devices = lax.axis_size(AXES)
    return lax.ppermute(value, AXES, [(k, k ^ mask) for k in range(devices)])


def span(steps):
    masks = [0]
    for step in steps:
        masks += [mask ^ step for mask in masks]
    return masks


def mask_steps(devices):
    bits = devices.bit_length() - 1
    number = bits // 2
    far_steps = [devices >> (k + 2) for k in range(number)]
    near_steps = [devices >> 1] + [devices >> (k + 1) for k in range(number + 1, bits)]
    return near_steps, far_steps


def spread(block, near_steps, far_steps, work):
    steps = list(near_steps) + list(far_steps)
    allowed = set(span(near_steps)) | set(span(far_steps))
    held = {0: block}
    fresh = {0: -1}
    sums = None
    while fresh:
        arrived = {}
        for mask, last in fresh.items():
            for at in range(last + 1, len(steps)):
                if mask ^ steps[at] in allowed:
                    arrived[mask ^ steps[at]] = (swap(held[mask], steps[at]), at)
        if arrived:
            quick, slow = [], list(arrived)
            if len(held) > 1 and sums is None:
                quick = [mask for mask in arrived if arrived[mask][1] == len(near_steps) - 1]
                slow = [mask for mask in arrived if mask not in quick]
                held.update(zip(quick, lax.optimization_barrier([arrived[mask][0] for mask in quick])))
                sums = work(held)
            values, sums = lax.optimization_barrier(([arrived[mask][0] for mask in slow], sums))
            held.update(zip(slow, values))
        fresh = {mask: at for mask, (value, at) in arrived.items()}
    return [held[mask] for mask in span(near_steps)], [held[mask] for mask in span(far_steps)], sums


def message_counts(steps):
    counts = [1] * min(len(steps) and 2, 1 << len(steps))
    while sum(counts) < 1 << len(steps):
        counts.append(2 if sum(counts) >= 4 or len(steps) < 3 else 1)
    return counts


def collect(outs, counts, steps):
    groups = list(zip(outs, counts))
    for step in reversed(steps):
        half = sum(count for value, count in groups) // 2
        kept, sent, seen = [], [], 0
        for value, count in groups:
            (kept if seen < half else sent).append((value, count))
            seen += count
        arrived = []
        for value, count in reversed(sent):
            got = swap(value, step)
            arrived = [got[k : k + 1] for k in range(count)] + arrived
        merged, at = [], 0
        for value, count in kept:
            more = arrived[at : at + count]
            merged.append((value + (jnp.concatenate(more) if count > 1 else more[0]), count))
            at += count
        groups = merged
    return groups[0][0][0]


def on_device(segments, send_tiles, pair_local, pair_remote, pair_count, tile_cell):
    width = segments.shape[2]
    tiles = segments.shape[0]
    devices = send_tiles.shape[1]
    slots = send_tiles.shape[2]
    near_steps, far_steps = mask_steps(devices)
    near_masks, far_masks = span(near_steps), span(far_steps)

    me = lax.axis_index(AXES).astype(jnp.int32).reshape(1)
    block = pack(
        me, segments, send_tiles, pair_local, pair_remote, pair_count, tile_cell, far_steps + near_steps
    )
    list_group = block.shape[0] - 2
    totals = (len(near_masks), len(far_masks))
    early = []

    def early_pairs(held):
        early.extend([k for k, mask in enumerate(masks) if mask in held] for masks in (near_masks, far_masks))
        blocks = [held[near_masks[k]] for k in early[0]] + [held[far_masks[k]] for k in early[1][1:]]
        return run_pairs(blocks, tiles, slots, list_group, totals, early[0], early[1])

    near_blocks, far_blocks, sums = spread(block, near_steps, far_steps, early_pairs)
    near_counts, far_counts = message_counts(near_steps), message_counts(far_steps)
    outs = run_pairs(
        near_blocks + far_blocks[1:], tiles, slots, list_group, totals, list(range(totals[0])), list(range(totals[1])),
        (near_counts, far_counts), early, sums,
    )
    near_total = collect(outs[: len(near_counts)], near_counts, near_steps)
    far_total = collect(outs[len(near_counts) :], far_counts, far_steps)
    forces = (near_total + far_total[: 3 * tiles]).reshape(3, tiles, width)
    rows = far_total[3 * tiles :]
    moment_sums = jnp.concatenate([rows[:, :NCELL], rows[:1, NCELL : 2 * NCELL]]).T
    total_segments = tiles * width * devices
    return forces.transpose(1, 0, 2) + far_field(segments, tile_cell, moment_sums, total_segments)


def solution(mesh):
    in_specs = (
        P(("dom", "sub"), None, None),
        P(("dom", "sub"), None, None),
        P(("dom", "sub"), None),
        P(("dom", "sub"), None),
        P(("dom", "sub")),
        P(("dom", "sub")),
    )
    out_specs = P(("dom", "sub"), None, None)
    return jax.shard_map(
        on_device, mesh=mesh, in_specs=in_specs, out_specs=out_specs, check_vma=False
    )
```

```python
import functools
import jax
import jax.numpy as jnp
from jax import lax
from jax.sharding import PartitionSpec as P
from jax.experimental import pallas as pl
from jax.experimental.pallas import tpu as pltpu

CORE = 0.25
GROUP = 8


def head(value):
    return value.astype(jnp.bfloat16).astype(jnp.float32)


def thirds(value):
    high = head(value)
    rest = value - high
    middle = head(rest)
    return high, middle, rest - middle


def halves(value):
    high = value.astype(jnp.bfloat16)
    return high, (value - high.astype(jnp.float32)).astype(jnp.bfloat16)


def tall(groups):
    return jnp.concatenate(groups, axis=0).astype(jnp.bfloat16)


def place(sub, rows, others=0.0):
    filled = others
    for at, row in rows.items():
        filled = jnp.where(sub == at, row, filled)
    return filled


def tile_parts(sub, rows):
    parts = [thirds(rows[k]) for k in range(3)]
    square = rows[0] * rows[0] + rows[1] * rows[1] + rows[2] * rows[2]
    ones = jnp.where(sub == 3, 1.0, 0.0)
    high, middle = [place(sub, {k: parts[k][at] for k in range(3)}, 0.0) for at in range(2)]
    sums = tall([high + ones, middle])
    return parts, square, sums, place(sub, {k: rows[k] for k in range(3)}, 0.0)


def products(sub, first, second, burgers):
    major = jnp.where(sub < 3, first[0], jnp.where(sub < 6, first[1], first[2]))
    minor = jnp.where(sub % 3 == 0, second[0], jnp.where(sub % 3 == 1, second[1], second[2]))
    rest = place(sub, {0: first[2] * second[2], 1: burgers[0], 2: burgers[1], 3: burgers[2]}, 0.0)
    return [head(major * minor), head(rest)], [major * minor - head(major * minor), rest - head(rest)]


def operands(near, far):
    sub = lax.broadcasted_iota(jnp.int32, (8, near[0].shape[1]), 0)
    near = [jnp.broadcast_to(row, sub.shape) for row in near]
    far = [jnp.broadcast_to(row, sub.shape) for row in far]
    scale = 1.0 / near[0].shape[1]
    for k in range(3):
        middle = jnp.sum(near[k], axis=1, keepdims=True) * scale
        near[k], far[k] = near[k] - middle, far[k] - middle
    zero = jnp.zeros(sub.shape, jnp.float32)
    parts, square, near_sums, near_spot = tile_parts(sub, near)
    square = thirds(square)
    ends = [{6: square[0], 7: square[1]}, {6: square[2], 7: 1.0}, {6: 1.0, 7: 1.0}]
    left = [
        place(sub, {1: middle, 5: middle, 3: low, **end}, high) for (high, middle, low), end in zip(parts, ends)
    ]
    high, low = products(sub, near[3:6], near[6:9], near[3:6])
    left = tall(left + [zero] + high + low + high)

    parts, square, far_sums, far_spot = tile_parts(sub, far)
    square = thirds(square + CORE)
    ends = [{6: 1.0, 7: 1.0}, {6: 1.0, 7: square[0]}, {6: square[1], 7: square[2]}]
    spread = [
        place(sub, {2: -2.0 * middle, 5: -2.0 * middle, 4: -2.0 * low, **end}, -2.0 * high)
        for (high, middle, low), end in zip(parts, ends)
    ]
    high, low = products(sub, far[6:9], far[3:6], far[3:6])
    return left.T, tall(spread + [zero]), tall(high + high + low), near_sums, near_spot, far_sums, far_spot


def matmul(left, right, contract=(1, 0)):
    dims = (((contract[0],), (contract[1],)), ((), ()))
    return lax.dot_general(left, right, dims, preferred_element_type=jnp.float32)


def live_list(near_rows, far_rows, ids_ref):
    slots = ids_ref.shape[1]

    def line(rows):
        return jnp.concatenate([rows[k : k + 1] for k in range(rows.shape[0])], axis=1)

    near, far = line(near_rows), line(far_rows)
    alive = near >= 0
    row = lax.broadcasted_iota(jnp.int32, (slots, slots), 0)
    lane = lax.broadcasted_iota(jnp.int32, (slots, slots), 1)
    before = jnp.where(row < lane, 1.0, 0.0).astype(jnp.bfloat16)
    flags = jnp.where(alive, 1.0, 0.0)
    rank = matmul(jnp.broadcast_to(flags, (8, slots)).astype(jnp.bfloat16), before)[0:1]
    rank = jnp.where(alive, rank, -1.0)
    chosen = jnp.where(jnp.broadcast_to(rank, (slots, slots)) == row.astype(jnp.float32), 1.0, 0.0).astype(jnp.bfloat16)
    sub = lax.broadcasted_iota(jnp.int32, (8, slots), 0)
    near, far = jnp.maximum(near, 0).astype(jnp.int32), jnp.maximum(far, 0).astype(jnp.int32)
    values = [near >> 6, near & 63, far >> 6, far & 63]
    values = place(sub, {k: value.astype(jnp.float32) for k, value in enumerate(values)}, jnp.zeros((8, slots), jnp.float32))
    packed = matmul(values.astype(jnp.bfloat16), chosen, (1, 1)).astype(jnp.int32)
    number = jnp.sum(flags, axis=1, keepdims=True).astype(jnp.int32)
    ids_ref[0:1, :] = packed[0:1] * 64 + packed[1:2]
    ids_ref[1:2, :] = packed[2:3] * 64 + packed[3:4]
    ids_ref[2:3, :] = jnp.broadcast_to(number, (1, slots))


def pair_kernel(plan, sources, earlier, refs_out, scratch):
    tiles, slots, list_group, near_total, far_total, near, far, done, final = plan
    near_number, far_number = len(near), len(far)
    (blocks, lists, near_sum, far_sum, ids_vmem, ids, left_ref, right_ref, part_ref, sums_ref, spots_ref, earlier_sums,
     sems, list_sems, sum_sems) = scratch
    list_copies = [
        pltpu.make_async_copy(source.at[pl.ds(list_group, 2)], lists.at[k], list_sems.at[k])
        for k, source in enumerate(sources)
    ]
    copies = [pltpu.make_async_copy(source, blocks.at[k], sems.at[k]) for k, source in enumerate(sources)]
    sum_copies = [pltpu.make_async_copy(given.at[0], earlier_sums.at[k], sum_sems.at[k]) for k, given in enumerate(earlier)]
    for copy in list_copies + copies + sum_copies:
        copy.start()
    near_sum[...] = jnp.zeros_like(near_sum)
    far_sum[...] = jnp.zeros_like(far_sum)
    right_ref[...] = jnp.zeros_like(right_ref)
    for copy in list_copies:
        copy.wait()

    width = blocks.shape[-1]
    shape = (4, width)
    position = lax.broadcasted_iota(jnp.int32, shape, 0) * width + lax.broadcasted_iota(jnp.int32, shape, 1)
    near_ids = jnp.full(shape, -1.0)
    near_at = position // (far_total * slots)
    far_at = position // slots % far_total
    for k, block in enumerate(near):
        given = lists[k, 0, 0:4]
        given = jnp.where(given >= 0, given + k * tiles, given)
        near_ids = jnp.where(near_at == block, given, near_ids)
    far_ids = jnp.full(shape, -1.0)
    for k, block in enumerate(far):
        given = lists[near_number - 1 + k if k else 0, 0, 4:8] + k * tiles
        far_ids = jnp.where(far_at == block, given, far_ids)
    near_ids = jnp.where(far_ids >= 0, near_ids, -1.0)
    if done:
        old_near = functools.reduce(jnp.logical_or, [near_at == block for block in done[0]])
        old_far = functools.reduce(jnp.logical_or, [far_at == block for block in done[1]])
        near_ids = jnp.where(jnp.logical_and(old_near, old_far), -1.0, near_ids)
    live_list(near_ids, far_ids, ids_vmem)
    move = pltpu.make_async_copy(ids_vmem, ids, list_sems.at[0])
    move.start()
    move.wait()
    count = ids[2, 0]
    last = ids.shape[1] - 1
    for copy in copies:
        copy.wait()

    def tile_of(block, tile):
        rows = [blocks[block, tile, pl.ds(k, 1), :] for k in range(8)]
        return rows[6:8] + [blocks[block, tiles + tile // 8, pl.ds(tile % 8, 1), :]] + rows[0:6]

    def pick(group, k):
        at = group * GROUP + k
        held = jnp.clip(at, 0, last)
        near, far = ids[0, held], ids[1, held]
        live = jnp.logical_and(at >= 0, at < count)
        return live, near // tiles, near % tiles, far // tiles, far % tiles

    def add_sums(group):
        for k in range(GROUP):
            live, near_block, near_tile, far_block, far_tile = pick(group, k)
            stash = lax.rem(group, 3)
            near_rows, far_rows = sums_ref[stash, k, 0], sums_ref[stash, k, 1]
            parts = part_ref[k]
            half = parts.shape[1] // 2
            for block, tile, spot, total, out in (
                (near_block, near_tile, 0, matmul(jnp.concatenate([far_rows, far_rows], axis=1), parts, (1, 1)), near_sum),
                (far_block, far_tile, 1, matmul(near_rows, parts), far_sum),
            ):
                total = total[0:8] + total[8:16]
                if total.shape[1] > half:
                    total = total[:, :half] + total[:, half:]
                force = spots_ref[stash, k, spot] * jnp.broadcast_to(total[3:4], total.shape) - total
                out[block, pl.ds(pl.multiple_of(tile * 8, 8), 8), :] += jnp.where(live, force, 0.0)

    def couple():
        for k in range(GROUP):
            terms = matmul(left_ref[k], right_ref[k])
            inverse = lax.rsqrt(terms[:, :width])
            coupling = terms[:, width:] * (inverse * inverse * inverse)
            high, low = halves(coupling)
            part_ref[k, :, :width] = high
            part_ref[k, :, width:] = low

    def build(group):
        for k in range(GROUP):
            live, near_block, near_tile, far_block, far_tile = pick(group, k)
            far_place = jnp.where(far_block > 0, far_block + (near_number - 1), 0)
            left, spread, numerator, near_rows, near_spot, far_rows, far_spot = operands(
                tile_of(near_block, near_tile), tile_of(far_place, far_tile)
            )
            stash = lax.rem(group, 3)
            left_ref[k] = left
            right_ref[k, : spread.shape[0], :width] = spread
            right_ref[k, spread.shape[0] :, width:] = numerator
            sums_ref[stash, k, 0] = near_rows
            sums_ref[stash, k, 1] = far_rows
            spots_ref[stash, k, 0] = near_spot
            spots_ref[stash, k, 1] = far_spot

    def step(group, carry):
        add_sums(group - 2)
        couple()
        build(group)
        return carry

    groups = jnp.maximum((count + GROUP - 1) // GROUP, 2)
    build(jnp.int32(0))
    couple()
    build(jnp.int32(1))
    lax.fori_loop(2, groups, step, 0)
    add_sums(groups - 2)
    couple()
    add_sums(groups - 1)

    for copy in sum_copies:
        copy.wait()
    at = 0
    if final:
        moments = functools.reduce(jnp.add, [lists[k, 1] for k in range(near_number)])
        old = [list(blocks) for blocks in done]
    for out in refs_out:
        for k in range(out.shape[0]):
            is_near = at < near_number
            total, block = (near_sum, at) if is_near else (far_sum, at - near_number)
            known = None
            if final:
                row = old[0 if is_near else 1]
                if block in row:
                    known = earlier_sums.at[row.index(block) + (0 if is_near else len(old[0]))]
            for axis in range(3):
                rows = slice(axis * tiles, (axis + 1) * tiles)
                value = total[block, pl.ds(axis, tiles, stride=8), :]
                out[k, rows, :] = value if known is None else value + known[rows, :]
            if final and not is_near:
                out[k, 3 * tiles :, :] = moments
            at += 1


def run_pairs(blocks, tiles, slots, list_group, totals, near, far, counts=None, done=None, earlier=()):
    width = blocks[0].shape[-1]
    final = counts is not None
    near_number, far_number = len(near), len(far)
    slot_count = totals[0] * totals[1] * slots
    hbm = pl.BlockSpec(memory_space=pl.ANY)
    vmem = pl.BlockSpec(memory_space=pltpu.VMEM)
    plan = (tiles, slots, list_group) + tuple(totals) + (near, far, done, final)
    if final:
        shapes = [(count, 3 * tiles, width) for count in counts[0]]
        shapes += [(count, 3 * tiles + 8, width) for count in counts[1]]
    else:
        shapes = [(1, 3 * tiles, width)] * (near_number + far_number)
    depth, sum_rows = 80, 16
    share = len(near) * len(far) / (totals[0] * totals[1])
    elements = int(share * slot_count / 3) * width * width

    scratch = [
        pltpu.VMEM((len(blocks),) + blocks[0].shape, jnp.float32),
        pltpu.VMEM((len(blocks), 2, 8, width), jnp.float32),
        pltpu.VMEM((near_number, 8 * tiles, width), jnp.float32),
        pltpu.VMEM((far_number, 8 * tiles, width), jnp.float32),
        pltpu.VMEM((8, slot_count), jnp.int32),
        pltpu.SMEM((8, slot_count), jnp.int32),
        pltpu.VMEM((GROUP, width, depth), jnp.bfloat16),
        pltpu.VMEM((GROUP, depth, 2 * width), jnp.bfloat16),
        pltpu.VMEM((GROUP, width, 2 * width), jnp.bfloat16),
        pltpu.VMEM((3, GROUP, 2, sum_rows, width), jnp.bfloat16),
        pltpu.VMEM((3, GROUP, 2, 8, width), jnp.float32),
        pltpu.VMEM((max(len(earlier), 1), 3 * tiles, width), jnp.float32),
        pltpu.SemaphoreType.DMA((len(blocks),)),
        pltpu.SemaphoreType.DMA((len(blocks),)),
        pltpu.SemaphoreType.DMA((max(len(earlier), 1),)),
    ]
    rows = 8 * blocks[0].shape[0] * len(blocks) + (11 * (near_number + far_number) + 3 * len(earlier)) * tiles
    limit = 4 * width * rows + 8 * 1024 * 1024

    def kernel(*refs):
        given = len(blocks)
        known = given + len(earlier)
        made = known + len(shapes)
        pair_kernel(plan, refs[:given], refs[given:known], refs[known:made], refs[made:])

    return pl.pallas_call(
        kernel,
        out_shape=[jax.ShapeDtypeStruct(shape, jnp.float32) for shape in shapes],
        in_specs=[hbm] * (len(blocks) + len(earlier)),
        out_specs=[vmem] * len(shapes),
        scratch_shapes=scratch,
        compiler_params=pltpu.CompilerParams(vmem_limit_bytes=limit),
        cost_estimate=pl.CostEstimate(flops=(1000 if final else 1) * elements, bytes_accessed=1 << 16, transcendentals=0),
        name="pairs" if final else "early_pairs",
    )(*blocks, *earlier)


NCELL = 64


def pack_kernel(steps, me_ref, count_ref, segment_ref, local_ref, remote_ref, sent_ref, cell_ref, out_ref):
    tiles, width = segment_ref.shape[1:]
    slots, devices = sent_ref.shape
    pairs = local_ref.shape[1]
    for row, axis in enumerate((3, 4, 5, 6, 7, 8, 0, 1)):
        out_ref[pl.ds(row, tiles, stride=8), :] = segment_ref[axis]
    out_ref[8 * tiles : 9 * tiles, :] = segment_ref[2]

    def order(shape, dim):
        slot = lax.broadcasted_iota(jnp.int32, shape, dim)
        part = slot // slots
        peer = jnp.full(shape, me_ref[0])
        for k, step in enumerate(steps):
            peer = jnp.bitwise_xor(peer, step * jnp.bitwise_and(part >> k, 1))
        return peer, slot % slots

    peer, column = order((pairs, width), 0)
    wanted = peer * slots + column
    table = jnp.zeros((8, pairs), jnp.float32)
    for k in range(pairs // width):
        lanes = slice(k * width, (k + 1) * width)
        position = lax.broadcasted_iota(jnp.int32, (8, width), 1) + k * width
        near = jnp.where(position < count_ref[0], local_ref[:, lanes] + 1, 0).astype(jnp.float32)
        named = jnp.where(wanted == remote_ref[:, lanes], 1.0, 0.0)
        table += matmul(near.astype(jnp.bfloat16), named.astype(jnp.bfloat16), (1, 1))
    peer = order((pairs, devices), 0)[0]
    named = jnp.where(peer == lax.broadcasted_iota(jnp.int32, (pairs, devices), 1), 1.0, 0.0)
    sent = matmul(sent_ref[...].astype(jnp.float32).astype(jnp.bfloat16), named.astype(jnp.bfloat16), (1, 1))
    column = lax.broadcasted_iota(jnp.int32, (slots, pairs), 1) % slots
    sent = jnp.where(lax.broadcasted_iota(jnp.int32, (slots, pairs), 0) == column, sent, 0.0)
    sent = jnp.sum(sent, axis=0, keepdims=True)
    for k in range(pairs // width):
        lanes = slice(k * width, (k + 1) * width)
        out_ref[9 * tiles + k : 9 * tiles + k + 1, :] = table[0:1, lanes] - 1.0
        out_ref[9 * tiles + 4 + k : 9 * tiles + 5 + k, :] = sent[:, lanes]

    lane = lax.broadcasted_iota(jnp.int32, (tiles, width), 1)
    outer = jnp.zeros((tiles, width), jnp.float32)
    for k in range(9):
        product = segment_ref[3 + k // 3] * segment_ref[6 + k % 3]
        outer = jnp.where(lane == k, jnp.sum(product, axis=1, keepdims=True), outer)
    cells = lax.broadcasted_iota(jnp.int32, (NCELL, tiles), 0)
    held = jnp.where(cells == cell_ref[...], 1.0, 0.0).astype(jnp.bfloat16)
    moments = sum(matmul(part.astype(jnp.bfloat16), held, (1, 1)) for part in thirds(outer.T[0:16]))
    last = jnp.where(lax.broadcasted_iota(jnp.int32, (8, NCELL), 0) == 0, moments[8:16], 0.0)
    out_ref[9 * tiles + 8 : 9 * tiles + 16, :] = jnp.concatenate([moments[0:8], last], axis=1)


def pack(me, segments, send_tiles, pair_local, pair_remote, pair_count, tile_cell, steps):
    tiles, rows, width = segments.shape
    smem = pl.BlockSpec(memory_space=pltpu.SMEM)
    vmem = pl.BlockSpec(memory_space=pltpu.VMEM)
    block = pl.pallas_call(
        functools.partial(pack_kernel, steps),
        out_shape=jax.ShapeDtypeStruct((rows * tiles + 16, width), jnp.float32),
        in_specs=[smem, smem] + [vmem] * 5,
        out_specs=vmem,
        compiler_params=pltpu.CompilerParams(vmem_limit_bytes=16 * 1024 * 1024),
        name="pack",
    )(
        me, pair_count, segments.transpose(1, 0, 2), pair_local, pair_remote, send_tiles[0].T, tile_cell.reshape(1, -1)
    )
    return block.reshape(-1, 8, width)


def far_field(segments, tile_cell, moment_sums, total_segments):
    moments = moment_sums.reshape(NCELL, 3, 3) / jnp.sqrt(jnp.float32(total_segments))
    moments = 0.5 * (moments + jnp.transpose(moments, (0, 2, 1)))
    cells = jnp.arange(NCELL).astype(jnp.float32)
    weights = 8.0 / (8.0 + jnp.abs(cells[:, None] - cells[None, :]))
    stress = jnp.dot(weights, moments.reshape(NCELL, 9), precision=lax.Precision.HIGHEST)
    onehot = (tile_cell[:, None] == jnp.arange(NCELL)[None, :]).astype(jnp.float32)
    tile_stress = jnp.dot(onehot, stress, precision=lax.Precision.HIGHEST).reshape(-1, 3, 3)
    traction = jnp.sum(tile_stress[:, :, :, None] * segments[:, None, 3:6, :], axis=2)
    lines = segments[:, 6:9, :]
    return jnp.stack(
        [
            traction[:, 1] * lines[:, 2] - traction[:, 2] * lines[:, 1],
            traction[:, 2] * lines[:, 0] - traction[:, 0] * lines[:, 2],
            traction[:, 0] * lines[:, 1] - traction[:, 1] * lines[:, 0],
        ],
        axis=1,
    )


AXES = ("dom", "sub")


def swap(value, mask):
    devices = lax.axis_size(AXES)
    return lax.ppermute(value, AXES, [(k, k ^ mask) for k in range(devices)])


def span(steps):
    masks = [0]
    for step in steps:
        masks += [mask ^ step for mask in masks]
    return masks


def mask_steps(devices):
    bits = devices.bit_length() - 1
    number = bits // 2
    far_steps = [devices >> (k + 2) for k in range(number)]
    near_steps = [devices >> 1] + [devices >> (k + 1) for k in range(number + 1, bits)]
    return near_steps, far_steps


def spread(block, near_steps, far_steps, work):
    steps = list(near_steps) + list(far_steps)
    allowed = set(span(near_steps)) | set(span(far_steps))
    held = {0: block}
    fresh = {0: -1}
    sums = None
    while fresh:
        arrived = {}
        for mask, last in fresh.items():
            for at in range(last + 1, len(steps)):
                if mask ^ steps[at] in allowed:
                    arrived[mask ^ steps[at]] = (swap(held[mask], steps[at]), at)
        if arrived:
            quick, slow = [], list(arrived)
            if len(held) > 1 and sums is None:
                quick = [mask for mask in arrived if arrived[mask][1] == len(near_steps) - 1]
                slow = [mask for mask in arrived if mask not in quick]
                held.update(zip(quick, lax.optimization_barrier([arrived[mask][0] for mask in quick])))
                sums = work(held)
            values, sums = lax.optimization_barrier(([arrived[mask][0] for mask in slow], sums))
            held.update(zip(slow, values))
        fresh = {mask: at for mask, (value, at) in arrived.items()}
    return [held[mask] for mask in span(near_steps)], [held[mask] for mask in span(far_steps)], sums


def message_counts(steps):
    counts = [1] * min(len(steps) and 2, 1 << len(steps))
    while sum(counts) < 1 << len(steps):
        counts.append(2 if sum(counts) >= 4 or len(steps) < 3 else 1)
    return counts


def collect(outs, counts, steps):
    groups = list(zip(outs, counts))
    for step in reversed(steps):
        half = sum(count for value, count in groups) // 2
        kept, sent, seen = [], [], 0
        for value, count in groups:
            (kept if seen < half else sent).append((value, count))
            seen += count
        arrived = []
        for value, count in reversed(sent):
            got = swap(value, step)
            arrived = [got[k : k + 1] for k in range(count)] + arrived
        merged, at = [], 0
        for value, count in kept:
            more = arrived[at : at + count]
            merged.append((value + (jnp.concatenate(more) if count > 1 else more[0]), count))
            at += count
        groups = merged
    return groups[0][0][0]


def on_device(segments, send_tiles, pair_local, pair_remote, pair_count, tile_cell):
    width = segments.shape[2]
    tiles = segments.shape[0]
    devices = send_tiles.shape[1]
    slots = send_tiles.shape[2]
    near_steps, far_steps = mask_steps(devices)
    near_masks, far_masks = span(near_steps), span(far_steps)

    me = lax.axis_index(AXES).astype(jnp.int32).reshape(1)
    block = pack(
        me, segments, send_tiles, pair_local, pair_remote, pair_count, tile_cell, far_steps + near_steps
    )
    list_group = block.shape[0] - 2
    totals = (len(near_masks), len(far_masks))
    early = []

    def early_pairs(held):
        early.extend([k for k, mask in enumerate(masks) if mask in held] for masks in (near_masks, far_masks))
        blocks = [held[near_masks[k]] for k in early[0]] + [held[far_masks[k]] for k in early[1][1:]]
        return run_pairs(blocks, tiles, slots, list_group, totals, early[0], early[1])

    near_blocks, far_blocks, sums = spread(block, near_steps, far_steps, early_pairs)
    near_counts, far_counts = message_counts(near_steps), [1] * len(far_masks)
    outs = run_pairs(
        near_blocks + far_blocks[1:], tiles, slots, list_group, totals, list(range(totals[0])), list(range(totals[1])),
        (near_counts, far_counts), early, sums,
    )
    near_total = collect(outs[: len(near_counts)], near_counts, near_steps)
    far_total = collect(outs[len(near_counts) :], far_counts, far_steps)
    near_total, far_total = lax.optimization_barrier((near_total, far_total))
    forces = (near_total + far_total[: 3 * tiles]).reshape(3, tiles, width)
    rows = far_total[3 * tiles :]
    moment_sums = jnp.concatenate([rows[:, :NCELL], rows[:1, NCELL : 2 * NCELL]]).T
    total_segments = tiles * width * devices
    return forces.transpose(1, 0, 2) + far_field(segments, tile_cell, moment_sums, total_segments)


def solution(mesh):
    in_specs = (
        P(("dom", "sub"), None, None),
        P(("dom", "sub"), None, None),
        P(("dom", "sub"), None),
        P(("dom", "sub"), None),
        P(("dom", "sub")),
        P(("dom", "sub")),
    )
    out_specs = P(("dom", "sub"), None, None)
    return jax.shard_map(
        on_device, mesh=mesh, in_specs=in_specs, out_specs=out_specs, check_vma=False
    )
```

```python
import functools
import jax
import jax.numpy as jnp
from jax import lax
from jax.sharding import PartitionSpec as P
from jax.experimental import pallas as pl
from jax.experimental.pallas import tpu as pltpu

CORE = 0.25
GROUP = 8


def head(value):
    return value.astype(jnp.bfloat16).astype(jnp.float32)


def thirds(value):
    high = head(value)
    rest = value - high
    middle = head(rest)
    return high, middle, rest - middle


def halves(value):
    high = value.astype(jnp.bfloat16)
    return high, (value - high.astype(jnp.float32)).astype(jnp.bfloat16)


def tall(groups):
    return jnp.concatenate(groups, axis=0).astype(jnp.bfloat16)


def place(sub, rows, others=0.0):
    filled = others
    for at, row in rows.items():
        filled = jnp.where(sub == at, row, filled)
    return filled


def tile_parts(sub, rows):
    parts = [thirds(rows[k]) for k in range(3)]
    square = rows[0] * rows[0] + rows[1] * rows[1] + rows[2] * rows[2]
    ones = jnp.where(sub == 3, 1.0, 0.0)
    high, middle = [place(sub, {k: parts[k][at] for k in range(3)}, 0.0) for at in range(2)]
    sums = tall([high + ones, middle])
    return parts, square, sums, place(sub, {k: rows[k] for k in range(3)}, 0.0)


def products(sub, first, second, burgers):
    major = jnp.where(sub < 3, first[0], jnp.where(sub < 6, first[1], first[2]))
    minor = jnp.where(sub % 3 == 0, second[0], jnp.where(sub % 3 == 1, second[1], second[2]))
    rows = {0: first[2] * second[2], 1: burgers[0], 2: burgers[1]}
    parts = []
    for value in (major * minor, place(sub % 4, rows, burgers[2])):
        high = head(value)
        parts.append((high, value - high))
    return parts


def operands(near, far):
    sub = lax.broadcasted_iota(jnp.int32, (8, near[0].shape[1]), 0)
    near = [jnp.broadcast_to(row, sub.shape) for row in near]
    far = [jnp.broadcast_to(row, sub.shape) for row in far]
    scale = 1.0 / near[0].shape[1]
    for k in range(3):
        middle = jnp.sum(near[k], axis=1, keepdims=True) * scale
        near[k], far[k] = near[k] - middle, far[k] - middle
    zero = jnp.zeros(sub.shape, jnp.float32)
    parts, square, near_sums, near_spot = tile_parts(sub, near)
    square = thirds(square)
    ends = [{6: square[0], 7: square[1]}, {6: square[2], 7: 1.0}, {6: 1.0, 7: 1.0}]
    left = [
        place(sub, {1: middle, 5: middle, 3: low, **end}, high) for (high, middle, low), end in zip(parts, ends)
    ]
    (main, main_low), (rest, rest_low) = products(sub, near[3:6], near[6:9], near[3:6])
    half = sub < 4
    left = tall(left + [main, jnp.where(half, rest, rest_low), main_low, main, jnp.where(half, rest, 0.0)])

    parts, square, far_sums, far_spot = tile_parts(sub, far)
    square = thirds(square + CORE)
    ends = [{6: 1.0, 7: 1.0}, {6: 1.0, 7: square[0]}, {6: square[1], 7: square[2]}]
    spread = [
        place(sub, {2: -2.0 * middle, 5: -2.0 * middle, 4: -2.0 * low, **end}, -2.0 * high)
        for (high, middle, low), end in zip(parts, ends)
    ]
    (main, main_low), (rest, rest_low) = products(sub, far[6:9], far[3:6], far[3:6])
    numerator = tall([zero, main, rest, main, main_low, jnp.where(half, rest_low, 0.0)])
    return left.T, tall(spread + [zero]), numerator, near_sums, near_spot, far_sums, far_spot


def matmul(left, right, contract=(1, 0)):
    dims = (((contract[0],), (contract[1],)), ((), ()))
    return lax.dot_general(left, right, dims, preferred_element_type=jnp.float32)


def live_list(near_rows, far_rows, ids_ref):
    slots = ids_ref.shape[1]

    def line(rows):
        return jnp.concatenate([rows[k : k + 1] for k in range(rows.shape[0])], axis=1)

    near, far = line(near_rows), line(far_rows)
    alive = near >= 0
    row = lax.broadcasted_iota(jnp.int32, (slots, slots), 0)
    lane = lax.broadcasted_iota(jnp.int32, (slots, slots), 1)
    before = jnp.where(row < lane, 1.0, 0.0).astype(jnp.bfloat16)
    flags = jnp.where(alive, 1.0, 0.0)
    rank = matmul(jnp.broadcast_to(flags, (8, slots)).astype(jnp.bfloat16), before)[0:1]
    rank = jnp.where(alive, rank, -1.0)
    chosen = jnp.where(jnp.broadcast_to(rank, (slots, slots)) == row.astype(jnp.float32), 1.0, 0.0).astype(jnp.bfloat16)
    sub = lax.broadcasted_iota(jnp.int32, (8, slots), 0)
    near, far = jnp.maximum(near, 0).astype(jnp.int32), jnp.maximum(far, 0).astype(jnp.int32)
    values = [near >> 6, near & 63, far >> 6, far & 63]
    values = place(sub, {k: value.astype(jnp.float32) for k, value in enumerate(values)}, jnp.zeros((8, slots), jnp.float32))
    packed = matmul(values.astype(jnp.bfloat16), chosen, (1, 1)).astype(jnp.int32)
    number = jnp.sum(flags, axis=1, keepdims=True).astype(jnp.int32)
    ids_ref[0:1, :] = packed[0:1] * 64 + packed[1:2]
    ids_ref[1:2, :] = packed[2:3] * 64 + packed[3:4]
    ids_ref[2:3, :] = jnp.broadcast_to(number, (1, slots))


def pair_kernel(plan, sources, earlier, refs_out, scratch):
    tiles, slots, list_group, near_total, far_total, near, far, done, final = plan
    near_number, far_number = len(near), len(far)
    (blocks, lists, near_sum, far_sum, ids_vmem, ids, left_ref, right_ref, part_ref, sums_ref, spots_ref, earlier_sums,
     sems, list_sems, sum_sems) = scratch
    list_copies = [
        pltpu.make_async_copy(source.at[pl.ds(list_group, 2)], lists.at[k], list_sems.at[k])
        for k, source in enumerate(sources)
    ]
    copies = [pltpu.make_async_copy(source, blocks.at[k], sems.at[k]) for k, source in enumerate(sources)]
    sum_copies = [pltpu.make_async_copy(given.at[0], earlier_sums.at[k], sum_sems.at[k]) for k, given in enumerate(earlier)]
    for copy in list_copies + copies + sum_copies:
        copy.start()
    near_sum[...] = jnp.zeros_like(near_sum)
    far_sum[...] = jnp.zeros_like(far_sum)
    right_ref[...] = jnp.zeros_like(right_ref)
    for copy in list_copies:
        copy.wait()

    width = blocks.shape[-1]
    shape = (4, width)
    position = lax.broadcasted_iota(jnp.int32, shape, 0) * width + lax.broadcasted_iota(jnp.int32, shape, 1)
    near_ids = jnp.full(shape, -1.0)
    near_at = position // (far_total * slots)
    far_at = position // slots % far_total
    for k, block in enumerate(near):
        given = lists[k, 0, 0:4]
        given = jnp.where(given >= 0, given + k * tiles, given)
        near_ids = jnp.where(near_at == block, given, near_ids)
    far_ids = jnp.full(shape, -1.0)
    for k, block in enumerate(far):
        given = lists[near_number - 1 + k if k else 0, 0, 4:8] + k * tiles
        far_ids = jnp.where(far_at == block, given, far_ids)
    near_ids = jnp.where(far_ids >= 0, near_ids, -1.0)
    if done:
        old_near = functools.reduce(jnp.logical_or, [near_at == block for block in done[0]])
        old_far = functools.reduce(jnp.logical_or, [far_at == block for block in done[1]])
        near_ids = jnp.where(jnp.logical_and(old_near, old_far), -1.0, near_ids)
    live_list(near_ids, far_ids, ids_vmem)
    move = pltpu.make_async_copy(ids_vmem, ids, list_sems.at[0])
    move.start()
    move.wait()
    count = ids[2, 0]
    last = ids.shape[1] - 1
    for copy in copies:
        copy.wait()

    def tile_of(block, tile):
        rows = [blocks[block, tile, pl.ds(k, 1), :] for k in range(8)]
        return rows[6:8] + [blocks[block, tiles + tile // 8, pl.ds(tile % 8, 1), :]] + rows[0:6]

    def pick(group, k):
        at = group * GROUP + k
        held = jnp.clip(at, 0, last)
        near, far = ids[0, held], ids[1, held]
        live = jnp.logical_and(at >= 0, at < count)
        return live, near // tiles, near % tiles, far // tiles, far % tiles

    def add_sums(group):
        for k in range(GROUP):
            live, near_block, near_tile, far_block, far_tile = pick(group, k)
            stash = lax.rem(group, 3)
            near_rows, far_rows = sums_ref[stash, k, 0], sums_ref[stash, k, 1]
            parts = part_ref[k]
            half = parts.shape[1] // 2
            for block, tile, spot, total, out in (
                (near_block, near_tile, 0, matmul(jnp.concatenate([far_rows, far_rows], axis=1), parts, (1, 1)), near_sum),
                (far_block, far_tile, 1, matmul(near_rows, parts), far_sum),
            ):
                total = total[0:8] + total[8:16]
                if total.shape[1] > half:
                    total = total[:, :half] + total[:, half:]
                force = spots_ref[stash, k, spot] * jnp.broadcast_to(total[3:4], total.shape) - total
                out[block, pl.ds(pl.multiple_of(tile * 8, 8), 8), :] += jnp.where(live, force, 0.0)

    def couple():
        for k in range(GROUP):
            terms = matmul(left_ref[k], right_ref[k])
            inverse = lax.rsqrt(terms[:, :width])
            coupling = terms[:, width:] * (inverse * inverse * inverse)
            high, low = halves(coupling)
            part_ref[k, :, :width] = high
            part_ref[k, :, width:] = low

    def build(group):
        for k in range(GROUP):
            live, near_block, near_tile, far_block, far_tile = pick(group, k)
            far_place = jnp.where(far_block > 0, far_block + (near_number - 1), 0)
            left, spread, numerator, near_rows, near_spot, far_rows, far_spot = operands(
                tile_of(near_block, near_tile), tile_of(far_place, far_tile)
            )
            stash = lax.rem(group, 3)
            left_ref[k] = left
            right_ref[k, : spread.shape[0], :width] = spread
            right_ref[k, right_ref.shape[1] - numerator.shape[0] :, width:] = numerator
            sums_ref[stash, k, 0] = near_rows
            sums_ref[stash, k, 1] = far_rows
            spots_ref[stash, k, 0] = near_spot
            spots_ref[stash, k, 1] = far_spot

    def step(group, carry):
        add_sums(group - 2)
        couple()
        build(group)
        return carry

    groups = jnp.maximum((count + GROUP - 1) // GROUP, 2)
    build(jnp.int32(0))
    couple()
    build(jnp.int32(1))
    lax.fori_loop(2, groups, step, 0)
    add_sums(groups - 2)
    couple()
    add_sums(groups - 1)

    for copy in sum_copies:
        copy.wait()
    at = 0
    if final:
        moments = functools.reduce(jnp.add, [lists[k, 1] for k in range(near_number)])
        old = [list(blocks) for blocks in done]
    for out in refs_out:
        for k in range(out.shape[0]):
            is_near = at < near_number
            total, block = (near_sum, at) if is_near else (far_sum, at - near_number)
            known = None
            if final:
                row = old[0 if is_near else 1]
                if block in row:
                    known = earlier_sums.at[row.index(block) + (0 if is_near else len(old[0]))]
            for axis in range(3):
                rows = slice(axis * tiles, (axis + 1) * tiles)
                value = total[block, pl.ds(axis, tiles, stride=8), :]
                out[k, rows, :] = value if known is None else value + known[rows, :]
            if final and not is_near:
                out[k, 3 * tiles :, :] = moments
            at += 1


def run_pairs(blocks, tiles, slots, list_group, totals, near, far, counts=None, done=None, earlier=()):
    width = blocks[0].shape[-1]
    final = counts is not None
    near_number, far_number = len(near), len(far)
    slot_count = totals[0] * totals[1] * slots
    hbm = pl.BlockSpec(memory_space=pl.ANY)
    vmem = pl.BlockSpec(memory_space=pltpu.VMEM)
    plan = (tiles, slots, list_group) + tuple(totals) + (near, far, done, final)
    if final:
        shapes = [(count, 3 * tiles, width) for count in counts[0]]
        shapes += [(count, 3 * tiles + 8, width) for count in counts[1]]
    else:
        shapes = [(1, 3 * tiles, width)] * (near_number + far_number)
    depth, sum_rows = 64, 16
    share = len(near) * len(far) / (totals[0] * totals[1])
    elements = int(share * slot_count / 3) * width * width

    scratch = [
        pltpu.VMEM((len(blocks),) + blocks[0].shape, jnp.float32),
        pltpu.VMEM((len(blocks), 2, 8, width), jnp.float32),
        pltpu.VMEM((near_number, 8 * tiles, width), jnp.float32),
        pltpu.VMEM((far_number, 8 * tiles, width), jnp.float32),
        pltpu.VMEM((8, slot_count), jnp.int32),
        pltpu.SMEM((8, slot_count), jnp.int32),
        pltpu.VMEM((GROUP, width, depth), jnp.bfloat16),
        pltpu.VMEM((GROUP, depth, 2 * width), jnp.bfloat16),
        pltpu.VMEM((GROUP, width, 2 * width), jnp.bfloat16),
        pltpu.VMEM((3, GROUP, 2, sum_rows, width), jnp.bfloat16),
        pltpu.VMEM((3, GROUP, 2, 8, width), jnp.float32),
        pltpu.VMEM((max(len(earlier), 1), 3 * tiles, width), jnp.float32),
        pltpu.SemaphoreType.DMA((len(blocks),)),
        pltpu.SemaphoreType.DMA((len(blocks),)),
        pltpu.SemaphoreType.DMA((max(len(earlier), 1),)),
    ]
    rows = 8 * blocks[0].shape[0] * len(blocks) + (11 * (near_number + far_number) + 3 * len(earlier)) * tiles
    limit = 4 * width * rows + 8 * 1024 * 1024

    def kernel(*refs):
        given = len(blocks)
        known = given + len(earlier)
        made = known + len(shapes)
        pair_kernel(plan, refs[:given], refs[given:known], refs[known:made], refs[made:])

    return pl.pallas_call(
        kernel,
        out_shape=[jax.ShapeDtypeStruct(shape, jnp.float32) for shape in shapes],
        in_specs=[hbm] * (len(blocks) + len(earlier)),
        out_specs=[vmem] * len(shapes),
        scratch_shapes=scratch,
        compiler_params=pltpu.CompilerParams(vmem_limit_bytes=limit),
        cost_estimate=pl.CostEstimate(flops=(1000 if final else 1) * elements, bytes_accessed=1 << 16, transcendentals=0),
        name="pairs" if final else "early_pairs",
    )(*blocks, *earlier)


NCELL = 64


def pack_kernel(steps, me_ref, count_ref, segment_ref, local_ref, remote_ref, sent_ref, cell_ref, out_ref):
    tiles, width = segment_ref.shape[1:]
    slots, devices = sent_ref.shape
    pairs = local_ref.shape[1]
    for row, axis in enumerate((3, 4, 5, 6, 7, 8, 0, 1)):
        out_ref[pl.ds(row, tiles, stride=8), :] = segment_ref[axis]
    out_ref[8 * tiles : 9 * tiles, :] = segment_ref[2]

    def order(shape, dim):
        slot = lax.broadcasted_iota(jnp.int32, shape, dim)
        part = slot // slots
        peer = jnp.full(shape, me_ref[0])
        for k, step in enumerate(steps):
            peer = jnp.bitwise_xor(peer, step * jnp.bitwise_and(part >> k, 1))
        return peer, slot % slots

    peer, column = order((pairs, width), 0)
    wanted = peer * slots + column
    table = jnp.zeros((8, pairs), jnp.float32)
    for k in range(pairs // width):
        lanes = slice(k * width, (k + 1) * width)
        position = lax.broadcasted_iota(jnp.int32, (8, width), 1) + k * width
        near = jnp.where(position < count_ref[0], local_ref[:, lanes] + 1, 0).astype(jnp.float32)
        named = jnp.where(wanted == remote_ref[:, lanes], 1.0, 0.0)
        table += matmul(near.astype(jnp.bfloat16), named.astype(jnp.bfloat16), (1, 1))
    peer = order((pairs, devices), 0)[0]
    named = jnp.where(peer == lax.broadcasted_iota(jnp.int32, (pairs, devices), 1), 1.0, 0.0)
    sent = matmul(sent_ref[...].astype(jnp.float32).astype(jnp.bfloat16), named.astype(jnp.bfloat16), (1, 1))
    column = lax.broadcasted_iota(jnp.int32, (slots, pairs), 1) % slots
    sent = jnp.where(lax.broadcasted_iota(jnp.int32, (slots, pairs), 0) == column, sent, 0.0)
    sent = jnp.sum(sent, axis=0, keepdims=True)
    for k in range(pairs // width):
        lanes = slice(k * width, (k + 1) * width)
        out_ref[9 * tiles + k : 9 * tiles + k + 1, :] = table[0:1, lanes] - 1.0
        out_ref[9 * tiles + 4 + k : 9 * tiles + 5 + k, :] = sent[:, lanes]

    lane = lax.broadcasted_iota(jnp.int32, (tiles, width), 1)
    outer = jnp.zeros((tiles, width), jnp.float32)
    for k in range(9):
        product = segment_ref[3 + k // 3] * segment_ref[6 + k % 3]
        outer = jnp.where(lane == k, jnp.sum(product, axis=1, keepdims=True), outer)
    cells = lax.broadcasted_iota(jnp.int32, (NCELL, tiles), 0)
    held = jnp.where(cells == cell_ref[...], 1.0, 0.0).astype(jnp.bfloat16)
    moments = sum(matmul(part.astype(jnp.bfloat16), held, (1, 1)) for part in thirds(outer.T[0:16]))
    last = jnp.where(lax.broadcasted_iota(jnp.int32, (8, NCELL), 0) == 0, moments[8:16], 0.0)
    out_ref[9 * tiles + 8 : 9 * tiles + 16, :] = jnp.concatenate([moments[0:8], last], axis=1)


def pack(me, segments, send_tiles, pair_local, pair_remote, pair_count, tile_cell, steps):
    tiles, rows, width = segments.shape
    smem = pl.BlockSpec(memory_space=pltpu.SMEM)
    vmem = pl.BlockSpec(memory_space=pltpu.VMEM)
    block = pl.pallas_call(
        functools.partial(pack_kernel, steps),
        out_shape=jax.ShapeDtypeStruct((rows * tiles + 16, width), jnp.float32),
        in_specs=[smem, smem] + [vmem] * 5,
        out_specs=vmem,
        compiler_params=pltpu.CompilerParams(vmem_limit_bytes=16 * 1024 * 1024),
        name="pack",
    )(
        me, pair_count, segments.transpose(1, 0, 2), pair_local, pair_remote, send_tiles[0].T, tile_cell.reshape(1, -1)
    )
    return block.reshape(-1, 8, width)


def far_field(segments, tile_cell, moment_sums, total_segments):
    moments = moment_sums.reshape(NCELL, 3, 3) / jnp.sqrt(jnp.float32(total_segments))
    moments = 0.5 * (moments + jnp.transpose(moments, (0, 2, 1)))
    cells = jnp.arange(NCELL).astype(jnp.float32)
    weights = 8.0 / (8.0 + jnp.abs(cells[:, None] - cells[None, :]))
    stress = jnp.dot(weights, moments.reshape(NCELL, 9), precision=lax.Precision.HIGHEST)
    onehot = (tile_cell[:, None] == jnp.arange(NCELL)[None, :]).astype(jnp.float32)
    tile_stress = jnp.dot(onehot, stress, precision=lax.Precision.HIGHEST).reshape(-1, 3, 3)
    traction = jnp.sum(tile_stress[:, :, :, None] * segments[:, None, 3:6, :], axis=2)
    lines = segments[:, 6:9, :]
    return jnp.stack(
        [
            traction[:, 1] * lines[:, 2] - traction[:, 2] * lines[:, 1],
            traction[:, 2] * lines[:, 0] - traction[:, 0] * lines[:, 2],
            traction[:, 0] * lines[:, 1] - traction[:, 1] * lines[:, 0],
        ],
        axis=1,
    )


AXES = ("dom", "sub")


def swap(value, mask):
    devices = lax.axis_size(AXES)
    return lax.ppermute(value, AXES, [(k, k ^ mask) for k in range(devices)])


def span(steps):
    masks = [0]
    for step in steps:
        masks += [mask ^ step for mask in masks]
    return masks


def mask_steps(devices):
    bits = devices.bit_length() - 1
    number = bits // 2
    far_steps = [devices >> (k + 2) for k in range(number)]
    near_steps = [devices >> 1] + [devices >> (k + 1) for k in range(number + 1, bits)]
    return near_steps, far_steps


def spread(block, near_steps, far_steps, work):
    steps = list(near_steps) + list(far_steps)
    allowed = set(span(near_steps)) | set(span(far_steps))
    held = {0: block}
    fresh = {0: -1}
    sums = None
    while fresh:
        arrived = {}
        for mask, last in fresh.items():
            for at in range(last + 1, len(steps)):
                if mask ^ steps[at] in allowed:
                    arrived[mask ^ steps[at]] = (swap(held[mask], steps[at]), at)
        if arrived:
            quick, slow = [], list(arrived)
            if len(held) > 1 and sums is None:
                quick = [mask for mask in arrived if arrived[mask][1] == len(near_steps) - 1]
                slow = [mask for mask in arrived if mask not in quick]
                held.update(zip(quick, lax.optimization_barrier([arrived[mask][0] for mask in quick])))
                sums = work(held)
            values, sums = lax.optimization_barrier(([arrived[mask][0] for mask in slow], sums))
            held.update(zip(slow, values))
        fresh = {mask: at for mask, (value, at) in arrived.items()}
    return [held[mask] for mask in span(near_steps)], [held[mask] for mask in span(far_steps)], sums


def message_counts(steps):
    counts = [1] * min(len(steps) and 2, 1 << len(steps))
    while sum(counts) < 1 << len(steps):
        counts.append(2 if sum(counts) >= 4 or len(steps) < 3 else 1)
    return counts


def collect(outs, counts, steps):
    groups = list(zip(outs, counts))
    for step in reversed(steps):
        half = sum(count for value, count in groups) // 2
        kept, sent, seen = [], [], 0
        for value, count in groups:
            (kept if seen < half else sent).append((value, count))
            seen += count
        arrived = []
        for value, count in reversed(sent):
            got = swap(value, step)
            arrived = [got[k : k + 1] for k in range(count)] + arrived
        merged, at = [], 0
        for value, count in kept:
            more = arrived[at : at + count]
            merged.append((value + (jnp.concatenate(more) if count > 1 else more[0]), count))
            at += count
        groups = merged
    return groups[0][0][0]


def on_device(segments, send_tiles, pair_local, pair_remote, pair_count, tile_cell):
    width = segments.shape[2]
    tiles = segments.shape[0]
    devices = send_tiles.shape[1]
    slots = send_tiles.shape[2]
    near_steps, far_steps = mask_steps(devices)
    near_masks, far_masks = span(near_steps), span(far_steps)

    me = lax.axis_index(AXES).astype(jnp.int32).reshape(1)
    block = pack(
        me, segments, send_tiles, pair_local, pair_remote, pair_count, tile_cell, far_steps + near_steps
    )
    list_group = block.shape[0] - 2
    totals = (len(near_masks), len(far_masks))
    early = []

    def early_pairs(held):
        early.extend([k for k, mask in enumerate(masks) if mask in held] for masks in (near_masks, far_masks))
        blocks = [held[near_masks[k]] for k in early[0]] + [held[far_masks[k]] for k in early[1][1:]]
        return run_pairs(blocks, tiles, slots, list_group, totals, early[0], early[1])

    near_blocks, far_blocks, sums = spread(block, near_steps, far_steps, early_pairs)
    near_counts, far_counts = message_counts(near_steps), [1] * len(far_masks)
    outs = run_pairs(
        near_blocks + far_blocks[1:], tiles, slots, list_group, totals, list(range(totals[0])), list(range(totals[1])),
        (near_counts, far_counts), early, sums,
    )
    near_total = collect(outs[: len(near_counts)], near_counts, near_steps)
    far_total = collect(outs[len(near_counts) :], far_counts, far_steps)
    near_total, far_total = lax.optimization_barrier((near_total, far_total))
    forces = (near_total + far_total[: 3 * tiles]).reshape(3, tiles, width)
    rows = far_total[3 * tiles :]
    moment_sums = jnp.concatenate([rows[:, :NCELL], rows[:1, NCELL : 2 * NCELL]]).T
    total_segments = tiles * width * devices
    return forces.transpose(1, 0, 2) + far_field(segments, tile_cell, moment_sums, total_segments)


def solution(mesh):
    in_specs = (
        P(("dom", "sub"), None, None),
        P(("dom", "sub"), None, None),
        P(("dom", "sub"), None),
        P(("dom", "sub"), None),
        P(("dom", "sub")),
        P(("dom", "sub")),
    )
    out_specs = P(("dom", "sub"), None, None)
    return jax.shard_map(
        on_device, mesh=mesh, in_specs=in_specs, out_specs=out_specs, check_vma=False
    )
```

```python
import functools
import jax
import jax.numpy as jnp
from jax import lax
from jax.sharding import PartitionSpec as P
from jax.experimental import pallas as pl
from jax.experimental.pallas import tpu as pltpu

CORE = 0.25
GROUP = 8


def head(value):
    return value.astype(jnp.bfloat16).astype(jnp.float32)


def thirds(value):
    high = head(value)
    rest = value - high
    middle = head(rest)
    return high, middle, rest - middle


def halves(value):
    high = value.astype(jnp.bfloat16)
    return high, (value - high.astype(jnp.float32)).astype(jnp.bfloat16)


def tall(groups):
    return jnp.concatenate(groups, axis=0).astype(jnp.bfloat16)


def place(sub, rows, others=0.0):
    filled = others
    for at, row in rows.items():
        filled = jnp.where(sub == at, row, filled)
    return filled


def tile_parts(sub, rows):
    parts = [thirds(rows[k]) for k in range(3)]
    square = rows[0] * rows[0] + rows[1] * rows[1] + rows[2] * rows[2]
    ones = jnp.where(sub == 3, 1.0, 0.0)
    high, middle = [place(sub, {k: parts[k][at] for k in range(3)}, 0.0) for at in range(2)]
    sums = tall([high + ones, middle])
    return parts, square, sums, place(sub, {k: rows[k] for k in range(3)}, 0.0)


def products(sub, first, second, burgers):
    major = jnp.where(sub < 3, first[0], jnp.where(sub < 6, first[1], first[2]))
    minor = jnp.where(sub % 3 == 0, second[0], jnp.where(sub % 3 == 1, second[1], second[2]))
    rows = {0: first[2] * second[2], 1: burgers[0], 2: burgers[1]}
    parts = []
    for value in (major * minor, place(sub % 4, rows, burgers[2])):
        high = head(value)
        parts.append((high, value - high))
    return parts


def operands(near, far):
    sub = lax.broadcasted_iota(jnp.int32, (8, near[0].shape[1]), 0)
    near = [jnp.broadcast_to(row, sub.shape) for row in near]
    far = [jnp.broadcast_to(row, sub.shape) for row in far]
    scale = 1.0 / near[0].shape[1]
    for k in range(3):
        middle = jnp.sum(near[k], axis=1, keepdims=True) * scale
        near[k], far[k] = near[k] - middle, far[k] - middle
    zero = jnp.zeros(sub.shape, jnp.float32)
    parts, square, near_sums, near_spot = tile_parts(sub, near)
    square = thirds(square)
    ends = [{6: square[0], 7: square[1]}, {6: square[2], 7: 1.0}, {6: 1.0, 7: 1.0}]
    left = [
        place(sub, {1: middle, 5: middle, 3: low, **end}, high) for (high, middle, low), end in zip(parts, ends)
    ]
    (main, main_low), (rest, rest_low) = products(sub, near[3:6], near[6:9], near[3:6])
    half = sub < 4
    left = tall(left + [main, jnp.where(half, rest, rest_low), main_low, main, jnp.where(half, rest, 0.0)])

    parts, square, far_sums, far_spot = tile_parts(sub, far)
    square = thirds(square + CORE)
    ends = [{6: 1.0, 7: 1.0}, {6: 1.0, 7: square[0]}, {6: square[1], 7: square[2]}]
    spread = [
        place(sub, {2: -2.0 * middle, 5: -2.0 * middle, 4: -2.0 * low, **end}, -2.0 * high)
        for (high, middle, low), end in zip(parts, ends)
    ]
    (main, main_low), (rest, rest_low) = products(sub, far[6:9], far[3:6], far[3:6])
    numerator = tall([zero, main, rest, main, main_low, jnp.where(half, rest_low, 0.0)])
    return left.T, tall(spread + [zero]), numerator, near_sums, near_spot, far_sums, far_spot


def matmul(left, right, contract=(1, 0)):
    dims = (((contract[0],), (contract[1],)), ((), ()))
    return lax.dot_general(left, right, dims, preferred_element_type=jnp.float32)


def live_list(near_rows, far_rows, ids_ref):
    slots = ids_ref.shape[1]

    def line(rows):
        return jnp.concatenate([rows[k : k + 1] for k in range(rows.shape[0])], axis=1)

    near, far = line(near_rows), line(far_rows)
    alive = near >= 0
    row = lax.broadcasted_iota(jnp.int32, (slots, slots), 0)
    lane = lax.broadcasted_iota(jnp.int32, (slots, slots), 1)
    before = jnp.where(row < lane, 1.0, 0.0).astype(jnp.bfloat16)
    flags = jnp.where(alive, 1.0, 0.0)
    rank = matmul(jnp.broadcast_to(flags, (8, slots)).astype(jnp.bfloat16), before)[0:1]
    rank = jnp.where(alive, rank, -1.0)
    chosen = jnp.where(jnp.broadcast_to(rank, (slots, slots)) == row.astype(jnp.float32), 1.0, 0.0).astype(jnp.bfloat16)
    sub = lax.broadcasted_iota(jnp.int32, (8, slots), 0)
    near, far = jnp.maximum(near, 0).astype(jnp.int32), jnp.maximum(far, 0).astype(jnp.int32)
    values = [near >> 6, near & 63, far >> 6, far & 63]
    values = place(sub, {k: value.astype(jnp.float32) for k, value in enumerate(values)}, jnp.zeros((8, slots), jnp.float32))
    packed = matmul(values.astype(jnp.bfloat16), chosen, (1, 1)).astype(jnp.int32)
    number = jnp.sum(flags, axis=1, keepdims=True).astype(jnp.int32)
    ids_ref[0:1, :] = packed[0:1] * 64 + packed[1:2]
    ids_ref[1:2, :] = packed[2:3] * 64 + packed[3:4]
    ids_ref[2:3, :] = jnp.broadcast_to(number, (1, slots))


def pair_kernel(plan, sources, earlier, refs_out, scratch):
    tiles, slots, list_group, near_total, far_total, near, far, done, final = plan
    near_number, far_number = len(near), len(far)
    (blocks, lists, near_sum, far_sum, ids_vmem, ids, left_ref, right_ref, part_ref, sums_ref, spots_ref, earlier_sums,
     sems, list_sems, sum_sems) = scratch
    list_copies = [
        pltpu.make_async_copy(source.at[pl.ds(list_group, 2)], lists.at[k], list_sems.at[k])
        for k, source in enumerate(sources)
    ]
    copies = [pltpu.make_async_copy(source, blocks.at[k], sems.at[k]) for k, source in enumerate(sources)]
    sum_copies = [pltpu.make_async_copy(given.at[0], earlier_sums.at[k], sum_sems.at[k]) for k, given in enumerate(earlier)]
    for copy in list_copies + copies + sum_copies:
        copy.start()
    near_sum[...] = jnp.zeros_like(near_sum)
    far_sum[...] = jnp.zeros_like(far_sum)
    right_ref[...] = jnp.zeros_like(right_ref)
    for copy in list_copies:
        copy.wait()

    width = blocks.shape[-1]
    shape = (4, width)
    position = lax.broadcasted_iota(jnp.int32, shape, 0) * width + lax.broadcasted_iota(jnp.int32, shape, 1)
    near_ids = jnp.full(shape, -1.0)
    near_at = position // (far_total * slots)
    far_at = position // slots % far_total
    for k, block in enumerate(near):
        given = lists[k, 0, 0:4]
        given = jnp.where(given >= 0, given + k * tiles, given)
        near_ids = jnp.where(near_at == block, given, near_ids)
    far_ids = jnp.full(shape, -1.0)
    for k, block in enumerate(far):
        given = lists[near_number - 1 + k if k else 0, 0, 4:8] + k * tiles
        far_ids = jnp.where(far_at == block, given, far_ids)
    near_ids = jnp.where(far_ids >= 0, near_ids, -1.0)
    if done:
        old_near = functools.reduce(jnp.logical_or, [near_at == block for block in done[0]])
        old_far = functools.reduce(jnp.logical_or, [far_at == block for block in done[1]])
        near_ids = jnp.where(jnp.logical_and(old_near, old_far), -1.0, near_ids)
    live_list(near_ids, far_ids, ids_vmem)
    move = pltpu.make_async_copy(ids_vmem, ids, list_sems.at[0])
    move.start()
    move.wait()
    count = ids[2, 0]
    last = ids.shape[1] - 1
    for copy in copies:
        copy.wait()

    def tile_of(block, tile):
        rows = [blocks[block, tile, pl.ds(k, 1), :] for k in range(8)]
        return rows[6:8] + [blocks[block, tiles + tile // 8, pl.ds(tile % 8, 1), :]] + rows[0:6]

    def pick(group, k):
        at = group * GROUP + k
        held = jnp.clip(at, 0, last)
        near, far = ids[0, held], ids[1, held]
        live = jnp.logical_and(at >= 0, at < count)
        return live, near // tiles, near % tiles, far // tiles, far % tiles

    def add_sums(group):
        for k in range(GROUP):
            live, near_block, near_tile, far_block, far_tile = pick(group, k)
            stash = lax.rem(group, 3)
            near_rows, far_rows = sums_ref[stash, k, 0], sums_ref[stash, k, 1]
            parts = part_ref[k]
            half = parts.shape[1] // 2
            for block, tile, spot, total, out in (
                (near_block, near_tile, 0, matmul(jnp.concatenate([far_rows, far_rows], axis=1), parts, (1, 1)), near_sum),
                (far_block, far_tile, 1, matmul(near_rows, parts), far_sum),
            ):
                total = total[0:8] + total[8:16]
                if total.shape[1] > half:
                    total = total[:, :half] + total[:, half:]
                force = spots_ref[stash, k, spot] * jnp.broadcast_to(total[3:4], total.shape) - total
                out[block, pl.ds(pl.multiple_of(tile * 8, 8), 8), :] += jnp.where(live, force, 0.0)

    def couple():
        for k in range(GROUP):
            terms = matmul(left_ref[k], right_ref[k])
            inverse = lax.rsqrt(terms[:, :width])
            coupling = terms[:, width:] * (inverse * inverse * inverse)
            high, low = halves(coupling)
            part_ref[k, :, :width] = high
            part_ref[k, :, width:] = low

    def build(group):
        for k in range(GROUP):
            live, near_block, near_tile, far_block, far_tile = pick(group, k)
            far_place = jnp.where(far_block > 0, far_block + (near_number - 1), 0)
            left, spread, numerator, near_rows, near_spot, far_rows, far_spot = operands(
                tile_of(near_block, near_tile), tile_of(far_place, far_tile)
            )
            stash = lax.rem(group, 3)
            left_ref[k] = left
            right_ref[k, : spread.shape[0], :width] = spread
            right_ref[k, right_ref.shape[1] - numerator.shape[0] :, width:] = numerator
            sums_ref[stash, k, 0] = near_rows
            sums_ref[stash, k, 1] = far_rows
            spots_ref[stash, k, 0] = near_spot
            spots_ref[stash, k, 1] = far_spot

    def step(group, carry):
        add_sums(group - 2)
        couple()
        build(group)
        return carry

    groups = jnp.maximum((count + GROUP - 1) // GROUP, 2)
    build(jnp.int32(0))
    couple()
    build(jnp.int32(1))
    lax.fori_loop(2, groups, step, 0)
    add_sums(groups - 2)
    couple()
    add_sums(groups - 1)

    for copy in sum_copies:
        copy.wait()
    at = 0
    if final:
        moments = functools.reduce(jnp.add, [lists[k, 1] for k in range(near_number)])
        old = [list(blocks) for blocks in done]
    for out in refs_out:
        for k in range(out.shape[0]):
            is_near = at < near_number
            total, block = (near_sum, at) if is_near else (far_sum, at - near_number)
            known = None
            if final:
                row = old[0 if is_near else 1]
                if block in row:
                    known = earlier_sums.at[row.index(block) + (0 if is_near else len(old[0]))]
            for axis in range(3):
                rows = slice(axis * tiles, (axis + 1) * tiles)
                value = total[block, pl.ds(axis, tiles, stride=8), :]
                out[k, rows, :] = value if known is None else value + known[rows, :]
            if final and not is_near:
                out[k, 3 * tiles :, :] = moments
            at += 1


def run_pairs(blocks, tiles, slots, list_group, totals, near, far, counts=None, done=None, earlier=()):
    width = blocks[0].shape[-1]
    final = counts is not None
    near_number, far_number = len(near), len(far)
    slot_count = totals[0] * totals[1] * slots
    hbm = pl.BlockSpec(memory_space=pl.ANY)
    vmem = pl.BlockSpec(memory_space=pltpu.VMEM)
    plan = (tiles, slots, list_group) + tuple(totals) + (near, far, done, final)
    if final:
        shapes = [(count, 3 * tiles, width) for count in counts[0]]
        shapes += [(count, 3 * tiles + 8, width) for count in counts[1]]
    else:
        shapes = [(1, 3 * tiles, width)] * (near_number + far_number)
    depth, sum_rows = 64, 16
    share = len(near) * len(far) / (totals[0] * totals[1])
    elements = int(share * slot_count / 3) * width * width

    scratch = [
        pltpu.VMEM((len(blocks),) + blocks[0].shape, jnp.float32),
        pltpu.VMEM((len(blocks), 2, 8, width), jnp.float32),
        pltpu.VMEM((near_number, 8 * tiles, width), jnp.float32),
        pltpu.VMEM((far_number, 8 * tiles, width), jnp.float32),
        pltpu.VMEM((8, slot_count), jnp.int32),
        pltpu.SMEM((8, slot_count), jnp.int32),
        pltpu.VMEM((GROUP, width, depth), jnp.bfloat16),
        pltpu.VMEM((GROUP, depth, 2 * width), jnp.bfloat16),
        pltpu.VMEM((GROUP, width, 2 * width), jnp.bfloat16),
        pltpu.VMEM((3, GROUP, 2, sum_rows, width), jnp.bfloat16),
        pltpu.VMEM((3, GROUP, 2, 8, width), jnp.float32),
        pltpu.VMEM((max(len(earlier), 1), 3 * tiles, width), jnp.float32),
        pltpu.SemaphoreType.DMA((len(blocks),)),
        pltpu.SemaphoreType.DMA((len(blocks),)),
        pltpu.SemaphoreType.DMA((max(len(earlier), 1),)),
    ]
    rows = 8 * blocks[0].shape[0] * len(blocks) + (11 * (near_number + far_number) + 3 * len(earlier)) * tiles
    limit = 4 * width * rows + 8 * 1024 * 1024

    def kernel(*refs):
        given = len(blocks)
        known = given + len(earlier)
        made = known + len(shapes)
        pair_kernel(plan, refs[:given], refs[given:known], refs[known:made], refs[made:])

    return pl.pallas_call(
        kernel,
        out_shape=[jax.ShapeDtypeStruct(shape, jnp.float32) for shape in shapes],
        in_specs=[hbm] * (len(blocks) + len(earlier)),
        out_specs=[vmem] * len(shapes),
        scratch_shapes=scratch,
        compiler_params=pltpu.CompilerParams(vmem_limit_bytes=limit),
        cost_estimate=pl.CostEstimate(flops=(1000 if final else 1) * elements, bytes_accessed=1 << 16, transcendentals=0),
        name="pairs" if final else "early_pairs",
    )(*blocks, *earlier)


NCELL = 64


def pack_kernel(steps, me_ref, count_ref, segment_ref, local_ref, remote_ref, sent_ref, cell_ref, out_ref):
    tiles, width = segment_ref.shape[1:]
    slots, devices = sent_ref.shape
    pairs = local_ref.shape[1]
    for row, axis in enumerate((3, 4, 5, 6, 7, 8, 0, 1)):
        out_ref[pl.ds(row, tiles, stride=8), :] = segment_ref[axis]
    out_ref[8 * tiles : 9 * tiles, :] = segment_ref[2]

    def order(shape, dim):
        slot = lax.broadcasted_iota(jnp.int32, shape, dim)
        part = slot // slots
        peer = jnp.full(shape, me_ref[0])
        for k, step in enumerate(steps):
            peer = jnp.bitwise_xor(peer, step * jnp.bitwise_and(part >> k, 1))
        return peer, slot % slots

    peer, column = order((pairs, width), 0)
    wanted = peer * slots + column
    table = jnp.zeros((8, pairs), jnp.float32)
    for k in range(pairs // width):
        lanes = slice(k * width, (k + 1) * width)
        position = lax.broadcasted_iota(jnp.int32, (8, width), 1) + k * width
        near = jnp.where(position < count_ref[0], local_ref[:, lanes] + 1, 0).astype(jnp.float32)
        named = jnp.where(wanted == remote_ref[:, lanes], 1.0, 0.0)
        table += matmul(near.astype(jnp.bfloat16), named.astype(jnp.bfloat16), (1, 1))
    peer = order((pairs, devices), 0)[0]
    named = jnp.where(peer == lax.broadcasted_iota(jnp.int32, (pairs, devices), 1), 1.0, 0.0)
    sent = matmul(sent_ref[...].astype(jnp.float32).astype(jnp.bfloat16), named.astype(jnp.bfloat16), (1, 1))
    column = lax.broadcasted_iota(jnp.int32, (slots, pairs), 1) % slots
    sent = jnp.where(lax.broadcasted_iota(jnp.int32, (slots, pairs), 0) == column, sent, 0.0)
    sent = jnp.sum(sent, axis=0, keepdims=True)
    for k in range(pairs // width):
        lanes = slice(k * width, (k + 1) * width)
        out_ref[9 * tiles + k : 9 * tiles + k + 1, :] = table[0:1, lanes] - 1.0
        out_ref[9 * tiles + 4 + k : 9 * tiles + 5 + k, :] = sent[:, lanes]

    lane = lax.broadcasted_iota(jnp.int32, (tiles, width), 1)
    outer = jnp.zeros((tiles, width), jnp.float32)
    for k in range(9):
        product = segment_ref[3 + k // 3] * segment_ref[6 + k % 3]
        outer = jnp.where(lane == k, jnp.sum(product, axis=1, keepdims=True), outer)
    cells = lax.broadcasted_iota(jnp.int32, (NCELL, tiles), 0)
    held = jnp.where(cells == cell_ref[...], 1.0, 0.0).astype(jnp.bfloat16)
    moments = sum(matmul(part.astype(jnp.bfloat16), held, (1, 1)) for part in thirds(outer.T[0:16]))
    last = jnp.where(lax.broadcasted_iota(jnp.int32, (8, NCELL), 0) == 0, moments[8:16], 0.0)
    out_ref[9 * tiles + 8 : 9 * tiles + 16, :] = jnp.concatenate([moments[0:8], last], axis=1)


def pack(me, segments, send_tiles, pair_local, pair_remote, pair_count, tile_cell, steps):
    tiles, rows, width = segments.shape
    smem = pl.BlockSpec(memory_space=pltpu.SMEM)
    vmem = pl.BlockSpec(memory_space=pltpu.VMEM)
    block = pl.pallas_call(
        functools.partial(pack_kernel, steps),
        out_shape=jax.ShapeDtypeStruct((rows * tiles + 16, width), jnp.float32),
        in_specs=[smem, smem] + [vmem] * 5,
        out_specs=vmem,
        compiler_params=pltpu.CompilerParams(vmem_limit_bytes=16 * 1024 * 1024),
        name="pack",
    )(
        me, pair_count, segments.transpose(1, 0, 2), pair_local, pair_remote, send_tiles[0].T, tile_cell.reshape(1, -1)
    )
    return block.reshape(-1, 8, width)


def far_field(segments, tile_cell, moment_sums, total_segments):
    moments = moment_sums.reshape(NCELL, 3, 3) / jnp.sqrt(jnp.float32(total_segments))
    moments = 0.5 * (moments + jnp.transpose(moments, (0, 2, 1)))
    cells = jnp.arange(NCELL).astype(jnp.float32)
    weights = 8.0 / (8.0 + jnp.abs(cells[:, None] - cells[None, :]))
    stress = jnp.dot(weights, moments.reshape(NCELL, 9), precision=lax.Precision.HIGHEST)
    onehot = (tile_cell[:, None] == jnp.arange(NCELL)[None, :]).astype(jnp.float32)
    tile_stress = jnp.dot(onehot, stress, precision=lax.Precision.HIGHEST).reshape(-1, 3, 3)
    traction = jnp.sum(tile_stress[:, :, :, None] * segments[:, None, 3:6, :], axis=2)
    lines = segments[:, 6:9, :]
    return jnp.stack(
        [
            traction[:, 1] * lines[:, 2] - traction[:, 2] * lines[:, 1],
            traction[:, 2] * lines[:, 0] - traction[:, 0] * lines[:, 2],
            traction[:, 0] * lines[:, 1] - traction[:, 1] * lines[:, 0],
        ],
        axis=1,
    )


AXES = ("dom", "sub")


def swap(value, mask):
    devices = lax.axis_size(AXES)
    return lax.ppermute(value, AXES, [(k, k ^ mask) for k in range(devices)])


def span(steps):
    masks = [0]
    for step in steps:
        masks += [mask ^ step for mask in masks]
    return masks


def mask_steps(devices):
    bits = devices.bit_length() - 1
    number = bits // 2
    far_steps = [devices >> (k + 2) for k in range(number)]
    near_steps = [devices >> 1] + [devices >> (k + 1) for k in range(number + 1, bits)]
    return near_steps, far_steps


def spread(block, near_steps, far_steps, work):
    steps = list(near_steps) + list(far_steps)
    allowed = set(span(near_steps)) | set(span(far_steps))
    held = {0: block}
    fresh = {0: -1}
    sums = None
    while fresh:
        arrived = {}
        for mask, last in fresh.items():
            for at in range(last + 1, len(steps)):
                if mask ^ steps[at] in allowed:
                    arrived[mask ^ steps[at]] = (swap(held[mask], steps[at]), at)
        if arrived:
            quick, slow = [], list(arrived)
            if len(held) > 1 and sums is None:
                quick = [mask for mask in arrived if arrived[mask][1] == len(near_steps) - 1]
                slow = [mask for mask in arrived if mask not in quick]
                held.update(zip(quick, lax.optimization_barrier([arrived[mask][0] for mask in quick])))
                sums = work(held)
            values, sums = lax.optimization_barrier(([arrived[mask][0] for mask in slow], sums))
            held.update(zip(slow, values))
        fresh = {mask: at for mask, (value, at) in arrived.items()}
    return [held[mask] for mask in span(near_steps)], [held[mask] for mask in span(far_steps)], sums


def message_counts(steps):
    counts = [1] * min(len(steps) and 2, 1 << len(steps))
    while sum(counts) < 1 << len(steps):
        counts.append(2 if sum(counts) >= 4 or len(steps) < 3 else 1)
    return counts


def collect(outs, counts, steps):
    groups = list(zip(outs, counts))
    for step in reversed(steps):
        half = sum(count for value, count in groups) // 2
        kept, sent, seen = [], [], 0
        for value, count in groups:
            (kept if seen < half else sent).append((value, count))
            seen += count
        arrived = []
        for value, count in reversed(sent):
            if arrived and step == steps[min(1, len(steps) - 1)]:
                value, arrived[0] = lax.optimization_barrier((value, arrived[0]))
            got = swap(value, step)
            arrived = [got[k : k + 1] for k in range(count)] + arrived
        merged, at = [], 0
        for value, count in kept:
            more = arrived[at : at + count]
            merged.append((value + (jnp.concatenate(more) if count > 1 else more[0]), count))
            at += count
        groups = merged
    return groups[0][0][0]


def on_device(segments, send_tiles, pair_local, pair_remote, pair_count, tile_cell):
    width = segments.shape[2]
    tiles = segments.shape[0]
    devices = send_tiles.shape[1]
    slots = send_tiles.shape[2]
    near_steps, far_steps = mask_steps(devices)
    near_masks, far_masks = span(near_steps), span(far_steps)

    me = lax.axis_index(AXES).astype(jnp.int32).reshape(1)
    block = pack(
        me, segments, send_tiles, pair_local, pair_remote, pair_count, tile_cell, far_steps + near_steps
    )
    list_group = block.shape[0] - 2
    totals = (len(near_masks), len(far_masks))
    early = []

    def early_pairs(held):
        early.extend([k for k, mask in enumerate(masks) if mask in held] for masks in (near_masks, far_masks))
        blocks = [held[near_masks[k]] for k in early[0]] + [held[far_masks[k]] for k in early[1][1:]]
        return run_pairs(blocks, tiles, slots, list_group, totals, early[0], early[1])

    near_blocks, far_blocks, sums = spread(block, near_steps, far_steps, early_pairs)
    near_counts, far_counts = message_counts(near_steps), [1] * len(far_masks)
    outs = run_pairs(
        near_blocks + far_blocks[1:], tiles, slots, list_group, totals, list(range(totals[0])), list(range(totals[1])),
        (near_counts, far_counts), early, sums,
    )
    near_total = collect(outs[: len(near_counts)], near_counts, near_steps)
    far_total = collect(outs[len(near_counts) :], far_counts, far_steps)
    near_total, far_total = lax.optimization_barrier((near_total, far_total))
    forces = (near_total + far_total[: 3 * tiles]).reshape(3, tiles, width)
    rows = far_total[3 * tiles :]
    moment_sums = jnp.concatenate([rows[:, :NCELL], rows[:1, NCELL : 2 * NCELL]]).T
    total_segments = tiles * width * devices
    return forces.transpose(1, 0, 2) + far_field(segments, tile_cell, moment_sums, total_segments)


def solution(mesh):
    in_specs = (
        P(("dom", "sub"), None, None),
        P(("dom", "sub"), None, None),
        P(("dom", "sub"), None),
        P(("dom", "sub"), None),
        P(("dom", "sub")),
        P(("dom", "sub")),
    )
    out_specs = P(("dom", "sub"), None, None)
    return jax.shard_map(
        on_device, mesh=mesh, in_specs=in_specs, out_specs=out_specs, check_vma=False
    )
```
